128 devices in a mesh: seq: 32 (over y, z, core), dp: 4 (over x).
Axes of the slice: x: 4, y: 4, z: 4, core: 2. Of those that a mesh axis runs over, the one named last changes fastest.
Arguments:
- block_in: bfloat16 [4, 8192, 1024], P('dp', 'seq'), may hold values from -6 to 6
- conv_state: float32 [4, 3, 1536], P('dp'), may hold values from -6 to 6
- init_state: float32 [4, 1536], P('dp'), may hold values from -6 to 6
- cotangent: bfloat16 [4, 8192, 1024], P('dp', 'seq'), may hold values from -6 to 6
- prenorm: bfloat16 [1024], P(('seq', 'dp')), may hold values from 0.099609375 to 1.8984375
- recurrent: bfloat16 [1024, 1536], P(('seq', 'dp')), may hold values from -0.1875 to 0.1875
- sidebranch: bfloat16 [1024, 1536], P(('seq', 'dp')), may hold values from -0.1875 to 0.1875
- convolve: bfloat16 [4, 1536], P(None, ('seq', 'dp')), may hold values from -3 to 3
- convbias: bfloat16 [1536], P(('seq', 'dp')), may hold values from -2 to 2
- inputgate: bfloat16 [1536, 192], P(('seq', 'dp')), may hold values from -0.4375 to 0.4375
- inputbias: bfloat16 [1536], P(('seq', 'dp')), may hold values from -4 to 4
- decaygate: bfloat16 [1536, 192], P(('seq', 'dp')), may hold values from -0.4375 to 0.4375
- decaybias: bfloat16 [1536], P(('seq', 'dp')), may hold values from -4 to 4
- decayrate: bfloat16 [1536], P(('seq', 'dp')), may hold values from -14 to -3.5
- outproject: bfloat16 [1536, 1024], P(('seq', 'dp')), may hold values from -0.15625 to 0.15625
- midnorm: bfloat16 [1024], P(('seq', 'dp')), may hold values from 0.099609375 to 1.8984375
- gating: bfloat16 [1024, 3072], P(('seq', 'dp')), may hold values from -0.1875 to 0.1875
- upward: bfloat16 [1024, 3072], P(('seq', 'dp')), may hold values from -0.1875 to 0.1875
- downward: bfloat16 [3072, 1024], P(('seq', 'dp')), may hold values from -0.109375 to 0.109375
Outputs:
- block_out: bfloat16 [4, 8192, 1024], P('dp', 'seq')
- grad_in: bfloat16 [4, 8192, 1024], P('dp', 'seq')
- conv_final: float32 [4, 3, 1536], P('dp', None, 'seq')
- state_final: float32 [4, 1536], P('dp', 'seq')
- grad_prenorm: float32 [1024], P(('seq', 'dp'))
- grad_recurrent: float32 [1024, 1536], P(('seq', 'dp'))
- grad_sidebranch: float32 [1024, 1536], P(('seq', 'dp'))
- grad_convolve: float32 [4, 1536], P(None, ('seq', 'dp'))
- grad_convbias: float32 [1536], P(('seq', 'dp'))
- grad_inputgate: float32 [1536, 192], P(('seq', 'dp'))
- grad_inputbias: float32 [1536], P(('seq', 'dp'))
- grad_decaygate: float32 [1536, 192], P(('seq', 'dp'))
- grad_decaybias: float32 [1536], P(('seq', 'dp'))
- grad_decayrate: float32 [1536], P(('seq', 'dp'))
- grad_outproject: float32 [1536, 1024], P(('seq', 'dp'))
- grad_midnorm: float32 [1024], P(('seq', 'dp'))
- grad_gating: float32 [1024, 3072], P(('seq', 'dp'))
- grad_upward: float32 [1024, 3072], P(('seq', 'dp'))
- grad_downward: float32 [3072, 1024], P(('seq', 'dp'))
The draws below stay inside these ranges and needn't reach their ends.
All inputs are finite; a program needn't handle non-finite values.
Results may differ from the reference program's by a relative error of at most 0.0088.
Values may be sent and summed in bfloat16 or wider, within the bound.
No kernel may reach another device: no remote copies, remote signals or barrier semaphores. Data moves between devices by JAX's collectives and lax.ppermute only.
A program may use at most 320 MiB of HBM per device.

```python
import jax
import jax.numpy as jnp
from jax import lax

D = 1024
R = 1536
FF = 3072
CONV = 4
HW = 192
LEN = 8192
SEGS = 4


def level_of(key, extent, split, least, largest):
    level, own = 1.0, jax.random.fold_in(key, 6)
    for position, blocks in split:
        draws = jnp.exp(jax.random.uniform(jax.random.fold_in(own, position), (blocks,), jnp.float32, least / len(split), largest / len(split)))
        level = level * jnp.repeat(draws, extent[position] // blocks).reshape([-1 if axis == position else 1 for axis in range(len(extent))])
    return level


def scatter_about(rng, dims, scale, limit, cuts=(), held_as=jnp.bfloat16):
    factor_of = level_of(rng, dims, cuts, -0.22, 0.18) if cuts else 1.0
    values = jax.random.normal(rng, dims, jnp.float32) * scale * factor_of
    return jnp.minimum(jnp.maximum(values, -limit), limit).astype(held_as)


def setup_inputs(seed: int = 0) -> dict:
    streams_of = jax.random.split(jax.random.key(seed), 20)
    return {
        "block_in": scatter_about(streams_of[0], (SEGS, LEN, D), 1.0, 6.0, ((0, 4), (1, 32))),
        "conv_state": scatter_about(streams_of[1], (SEGS, CONV - 1, R), 1.0, 6.0, ((0, 4),), jnp.float32),
        "init_state": scatter_about(streams_of[2], (SEGS, R), 1.0, 6.0, ((0, 4),), jnp.float32),
        "cotangent": scatter_about(streams_of[3], (SEGS, LEN, D), 1.0, 6.0, ((0, 4), (1, 32))),
        "prenorm": jnp.clip(1.0 + 0.18 * jax.random.normal(streams_of[4], (D,), jnp.float32), 0.099609375, 1.8984375).astype(jnp.bfloat16),
        "recurrent": scatter_about(streams_of[5], (D, R), D ** -0.5, 0.1875, ((0, 128),)),
        "sidebranch": scatter_about(streams_of[6], (D, R), D ** -0.5, 0.1875, ((0, 128),)),
        "convolve": scatter_about(streams_of[7], (CONV, R), 0.5, 3.0, ((1, 128),)),
        "convbias": scatter_about(streams_of[8], (R,), 0.3, 2.0, ((0, 128),)),
        "inputgate": scatter_about(streams_of[9], (R, HW), HW ** -0.5, 0.4375, ((0, 128),)),
        "inputbias": scatter_about(streams_of[10], (R,), 1.0, 4.0, ((0, 128),)),
        "decaygate": scatter_about(streams_of[11], (R, HW), HW ** -0.5, 0.4375, ((0, 128),)),
        "decaybias": scatter_about(streams_of[12], (R,), 1.0, 4.0, ((0, 128),)),
        "decayrate": jnp.clip(-14.0 + 10.5 * jax.random.uniform(streams_of[13], (R,), jnp.float32) ** level_of(streams_of[13], (R,), ((0, 128),), -0.2, 0.2), -14.0, -3.5).astype(jnp.bfloat16),
        "outproject": scatter_about(streams_of[14], (R, D), R ** -0.5, 0.15625, ((0, 128),)),
        "midnorm": jnp.clip(1.0 + 0.18 * jax.random.normal(streams_of[15], (D,), jnp.float32), 0.099609375, 1.8984375).astype(jnp.bfloat16),
        "gating": scatter_about(streams_of[16], (D, FF), D ** -0.5, 0.1875, ((0, 128),)),
        "upward": scatter_about(streams_of[17], (D, FF), D ** -0.5, 0.1875, ((0, 128),)),
        "downward": scatter_about(streams_of[18], (FF, D), FF ** -0.5, 0.109375, ((0, 128),)),
    }


EPSILON = 1e-06
HIGHEST = lax.Precision.HIGHEST

@jax.custom_vjp
def low(v):
    return lax.optimization_barrier(v.astype(jnp.bfloat16)).astype(jnp.float32)

@jax.custom_vjp
def low_back(v):
    return v

def low_keep(v):
    return (low(v), None)

def low_pass(kept, grad):
    return (grad,)

def back_keep(v):
    return (v, None)

def back_low(kept, grad):
    return (low(grad),)
low.defvjp(low_keep, low_pass)
low_back.defvjp(back_keep, back_low)

def product(left, right):
    return jnp.dot(left, right, precision=HIGHEST, preferred_element_type=jnp.float32)

def rms_scale(values):
    return lax.rsqrt(lax.optimization_barrier(jnp.mean(values * values, axis=-1, keepdims=True)) + EPSILON)

def block_heads(values, weight):
    rows = values.shape[0]
    width = weight.shape[1]
    count = weight.shape[0] // width
    blocks = weight.reshape(count, width, width)
    result = jnp.einsum('thi,hij->thj', values.reshape(rows, count, width), blocks, precision=HIGHEST)
    return result.reshape(rows, count * width)

def gate_piece(extended, convolve, convbias, inputgate, inputbias, decaygate, decaybias, decayrate):
    taps = convolve.shape[0]
    rows = extended.shape[0] - taps + 1
    mixed = convbias + convolve[0] * extended[taps - 1:taps - 1 + rows]
    for offset in range(1, taps):
        mixed = mixed + convolve[offset] * extended[taps - 1 - offset:taps - 1 - offset + rows]
    opened = jax.nn.sigmoid(block_heads(mixed, inputgate) + inputbias)
    forget = jax.nn.sigmoid(block_heads(mixed, decaygate) + decaybias)
    log_decay = -8.0 * forget * jax.nn.softplus(decayrate)
    scaled = jnp.sqrt(-jnp.expm1(2.0 * log_decay))
    return (log_decay, scaled * opened * mixed)

def combine_pairs(first, second):
    return (first[0] + second[0], jnp.exp(second[0]) * first[1] + second[1])

def run_forward(log_decay, drive, start):
    seeded = jnp.concatenate([drive[:1] + jnp.exp(log_decay[:1]) * start, drive[1:]], axis=0)
    return lax.associative_scan(combine_pairs, (log_decay, seeded))

def segment_forward(tokens, conv_prev, start, params):
    prenorm, recurrent, sidebranch, convolve, convbias, inputgate, inputbias, decaygate, decaybias, decayrate, outproject, midnorm, gating, upward, downward = params
    normed_in = low(tokens * rms_scale(tokens) * prenorm)
    branch_x = low_back(product(normed_in, recurrent))
    side_pre = low_back(product(normed_in, sidebranch))
    side_act = jax.nn.gelu(side_pre)
    extended = jnp.concatenate([conv_prev, branch_x], axis=0)
    log_decay, drive = gate_piece(extended, convolve, convbias, inputgate, inputbias, decaygate, decaybias, decayrate)
    states = run_forward(log_decay, drive, start)[1]
    mixed_rec = low(states * side_act)
    branch_out = low_back(product(mixed_rec, outproject))
    resid = tokens + branch_out
    mid_normed = low(resid * rms_scale(resid) * midnorm)
    gate_pre = low_back(product(mid_normed, gating))
    up_pre = low_back(product(mid_normed, upward))
    hidden = low(jax.nn.gelu(gate_pre) * up_pre)
    result = resid + product(hidden, downward)
    taps = conv_prev.shape[0]
    return (result, (branch_x[branch_x.shape[0] - taps:], states[states.shape[0] - 1]))

def reference(block_in, conv_state, init_state, cotangent, prenorm, recurrent, sidebranch, convolve, convbias, inputgate, inputbias, decaygate, decaybias, decayrate, outproject, midnorm, gating, upward, downward):
    params = tuple((p.astype(jnp.float32) for p in (prenorm, recurrent, sidebranch, convolve, convbias, inputgate, inputbias, decaygate, decaybias, decayrate, outproject, midnorm, gating, upward, downward)))

    def step(totals, inputs):
        tokens, conv_prev, start, grad_out = inputs

        def forward(values, *weights):
            return segment_forward(values, conv_prev, start, weights)
        result, back, extras = jax.vjp(forward, tokens, *params, has_aux=True)
        grads = back(grad_out)
        updated = tuple((t + g for t, g in zip(totals, grads[1:])))
        return (updated, (result.astype(jnp.bfloat16), grads[0].astype(jnp.bfloat16), extras[0], extras[1]))
    initial = tuple((jnp.zeros_like(p) for p in params))
    totals, stacked = lax.scan(step, initial, (block_in.astype(jnp.float32), conv_state, init_state, cotangent.astype(jnp.float32)))
    return (stacked[0], stacked[1], stacked[2], stacked[3], totals[0], totals[1], totals[2], totals[3], totals[4], totals[5], totals[6], totals[7], totals[8], totals[9], totals[10], totals[11], totals[12], totals[13], totals[14])
```

```python
import functools

import jax
import jax.numpy as jnp
from jax import lax
from jax.experimental import pallas as pl
from jax.experimental.pallas import tpu as pltpu
from jax.sharding import Mesh
from jax.sharding import PartitionSpec as P

EPSILON = 1e-06
F32 = jnp.float32
BF16 = jnp.bfloat16
RANK = {"y": 0, "z": 1, "c": 2, "x": 3}
SWAP = [(0, 1), (1, 0)]
VMEM = 48 * 1024 * 1024


def dot(left, right, left_dim, right_dim):
    return lax.dot_general(
        left, right, (((left_dim,), (right_dim,)), ((), ())), preferred_element_type=F32
    )


def rms_scale(values):
    return lax.rsqrt(jnp.mean(values * values, axis=-1, keepdims=True) + EPSILON)


def fetch(block, axis, by):
    count = lax.axis_size(axis)
    return lax.ppermute(block, axis, [(i, (i - by) % count) for i in range(count)])


def swap_cores(block):
    return lax.ppermute(block, "c", SWAP)


def place_of(held, axis):
    return sum(RANK[h] < RANK[axis] for h in held)


def gather_round(jobs, *others):
    pieces = [[fetch(block, axis, by) for by in range(1, lax.axis_size(axis))] for block, axis, _ in jobs]
    pieces, others = lax.optimization_barrier((pieces, others))
    results = []
    for (block, axis, place), held in zip(jobs, pieces):
        count, me = lax.axis_size(axis), lax.axis_index(axis)
        shape = block.shape[:place] + (count,) + block.shape[place:]
        out = jnp.broadcast_to(jnp.expand_dims(block, place), shape)
        for by, piece in enumerate(held, 1):
            out = lax.dynamic_update_index_in_dim(out, piece, (me + by) % count, place)
        results.append(out)
    return results, others


def scatter_round(jobs, *others):
    kept, sent = [], []
    for array, axis, place in jobs:
        count, me = lax.axis_size(axis), lax.axis_index(axis)
        pick = lambda by: lax.dynamic_index_in_dim(array, (me + by) % count, place, keepdims=False)
        kept.append(pick(0))
        sent.append([fetch(pick(by), axis, -by) for by in range(1, count)])
    sent, others = lax.optimization_barrier((sent, others))
    results = []
    for own, pieces in zip(kept, sent):
        total = own.astype(F32)
        for piece in pieces:
            total = total + piece.astype(F32)
        results.append(total)
    return results, others


def split_cols(grad, rows):
    sizes = [lax.axis_size(a) for a in ("y", "z", "c", "x")]
    return grad.astype(BF16).reshape(*sizes, rows, grad.shape[-1])


def split_rows(grad, rows):
    sizes = [lax.axis_size(a) for a in ("y", "z", "x")]
    return grad.astype(BF16).reshape(*sizes, rows, grad.shape[-1])


def owners(inverse):
    ny, nz = lax.axis_size("y"), lax.axis_size("z")
    pairs = []
    for y in range(ny):
        for z in range(nz):
            for c in (0, 1):
                block = ((y % (ny // 2)) * nz + z) * 2 + c
                pairs.append(((y * nz + z) * 2 + c, block * 2 + y // (ny // 2)))
    return [(b, a) for a, b in pairs] if inverse else pairs


def to_half(block):
    return lax.ppermute(block, ("y", "z", "c"), owners(False))


def to_owner(block):
    return lax.ppermute(block, ("y", "z", "c"), owners(True))


def gather_chips(block):
    (block,), _ = gather_round([(block, "z", 0)])
    (block,), _ = gather_round([(block, "y", 0)])
    return block.reshape(-1, *block.shape[2:])


def one_less_square(log_decay, decay):
    twice = 2.0 * log_decay
    series = 1.0 + twice * (1.0 / 7.0)
    for order in (6.0, 5.0, 4.0, 3.0, 2.0):
        series = 1.0 + twice * (1.0 / order) * series
    return jnp.where(twice > -0.25, -twice * series, 1.0 - decay * decay)


def split_dot(values, weight):
    high = values.astype(BF16)
    rest = (values - high.astype(F32)).astype(BF16)
    return dot(high, weight, 1, 0) + dot(rest, weight, 1, 0)


def gates_kernel(
    ext_ref, open_ref, forget_ref, prm_ref,
    mixed_out, opened_out, forget_out, local_out, product_out,
    decay_s, drive_s, carry_s,
):
    step = pl.program_id(1)
    chunk, width = mixed_out.shape

    @pl.when(step == 0)
    def _():
        carry_s[0:1, :] = jnp.zeros((1, width), F32)
        carry_s[1:2, :] = jnp.ones((1, width), F32)

    start = pl.multiple_of(step * chunk, chunk)
    ext = ext_ref[pl.ds(start, chunk + 8), :]
    prm = prm_ref[...]
    mixed = prm[4:5] + prm[0:1] * ext[8 : 8 + chunk]
    for tap in range(1, 4):
        mixed = mixed + prm[tap : tap + 1] * ext[8 - tap : 8 - tap + chunk]
    opened = jax.nn.sigmoid(split_dot(mixed, open_ref[...]) + prm[5:6])
    forget = jax.nn.sigmoid(split_dot(mixed, forget_ref[...]) + prm[6:7])
    log_decay = forget * prm[7:8]
    decay = jnp.exp(log_decay)
    mixed_out[...] = mixed
    opened_out[...] = opened
    forget_out[...] = forget
    decay_s[...] = decay
    drive_s[...] = jnp.sqrt(one_less_square(log_decay, decay)) * opened * mixed
    rows = lax.broadcasted_iota(jnp.int32, (8, width), 0)

    def group(index, carry):
        state, product = carry
        at = pl.ds(pl.multiple_of(index * 8, 8), 8)
        a, b = decay_s[at, :], drive_s[at, :]
        for by in (1, 2, 4):
            inside = rows >= by
            b = jnp.where(inside, a * pltpu.roll(b, by, 0) + b, b)
            a = jnp.where(inside, a * pltpu.roll(a, by, 0), a)
        local = b + a * state
        total = a * product
        local_out[at, :] = local
        product_out[at, :] = total
        return local[7:8], total[7:8]

    state, product = lax.fori_loop(0, chunk // 8, group, (carry_s[0:1, :], carry_s[1:2, :]), unroll=4)
    carry_s[0:1, :] = state
    carry_s[1:2, :] = product


def reverse_kernel(grad_ref, forget_ref, prm_ref, local_out, product_out, first_out, decay_s, carry_s):
    step = pl.program_id(1)
    chunk, width = local_out.shape

    @pl.when(step == 0)
    def _():
        carry_s[0:1, :] = jnp.zeros((1, width), F32)
        carry_s[1:2, :] = jnp.ones((1, width), F32)
        carry_s[2:3, :] = jnp.ones((1, width), F32)

    decay = jnp.exp(forget_ref[...] * prm_ref[7:8, :])
    last = carry_s[2:3, :]
    decay_s[0:chunk, :] = decay
    carry_s[2:3, :] = decay[0:1]
    rows = lax.broadcasted_iota(jnp.int32, (8, width), 0)
    following = jnp.where(
        lax.broadcasted_iota(jnp.int32, (chunk, width), 0) == chunk - 1, last, pltpu.roll(decay, chunk - 1, 0)
    )
    decay_s[...] = following

    def group(index, carry):
        state, product = carry
        at = pl.ds(pl.multiple_of(chunk - 8 - index * 8, 8), 8)
        a, b = decay_s[at, :], grad_ref[at, :]
        for by in (1, 2, 4):
            inside = rows < 8 - by
            b = jnp.where(inside, a * pltpu.roll(b, 8 - by, 0) + b, b)
            a = jnp.where(inside, a * pltpu.roll(a, 8 - by, 0), a)
        local = b + a * state
        total = a * product
        local_out[at, :] = local
        product_out[at, :] = total
        return local[0:1], total[0:1]

    state, product = lax.fori_loop(0, chunk // 8, group, (carry_s[0:1, :], carry_s[1:2, :]), unroll=4)
    carry_s[0:1, :] = state
    carry_s[1:2, :] = product
    first_out[...] = jnp.broadcast_to(decay[0:1] * state, (8, width))


def gates_back_kernel(
    ext_ref, open_ref, shut_ref, prm_ref, ends_ref,
    mixed_ref, opened_ref, forget_ref, states_ref, local_ref, product_ref,
    grad_out, head_out, grad_open, grad_shut, sums_out,
    next_s,
):
    step = pl.program_id(1)
    steps = pl.num_programs(1)
    chunk, width = mixed_ref.shape

    @pl.when(step == 0)
    def _():
        next_s[...] = jnp.zeros_like(next_s)
        grad_open[...] = jnp.zeros_like(grad_open)
        grad_shut[...] = jnp.zeros_like(grad_shut)
        sums_out[...] = jnp.zeros_like(sums_out)

    place = steps - 1 - step
    start = pl.multiple_of(place * chunk, chunk)
    prm = prm_ref[...]
    mixed, opened, forget = mixed_ref[...], opened_ref[...], forget_ref[...]
    log_decay = forget * prm[7:8]
    decay = jnp.exp(log_decay)
    scaled = jnp.sqrt(one_less_square(log_decay, decay))
    grad_drive = local_ref[...] + product_ref[...] * ends_ref[1:2, :]
    states = states_ref[pl.ds(start, chunk), :]
    before = states_ref[pl.ds(pl.multiple_of(jnp.maximum(start - 8, 0), 8), 8), :]
    before = jnp.where(place == 0, ends_ref[0:1, :], before[7:8])
    prior = jnp.where(
        lax.broadcasted_iota(jnp.int32, (chunk, width), 0) == 0, before, pltpu.roll(states, 1, 0)
    )
    grad_scaled = grad_drive * opened * mixed
    grad_log = grad_drive * decay * prior - grad_scaled * decay * decay / scaled
    grad_opened = grad_drive * scaled * mixed * opened * (1.0 - opened)
    grad_forget = grad_log * prm[7:8] * forget * (1.0 - forget)
    low_mixed = mixed.astype(BF16)
    low_opened = grad_opened.astype(BF16)
    low_forget = grad_forget.astype(BF16)
    grad_open[...] += dot(low_mixed, low_opened, 0, 0)
    grad_shut[...] += dot(low_mixed, low_forget, 0, 0)
    grad_mixed = (
        grad_drive * scaled * opened
        + dot(low_opened, open_ref[...], 1, 1)
        + dot(low_forget, shut_ref[...], 1, 1)
    )
    spread = jnp.concatenate([grad_mixed, next_s[...]], axis=0)
    grad = prm[0:1] * grad_mixed
    for tap in range(1, 4):
        grad = grad + prm[tap : tap + 1] * spread[tap : tap + chunk]
    grad_out[...] = grad
    first = grad_mixed[0:8]
    next_s[...] = first
    lead = jnp.concatenate([jnp.zeros((8, width), F32), first], axis=0)
    head = jnp.zeros((8, width), F32)
    for tap in range(1, 4):
        head = head + prm[tap : tap + 1] * lead[tap : tap + 8]
    head_out[...] = head
    ext = ext_ref[pl.ds(start, chunk + 8), :]
    total = lambda v: jnp.sum(v, axis=0, keepdims=True)
    sums_out[...] += jnp.concatenate(
        [total(grad_mixed * ext[8 - tap : 8 - tap + chunk]) for tap in range(4)]
        + [total(grad_mixed), total(grad_opened), total(grad_forget), total(grad_log * forget)],
        axis=0,
    )


PAIR = 384
CHUNK = 128


def params_of(steps):
    return pltpu.CompilerParams(vmem_limit_bytes=VMEM, dimension_semantics=("arbitrary",) * steps)


def run_gates(ext, open_w, forget_w, prm):
    length, channels = ext.shape[0] - 8, ext.shape[1]
    chunk = min(CHUNK, length)
    grid = (channels // PAIR, length // chunk)
    whole = pl.BlockSpec((length + 8, PAIR), lambda j, i: (0, j))
    weight = pl.BlockSpec((None, PAIR, PAIR), lambda j, i: (j, 0, 0))
    row = pl.BlockSpec((8, PAIR), lambda j, i: (0, j))
    part = pl.BlockSpec((chunk, PAIR), lambda j, i: (i, j))
    return pl.pallas_call(
        gates_kernel,
        grid=grid,
        in_specs=[whole, weight, weight, row],
        out_specs=[part] * 5,
        out_shape=[jax.ShapeDtypeStruct((length, channels), F32)] * 5,
        scratch_shapes=[pltpu.VMEM((chunk, PAIR), F32)] * 2 + [pltpu.VMEM((8, PAIR), F32)],
        compiler_params=params_of(2),
        name="gates",
    )(ext, open_w, forget_w, prm)


def run_reverse(grad, forget, prm):
    length, channels = grad.shape
    chunk = min(CHUNK, length)
    steps = length // chunk
    row = pl.BlockSpec((8, PAIR), lambda j, i: (0, j))
    part = pl.BlockSpec((chunk, PAIR), lambda j, i: (steps - 1 - i, j))
    full = jax.ShapeDtypeStruct((length, channels), F32)
    return pl.pallas_call(
        reverse_kernel,
        grid=(channels // PAIR, steps),
        in_specs=[part, part, row],
        out_specs=[part, part, row],
        out_shape=[full, full, jax.ShapeDtypeStruct((8, channels), F32)],
        scratch_shapes=[pltpu.VMEM((chunk, PAIR), F32), pltpu.VMEM((8, PAIR), F32)],
        compiler_params=params_of(2),
        name="reverse",
    )(grad, forget, prm)


def run_gates_back(ext, open_w, forget_w, prm, ends, mixed, opened, forget, states, local, product):
    length, channels = mixed.shape
    chunk = min(CHUNK, length)
    steps = length // chunk
    pairs = channels // PAIR
    whole = pl.BlockSpec((length + 8, PAIR), lambda j, i: (0, j))
    held = pl.BlockSpec((length, PAIR), lambda j, i: (0, j))
    weight = pl.BlockSpec((None, PAIR, PAIR), lambda j, i: (j, 0, 0))
    row = pl.BlockSpec((8, PAIR), lambda j, i: (0, j))
    part = pl.BlockSpec((chunk, PAIR), lambda j, i: (steps - 1 - i, j))
    return pl.pallas_call(
        gates_back_kernel,
        grid=(pairs, steps),
        in_specs=[whole, weight, weight, row, row, part, part, part, held, part, part],
        out_specs=[part, row, weight, weight, row],
        out_shape=[
            jax.ShapeDtypeStruct((length, channels), F32),
            jax.ShapeDtypeStruct((8, channels), F32),
            jax.ShapeDtypeStruct((pairs, PAIR, PAIR), F32),
            jax.ShapeDtypeStruct((pairs, PAIR, PAIR), F32),
            jax.ShapeDtypeStruct((8, channels), F32),
        ],
        scratch_shapes=[pltpu.VMEM((8, PAIR), F32)],
        compiler_params=params_of(2),
        name="gates_back",
    )(ext, open_w, forget_w, prm, ends, mixed, opened, forget, states, local, product)


def paired(blocks):
    head = blocks.shape[1]
    split = blocks.reshape(-1, 2, head, head)
    none = jnp.zeros_like(split[:, 0])
    above = jnp.concatenate([split[:, 0], none], axis=2)
    below = jnp.concatenate([none, split[:, 1]], axis=2)
    return jnp.concatenate([above, below], axis=1)


def unpaired(pairs):
    head = pairs.shape[1] // 2
    blocks = jnp.stack([pairs[:, :head, :head], pairs[:, head:, head:]], axis=1)
    return blocks.reshape(-1, head)


def on_device(
    block_in,
    conv_state,
    init_state,
    cotangent,
    prenorm,
    recurrent,
    sidebranch,
    convolve,
    convbias,
    inputgate,
    inputbias,
    decaygate,
    decaybias,
    decayrate,
    outproject,
    midnorm,
    gating,
    upward,
    downward,
):
    core = lax.axis_index("c")
    first = core == 0
    ny, nz = lax.axis_size("y"), lax.axis_size("z")
    chips = ny * nz
    chip = lax.axis_index("y") * nz + lax.axis_index("z")
    rows = block_in.shape[1]
    width = recurrent.shape[1] // 2
    hidden_width = gating.shape[1] // 2
    head = inputgate.shape[1]
    model = block_in.shape[2]
    taps = convolve.shape[0]

    def in_order(own, other, axis=0):
        return jnp.concatenate([jnp.where(first, own, other), jnp.where(first, other, own)], axis=axis)

    def half(array, which, axis):
        size = array.shape[axis] // 2
        low = lax.slice_in_dim(array, 0, size, axis=axis)
        high = lax.slice_in_dim(array, size, 2 * size, axis=axis)
        return jnp.where(which == 0, low, high)

    def to_cols(grad):
        kept = jnp.where(first, grad[0], grad[1])
        sent = jnp.where(first, grad[1], grad[0])
        return in_order(kept, swap_cores(sent), axis=1)

    gains = jnp.pad(jnp.stack([prenorm, midnorm], axis=1), ((0, 0), (0, 126)))
    mats = (recurrent, gating, sidebranch, upward)
    mine = jnp.concatenate([gains] + [half(m, core, 1) for m in mats], axis=1)
    theirs = jnp.concatenate([gains] + [half(m, 1 - core, 1) for m in mats], axis=1)
    smalls = jnp.concatenate([convolve, jnp.stack([convbias, inputbias, decaybias, decayrate])], axis=0).T
    out_blk = jnp.concatenate(
        [outproject, inputgate, decaygate, jnp.pad(smalls, ((0, 0), (0, 120)))], axis=1
    )
    theirs, out_blk, down_blk, x_other, grad_other = lax.optimization_barrier(
        (
            swap_cores(theirs),
            to_half(out_blk),
            to_half(downward),
            swap_cores(block_in[0]),
            swap_cores(cotangent[0]),
        )
    )
    down_w = lax.all_gather(down_blk, ("y", "z", "x"), axis=0, tiled=True)
    x_low = in_order(block_in[0], x_other)
    grad_low = in_order(cotangent[0], grad_other)
    onward = [(i, i + 1) for i in range(chips - 1)]
    back = [(i + 1, i) for i in range(chips - 1)]

    both = in_order(mine[None], theirs[None])
    cut = 128 + width + hidden_width
    a_blk, b_blk = both[:, :, :cut], both[:, :, cut:]
    (a_blk, b_blk, o_blk), (x_before,) = gather_round(
        [(a_blk, "x", 1), (b_blk, "y", 0), (out_blk, "z", 0)],
        lax.ppermute(x_low[-8:], ("y", "z"), onward),
    )
    (a_blk, b_blk, o_blk), _ = gather_round([(a_blk, "y", 0), (b_blk, "z", 1), (o_blk, "x", 1)])
    cut = 128 + width
    (rec_all, side_w, out_all), (gating_blk, upward_blk) = gather_round(
        [(a_blk[..., :cut], "z", 1), (b_blk[..., :width], "x", 3), (o_blk, "y", 0)],
        a_blk[..., cut:],
        b_blk[..., width:],
    )
    (gating_w, upward_w), _ = gather_round([(gating_blk, "z", 1), (upward_blk, "x", 3)])
    rec_all, side_w, out_all, gating_w, upward_w = (
        w.reshape(-1, w.shape[-1]) for w in (rec_all, side_w, out_all, gating_w, upward_w)
    )
    rec_w = rec_all[:, 128:]
    pre_gain = rec_all[:, 0].astype(F32)
    mid_gain = rec_all[:, 1].astype(F32)
    out_w = out_all[:, :model]
    open_w = paired(out_all[:, model : model + head])
    shut_w = paired(out_all[:, model + head : model + 2 * head])
    prm = out_all[:, model + 2 * head : model + 2 * head + 8].T.astype(F32)
    rate = prm[7]
    prm = jnp.concatenate([prm[:7], -8.0 * jax.nn.softplus(rate)[None]], axis=0)

    tokens = x_low.astype(F32)
    pre_scale = rms_scale(tokens)
    normed = (tokens * pre_scale * pre_gain).astype(BF16)
    before = x_before.astype(F32)
    normed_before = (before * rms_scale(before) * pre_gain).astype(BF16)
    branch_ext = dot(jnp.concatenate([normed_before, normed], axis=0), rec_w, 1, 0)
    conv_prev = jnp.pad(half(conv_state[0], core, 1), ((8 - taps + 1, 2 * rows), (0, 0)))
    is_before = lax.broadcasted_iota(jnp.int32, branch_ext.shape, 0) < 8
    branch_ext = jnp.where(is_before & (chip == 0), conv_prev, branch_ext)
    side_pre = dot(normed, side_w, 1, 0)
    side_act, side_back = jax.vjp(jax.nn.gelu, side_pre)
    mixed, opened, forget, local, product = run_gates(branch_ext, open_w, shut_w, prm)
    ends = jnp.concatenate([product[-1:], local[-1:], branch_ext[-6:]], axis=0)
    all_ends = gather_chips(ends)
    products, lasts = all_ends[:, 0], all_ends[:, 1]
    state = half(init_state[0], core, 0)
    start = state
    for i in range(chips):
        start = jnp.where(chip == i, state, start)
        state = products[i] * state + lasts[i]
    states = local + product * start
    mixed_rec = (states * side_act).astype(BF16)
    branch_part = dot(mixed_rec, out_w, 1, 0)
    resid = tokens + (branch_part + swap_cores(branch_part))

    mid_scale = rms_scale(resid)
    mid_low = (resid * mid_scale * mid_gain).astype(BF16)
    gate_pre = dot(mid_low, gating_w, 1, 0)
    up_pre = dot(mid_low, upward_w, 1, 0)
    gate_act, gelu_back = jax.vjp(jax.nn.gelu, gate_pre)
    hidden = (gate_act * up_pre).astype(BF16)
    result_part = dot(hidden, down_w, 1, 0)
    result = half(resid + result_part, core, 0) + swap_cores(half(result_part, 1 - core, 0))

    grad_hidden = dot(grad_low, down_w, 1, 1)
    grad_gate = gelu_back(grad_hidden * up_pre)[0].astype(BF16)
    grad_up = (grad_hidden * gate_act).astype(BF16)
    grad_down = dot(hidden, grad_low, 0, 0).astype(BF16)
    grad_gating = dot(mid_low, grad_gate, 0, 0).astype(BF16)
    grad_upward = dot(mid_low, grad_up, 0, 0).astype(BF16)
    grad_down = split_rows(grad_down, downward.shape[0]).reshape(grad_down.shape)
    for axis in ("y", "z", "x"):
        grad_down = lax.psum_scatter(grad_down, axis, scatter_dimension=0, tiled=True)
    grad_down = to_owner(grad_down).astype(F32)
    mid_part = dot(grad_gate, gating_w, 1, 1) + dot(grad_up, upward_w, 1, 1)
    (a, b), _ = scatter_round(
        [(split_cols(grad_gating, gating.shape[0]), "z", 1), (split_cols(grad_upward, upward.shape[0]), "x", 3)]
    )
    grad_mid = mid_part + swap_cores(mid_part)
    scaled = mid_gain * grad_mid
    grad_resid = (
        grad_low.astype(F32)
        + mid_scale * scaled
        - resid * mid_scale**3 * jnp.mean(scaled * resid, axis=-1, keepdims=True)
    )

    grad_branch = grad_resid.astype(BF16)
    grad_out = dot(mixed_rec, grad_branch, 0, 0).astype(BF16)
    grad_mixed = dot(grad_branch, out_w, 1, 1)
    grad_states = grad_mixed * side_act
    grad_side = side_back(grad_mixed * states)[0].astype(BF16)
    grad_sidebranch = dot(normed, grad_side, 0, 0).astype(BF16)
    (o, side), (a, b) = scatter_round(
        [(split_rows(grad_out, outproject.shape[0]), "y", 0), (split_cols(grad_sidebranch, sidebranch.shape[0]), "z", 1)],
        a,
        b,
    )
    a = jnp.concatenate([a.astype(BF16), side.astype(BF16)], axis=-1)
    (a, b, o), _ = scatter_round([(a, "y", 0), (b.astype(BF16), "z", 1), (o.astype(BF16), "x", 1)])
    (a, b, o), _ = scatter_round([(a.astype(BF16), "x", 1), (b.astype(BF16), "y", 0), (o.astype(BF16), "z", 0)])
    grad_out = to_owner(o)
    grad_gating = to_cols(a[..., :hidden_width])
    grad_sidebranch = to_cols(a[..., hidden_width:])
    grad_upward = to_cols(b)
    back_local, back_product, back_first = run_reverse(grad_states, forget, prm)
    firsts = gather_chips(back_first)[:, 0]
    carry = jnp.zeros((width,), F32)
    coming = carry
    for i in reversed(range(chips)):
        coming = jnp.where(chip == i, carry, coming)
        carry = firsts[i] + products[i] * carry
    grad_ext, grad_head, grad_open, grad_shut, sums = run_gates_back(
        branch_ext, open_w, shut_w, prm,
        jnp.concatenate([start[None], coming[None], jnp.zeros((6, width), F32)], axis=0),
        mixed, opened, forget, states, back_local, back_product,
    )
    from_next = lax.ppermute(grad_head, ("y", "z"), back)
    grad_x = jnp.concatenate([grad_ext[:-8], grad_ext[-8:] + from_next], axis=0).astype(BF16)
    grad_recurrent = dot(normed, grad_x, 0, 0).astype(BF16)
    pre_part = dot(grad_x, rec_w, 1, 1) + dot(grad_side, side_w, 1, 1)
    grad_pre = half(pre_part, core, 0) + swap_cores(half(pre_part, 1 - core, 0))
    own = block_in[0].astype(F32)
    own_scale = rms_scale(own)
    scaled = pre_gain * grad_pre
    grad_in = half(grad_resid, core, 0) + (
        own_scale * scaled - own * own_scale**3 * jnp.mean(scaled * own, axis=-1, keepdims=True)
    )

    sums = jnp.concatenate([sums[:7], sums[7:] * (-8.0 * jax.nn.sigmoid(rate))[None]], axis=0)
    gate_grads = jnp.concatenate(
        [unpaired(grad_open), unpaired(grad_shut), jnp.pad(sums.T, ((0, 0), (0, 120)))], axis=1
    )
    r = split_cols(grad_recurrent, recurrent.shape[0])
    l = split_rows(gate_grads, inputgate.shape[0])
    quarter = width // 2
    (r1, r2, l), _ = scatter_round([(r[..., :quarter], "z", 1), (r[..., quarter:], "x", 3), (l, "y", 0)])
    (r1, r2, l), _ = scatter_round(
        [(r1.astype(BF16), "y", 0), (r2.astype(BF16), "z", 1), (l.astype(BF16), "x", 1)]
    )
    (r1, r2, l), _ = scatter_round(
        [(r1.astype(BF16), "x", 1), (r2.astype(BF16), "y", 0), (l.astype(BF16), "z", 0)]
    )
    grad_recurrent = to_cols(jnp.concatenate([r1, r2], axis=-1))
    gate_grads = to_owner(l)

    def along(weight, grad):
        return jnp.sum(weight.astype(F32) * grad, axis=1)

    grad_prenorm = (along(recurrent, grad_recurrent) + along(sidebranch, grad_sidebranch)) / prenorm.astype(F32)
    grad_midnorm = (along(gating, grad_gating) + along(upward, grad_upward)) / midnorm.astype(F32)
    small = gate_grads[:, 2 * head : 2 * head + 8].T

    finals = jnp.concatenate([all_ends[-1, 8 - taps + 1 :], state[None]], axis=0)
    finals = jnp.where(core == lax.axis_index("y") // (ny // 2), finals, swap_cores(finals))
    slot = width // chips
    finals = lax.dynamic_slice_in_dim(finals, ((chip * 2 + core) % chips) * slot, slot, axis=1)

    return (
        result.astype(BF16)[None],
        grad_in.astype(BF16)[None],
        finals[None, : taps - 1],
        finals[None, taps - 1],
        grad_prenorm,
        grad_recurrent,
        grad_sidebranch,
        small[:4],
        small[4],
        gate_grads[:, :head],
        small[5],
        gate_grads[:, head : 2 * head],
        small[6],
        small[7],
        grad_out,
        grad_midnorm,
        grad_gating,
        grad_upward,
        grad_down,
    )


def solution(mesh):
    seq, dp = mesh.shape["seq"], mesh.shape["dp"]
    side = next(s for s in range(1, seq + 1) if 2 * s * s >= seq)
    fine = Mesh(mesh.devices.reshape(side, side, 2, dp), ("y", "z", "c", "x"))
    part = ("y", "z", "c")
    every = ("y", "z", "c", "x")
    vector, matrix = P(every), P(every, None)
    placed = (
        P("x", part, None),
        P("x", None, None),
        P("x", None),
        P("x", part, None),
        vector,
        matrix,
        matrix,
        P(None, every),
        vector,
        matrix,
        vector,
        matrix,
        vector,
        vector,
        matrix,
        vector,
        matrix,
        matrix,
        matrix,
    )
    return jax.shard_map(
        on_device,
        mesh=fine,
        in_specs=placed,
        out_specs=(P("x", part, None), P("x", part, None), P("x", None, part), P("x", part)) + placed[4:],
        check_vma=False,
    )
```

```python
import functools

import jax
import jax.numpy as jnp
from jax import lax
from jax.experimental import pallas as pl
from jax.experimental.pallas import tpu as pltpu
from jax.sharding import Mesh
from jax.sharding import PartitionSpec as P

EPSILON = 1e-06
F32 = jnp.float32
BF16 = jnp.bfloat16
RANK = {"y": 0, "z": 1, "c": 2, "x": 3}
SWAP = [(0, 1), (1, 0)]
VMEM = 48 * 1024 * 1024


def dot(left, right, left_dim, right_dim):
    return lax.dot_general(
        left, right, (((left_dim,), (right_dim,)), ((), ())), preferred_element_type=F32
    )


def rms_scale(values):
    return lax.rsqrt(jnp.mean(values * values, axis=-1, keepdims=True) + EPSILON)


def fetch(block, axis, by):
    count = lax.axis_size(axis)
    return lax.ppermute(block, axis, [(i, (i - by) % count) for i in range(count)])


def swap_cores(block):
    return lax.ppermute(block, "c", SWAP)


def place_of(held, axis):
    return sum(RANK[h] < RANK[axis] for h in held)


def gather_round(jobs, *others):
    pieces = [[fetch(block, axis, by) for by in range(1, lax.axis_size(axis))] for block, axis, _ in jobs]
    pieces, others = lax.optimization_barrier((pieces, others))
    results = []
    for (block, axis, place), held in zip(jobs, pieces):
        count, me = lax.axis_size(axis), lax.axis_index(axis)
        shape = block.shape[:place] + (count,) + block.shape[place:]
        out = jnp.broadcast_to(jnp.expand_dims(block, place), shape)
        for by, piece in enumerate(held, 1):
            out = lax.dynamic_update_index_in_dim(out, piece, (me + by) % count, place)
        results.append(out)
    return results, others


def scatter_send(array, axis, place):
    array = array.astype(BF16)
    count, me = lax.axis_size(axis), lax.axis_index(axis)
    pick = lambda by: lax.dynamic_index_in_dim(array, (me + by) % count, place, keepdims=False)
    return [pick(0)] + [fetch(pick(by), axis, -by) for by in range(1, count)]


def add_up(pieces):
    total = pieces[0].astype(F32)
    for piece in pieces[1:]:
        total = total + piece.astype(F32)
    return total


def tied(*values):
    return lax.optimization_barrier(values)


def split_cols(grad, rows):
    sizes = [lax.axis_size(a) for a in ("y", "z", "c", "x")]
    return grad.astype(BF16).reshape(*sizes, rows, grad.shape[-1])


def split_rows(grad, rows):
    sizes = [lax.axis_size(a) for a in ("y", "z", "x")]
    return grad.astype(BF16).reshape(*sizes, rows, grad.shape[-1])


def owners(inverse):
    ny, nz = lax.axis_size("y"), lax.axis_size("z")
    pairs = []
    for y in range(ny):
        for z in range(nz):
            for c in (0, 1):
                block = ((y % (ny // 2)) * nz + z) * 2 + c
                pairs.append(((y * nz + z) * 2 + c, block * 2 + y // (ny // 2)))
    return [(b, a) for a, b in pairs] if inverse else pairs


def to_half(block):
    return lax.ppermute(block, ("y", "z", "c"), owners(False))


def to_owner(block):
    return lax.ppermute(block, ("y", "z", "c"), owners(True))


def one_less_square(log_decay, decay):
    twice = 2.0 * log_decay
    series = 1.0 + twice * (1.0 / 7.0)
    for order in (6.0, 5.0, 4.0, 3.0, 2.0):
        series = 1.0 + twice * (1.0 / order) * series
    return jnp.where(twice > -0.25, -twice * series, 1.0 - decay * decay)


def split_dot(values, weight):
    high = values.astype(BF16)
    rest = (values - high.astype(F32)).astype(BF16)
    return dot(high, weight, 1, 0) + dot(rest, weight, 1, 0)


def gates_kernel(
    ext_ref, open_ref, forget_ref, prm_ref,
    mixed_out, opened_out, forget_out, local_out, product_out,
    decay_s, drive_s, carry_s,
):
    step = pl.program_id(1)
    chunk, width = mixed_out.shape

    @pl.when(step == 0)
    def _():
        carry_s[0:1, :] = jnp.zeros((1, width), F32)
        carry_s[1:2, :] = jnp.ones((1, width), F32)

    start = pl.multiple_of(step * chunk, chunk)
    ext = ext_ref[pl.ds(start, chunk + 8), :]
    prm = prm_ref[...]
    mixed = prm[4:5] + prm[0:1] * ext[8 : 8 + chunk]
    for tap in range(1, 4):
        mixed = mixed + prm[tap : tap + 1] * ext[8 - tap : 8 - tap + chunk]
    opened = jax.nn.sigmoid(split_dot(mixed, open_ref[...]) + prm[5:6])
    forget = jax.nn.sigmoid(split_dot(mixed, forget_ref[...]) + prm[6:7])
    log_decay = forget * prm[7:8]
    decay = jnp.exp(log_decay)
    mixed_out[...] = mixed
    opened_out[...] = opened
    forget_out[...] = forget
    decay_s[...] = decay
    drive_s[...] = jnp.sqrt(one_less_square(log_decay, decay)) * opened * mixed
    rows = lax.broadcasted_iota(jnp.int32, (8, width), 0)

    def group(index, carry):
        state, product = carry
        at = pl.ds(pl.multiple_of(index * 8, 8), 8)
        a, b = decay_s[at, :], drive_s[at, :]
        for by in (1, 2, 4):
            inside = rows >= by
            b = jnp.where(inside, a * pltpu.roll(b, by, 0) + b, b)
            a = jnp.where(inside, a * pltpu.roll(a, by, 0), a)
        local = b + a * state
        total = a * product
        local_out[at, :] = local
        product_out[at, :] = total
        return local[7:8], total[7:8]

    state, product = lax.fori_loop(0, chunk // 8, group, (carry_s[0:1, :], carry_s[1:2, :]), unroll=4)
    carry_s[0:1, :] = state
    carry_s[1:2, :] = product


def reverse_kernel(grad_ref, forget_ref, prm_ref, local_out, product_out, first_out, decay_s, carry_s):
    step = pl.program_id(1)
    chunk, width = local_out.shape

    @pl.when(step == 0)
    def _():
        carry_s[0:1, :] = jnp.zeros((1, width), F32)
        carry_s[1:2, :] = jnp.ones((1, width), F32)
        carry_s[2:3, :] = jnp.ones((1, width), F32)

    decay = jnp.exp(forget_ref[...] * prm_ref[7:8, :])
    last = carry_s[2:3, :]
    decay_s[0:chunk, :] = decay
    carry_s[2:3, :] = decay[0:1]
    rows = lax.broadcasted_iota(jnp.int32, (8, width), 0)
    following = jnp.where(
        lax.broadcasted_iota(jnp.int32, (chunk, width), 0) == chunk - 1, last, pltpu.roll(decay, chunk - 1, 0)
    )
    decay_s[...] = following

    def group(index, carry):
        state, product = carry
        at = pl.ds(pl.multiple_of(chunk - 8 - index * 8, 8), 8)
        a, b = decay_s[at, :], grad_ref[at, :]
        for by in (1, 2, 4):
            inside = rows < 8 - by
            b = jnp.where(inside, a * pltpu.roll(b, 8 - by, 0) + b, b)
            a = jnp.where(inside, a * pltpu.roll(a, 8 - by, 0), a)
        local = b + a * state
        total = a * product
        local_out[at, :] = local
        product_out[at, :] = total
        return local[0:1], total[0:1]

    state, product = lax.fori_loop(0, chunk // 8, group, (carry_s[0:1, :], carry_s[1:2, :]), unroll=4)
    carry_s[0:1, :] = state
    carry_s[1:2, :] = product
    first_out[...] = jnp.broadcast_to(decay[0:1] * state, (8, width))


def gates_back_kernel(
    ext_ref, open_ref, shut_ref, prm_ref, ends_ref,
    mixed_ref, opened_ref, forget_ref, states_ref, local_ref, product_ref,
    grad_out, head_out, grad_open, grad_shut, sums_out,
    next_s,
):
    step = pl.program_id(1)
    steps = pl.num_programs(1)
    chunk, width = mixed_ref.shape

    @pl.when(step == 0)
    def _():
        next_s[...] = jnp.zeros_like(next_s)
        grad_open[...] = jnp.zeros_like(grad_open)
        grad_shut[...] = jnp.zeros_like(grad_shut)
        sums_out[...] = jnp.zeros_like(sums_out)

    place = steps - 1 - step
    start = pl.multiple_of(place * chunk, chunk)
    prm = prm_ref[...]
    mixed, opened, forget = mixed_ref[...], opened_ref[...], forget_ref[...]
    log_decay = forget * prm[7:8]
    decay = jnp.exp(log_decay)
    scaled = jnp.sqrt(one_less_square(log_decay, decay))
    grad_drive = local_ref[...] + product_ref[...] * ends_ref[1:2, :]
    states = states_ref[pl.ds(start, chunk), :]
    before = states_ref[pl.ds(pl.multiple_of(jnp.maximum(start - 8, 0), 8), 8), :]
    before = jnp.where(place == 0, ends_ref[0:1, :], before[7:8])
    prior = jnp.where(
        lax.broadcasted_iota(jnp.int32, (chunk, width), 0) == 0, before, pltpu.roll(states, 1, 0)
    )
    grad_scaled = grad_drive * opened * mixed
    grad_log = grad_drive * decay * prior - grad_scaled * decay * decay / scaled
    grad_opened = grad_drive * scaled * mixed * opened * (1.0 - opened)
    grad_forget = grad_log * prm[7:8] * forget * (1.0 - forget)
    low_mixed = mixed.astype(BF16)
    low_opened = grad_opened.astype(BF16)
    low_forget = grad_forget.astype(BF16)
    grad_open[...] += dot(low_mixed, low_opened, 0, 0)
    grad_shut[...] += dot(low_mixed, low_forget, 0, 0)
    grad_mixed = (
        grad_drive * scaled * opened
        + dot(low_opened, open_ref[...], 1, 1)
        + dot(low_forget, shut_ref[...], 1, 1)
    )
    spread = jnp.concatenate([grad_mixed, next_s[...]], axis=0)
    grad = prm[0:1] * grad_mixed
    for tap in range(1, 4):
        grad = grad + prm[tap : tap + 1] * spread[tap : tap + chunk]
    grad_out[...] = grad
    first = grad_mixed[0:8]
    next_s[...] = first
    lead = jnp.concatenate([jnp.zeros((8, width), F32), first], axis=0)
    head = jnp.zeros((8, width), F32)
    for tap in range(1, 4):
        head = head + prm[tap : tap + 1] * lead[tap : tap + 8]
    head_out[...] = head
    ext = ext_ref[pl.ds(start, chunk + 8), :]
    total = lambda v: jnp.sum(v, axis=0, keepdims=True)
    sums_out[...] += jnp.concatenate(
        [total(grad_mixed * ext[8 - tap : 8 - tap + chunk]) for tap in range(4)]
        + [total(grad_mixed), total(grad_opened), total(grad_forget), total(grad_log * forget)],
        axis=0,
    )


PAIR = 384
CHUNK = 128


def params_of(steps):
    return pltpu.CompilerParams(vmem_limit_bytes=VMEM, dimension_semantics=("arbitrary",) * steps)


def run_gates(ext, open_w, forget_w, prm):
    length, channels = ext.shape[0] - 8, ext.shape[1]
    chunk = min(CHUNK, length)
    grid = (channels // PAIR, length // chunk)
    whole = pl.BlockSpec((length + 8, PAIR), lambda j, i: (0, j))
    weight = pl.BlockSpec((None, PAIR, PAIR), lambda j, i: (j, 0, 0))
    row = pl.BlockSpec((8, PAIR), lambda j, i: (0, j))
    part = pl.BlockSpec((chunk, PAIR), lambda j, i: (i, j))
    return pl.pallas_call(
        gates_kernel,
        grid=grid,
        in_specs=[whole, weight, weight, row],
        out_specs=[part] * 5,
        out_shape=[jax.ShapeDtypeStruct((length, channels), F32)] * 5,
        scratch_shapes=[pltpu.VMEM((chunk, PAIR), F32)] * 2 + [pltpu.VMEM((8, PAIR), F32)],
        compiler_params=params_of(2),
        name="gates",
    )(ext, open_w, forget_w, prm)


def run_reverse(grad, forget, prm):
    length, channels = grad.shape
    chunk = min(CHUNK, length)
    steps = length // chunk
    row = pl.BlockSpec((8, PAIR), lambda j, i: (0, j))
    part = pl.BlockSpec((chunk, PAIR), lambda j, i: (steps - 1 - i, j))
    full = jax.ShapeDtypeStruct((length, channels), F32)
    return pl.pallas_call(
        reverse_kernel,
        grid=(channels // PAIR, steps),
        in_specs=[part, part, row],
        out_specs=[part, part, row],
        out_shape=[full, full, jax.ShapeDtypeStruct((8, channels), F32)],
        scratch_shapes=[pltpu.VMEM((chunk, PAIR), F32), pltpu.VMEM((8, PAIR), F32)],
        compiler_params=params_of(2),
        name="reverse",
    )(grad, forget, prm)


def run_gates_back(ext, open_w, forget_w, prm, ends, mixed, opened, forget, states, local, product):
    length, channels = mixed.shape
    chunk = min(CHUNK, length)
    steps = length // chunk
    pairs = channels // PAIR
    whole = pl.BlockSpec((length + 8, PAIR), lambda j, i: (0, j))
    held = pl.BlockSpec((length, PAIR), lambda j, i: (0, j))
    weight = pl.BlockSpec((None, PAIR, PAIR), lambda j, i: (j, 0, 0))
    row = pl.BlockSpec((8, PAIR), lambda j, i: (0, j))
    part = pl.BlockSpec((chunk, PAIR), lambda j, i: (steps - 1 - i, j))
    return pl.pallas_call(
        gates_back_kernel,
        grid=(pairs, steps),
        in_specs=[whole, weight, weight, row, row, part, part, part, held, part, part],
        out_specs=[part, row, weight, weight, row],
        out_shape=[
            jax.ShapeDtypeStruct((length, channels), F32),
            jax.ShapeDtypeStruct((8, channels), F32),
            jax.ShapeDtypeStruct((pairs, PAIR, PAIR), F32),
            jax.ShapeDtypeStruct((pairs, PAIR, PAIR), F32),
            jax.ShapeDtypeStruct((8, channels), F32),
        ],
        scratch_shapes=[pltpu.VMEM((8, PAIR), F32)],
        compiler_params=params_of(2),
        name="gates_back",
    )(ext, open_w, forget_w, prm, ends, mixed, opened, forget, states, local, product)


def paired(blocks):
    head = blocks.shape[1]
    split = blocks.reshape(-1, 2, head, head)
    none = jnp.zeros_like(split[:, 0])
    above = jnp.concatenate([split[:, 0], none], axis=2)
    below = jnp.concatenate([none, split[:, 1]], axis=2)
    return jnp.concatenate([above, below], axis=1)


def unpaired(pairs):
    head = pairs.shape[1] // 2
    blocks = jnp.stack([pairs[:, :head, :head], pairs[:, head:, head:]], axis=1)
    return blocks.reshape(-1, head)


def on_device(
    block_in,
    conv_state,
    init_state,
    cotangent,
    prenorm,
    recurrent,
    sidebranch,
    convolve,
    convbias,
    inputgate,
    inputbias,
    decaygate,
    decaybias,
    decayrate,
    outproject,
    midnorm,
    gating,
    upward,
    downward,
):
    core = lax.axis_index("c")
    first = core == 0
    ny, nz = lax.axis_size("y"), lax.axis_size("z")
    chips = ny * nz
    chip = lax.axis_index("y") * nz + lax.axis_index("z")
    rows = block_in.shape[1]
    width = recurrent.shape[1] // 2
    hidden_width = gating.shape[1] // 2
    head = inputgate.shape[1]
    model = block_in.shape[2]
    taps = convolve.shape[0]

    def in_order(own, other, axis=0):
        return jnp.concatenate([jnp.where(first, own, other), jnp.where(first, other, own)], axis=axis)

    def half(array, which, axis):
        size = array.shape[axis] // 2
        low = lax.slice_in_dim(array, 0, size, axis=axis)
        high = lax.slice_in_dim(array, size, 2 * size, axis=axis)
        return jnp.where(which == 0, low, high)

    shard = recurrent.shape[0]
    tall = inputgate.shape[0]
    out_blk = jnp.concatenate(
        [outproject, inputgate, decaygate, jnp.zeros((tall, 128), BF16)], axis=1
    )
    span = out_blk.shape[1]
    extra = out_blk[shard:]
    extra = jnp.concatenate([extra[:, : span // 2], extra[:, span // 2 :]], axis=0)
    vectors = jnp.concatenate([convolve, convbias[None], inputbias[None], decaybias[None], decayrate[None]], axis=0)
    gains = jnp.pad(jnp.concatenate([prenorm[None], midnorm[None]], axis=0), ((0, shard - 2), (0, 0)))
    vectors = jnp.concatenate([jnp.pad(vectors, ((0, shard - 8), (0, 0))), gains], axis=1)
    vectors = jnp.pad(vectors, ((0, 0), (0, 128 - vectors.shape[1])))
    temporal_blk = jnp.concatenate([recurrent, sidebranch, out_blk[:shard], extra, vectors], axis=1)
    temporal_all = lax.all_gather(temporal_blk, ("y", "z", "c", "x"), axis=0, tiled=True)

    mine = jnp.concatenate([half(gating, core, 1), half(upward, core, 1)], axis=1)
    theirs = jnp.concatenate([half(gating, 1 - core, 1), half(upward, 1 - core, 1)], axis=1)
    theirs, down_blk, x_other, grad_other = tied(
        swap_cores(theirs), to_half(downward), swap_cores(block_in[0]), swap_cores(cotangent[0])
    )
    x_low = in_order(block_in[0], x_other)
    grad_low = in_order(cotangent[0], grad_other)
    onward = [(i, i + 1) for i in range(chips - 1)]
    back = [(i + 1, i) for i in range(chips - 1)]

    both = in_order(mine[None], theirs[None])
    (gu_blk, down_blk), (x_before,) = gather_round(
        [(both, "x", 1), (down_blk, "y", 0)], lax.ppermute(x_low[-8:], ("y", "z"), onward)
    )
    (gating_blk, upward_blk, down_blk), _ = gather_round(
        [(gu_blk[..., :hidden_width], "y", 0), (gu_blk[..., hidden_width:], "z", 0), (down_blk, "z", 1)]
    )

    temporal_all = temporal_all.reshape(-1, shard, temporal_all.shape[-1])
    count = temporal_all.shape[0]
    rec_w = lax.dynamic_slice_in_dim(temporal_all, core * width, width, axis=2).reshape(-1, width)
    side_w = lax.dynamic_slice_in_dim(temporal_all, 2 * width + core * width, width, axis=2).reshape(-1, width)
    at = 4 * width
    halved = lax.dynamic_slice(
        temporal_all, (core * (count // 2), 0, at), (count // 2, shard, temporal_all.shape[-1] - at)
    )
    short = tall - shard
    extra = halved[:, :, span : span + span // 2]
    extra = jnp.concatenate([extra[:, :short], extra[:, short : 2 * short]], axis=2)
    out_all = jnp.concatenate([halved[:, :, :span], extra], axis=1).reshape(-1, span)
    at = span + span // 2
    prm = halved[:, :8, at : at + tall].transpose(1, 0, 2).reshape(8, -1).astype(F32)
    gains = temporal_all[:, :2, 4 * width + at + tall : 4 * width + at + tall + shard].astype(F32)
    pre_gain, mid_gain = gains[:, 0].reshape(-1), gains[:, 1].reshape(-1)
    out_w = out_all[:, :model]
    open_w = paired(out_all[:, model : model + head])
    shut_w = paired(out_all[:, model + head : model + 2 * head])
    rate = prm[7]
    prm = jnp.concatenate([prm[:7], -8.0 * jax.nn.softplus(rate)[None]], axis=0)

    tokens = x_low.astype(F32)
    pre_scale = rms_scale(tokens)
    normed = (tokens * pre_scale * pre_gain).astype(BF16)
    before = x_before.astype(F32)
    normed_before = (before * rms_scale(before) * pre_gain).astype(BF16)
    branch_ext = dot(jnp.concatenate([normed_before, normed], axis=0), rec_w, 1, 0)
    conv_prev = jnp.pad(half(conv_state[0], core, 1), ((8 - taps + 1, 2 * rows), (0, 0)))
    is_before = lax.broadcasted_iota(jnp.int32, branch_ext.shape, 0) < 8
    branch_ext = jnp.where(is_before & (chip == 0), conv_prev, branch_ext)
    side_pre = dot(normed, side_w, 1, 0)
    side_act, side_back = jax.vjp(jax.nn.gelu, side_pre)
    mixed, opened, forget, local, product = run_gates(branch_ext, open_w, shut_w, prm)
    ends = jnp.concatenate([product[-1:], local[-1:], branch_ext[-6:]], axis=0)
    (gating_w, upward_w, down_w), (ends,) = gather_round(
        [(gating_blk, "z", 1), (upward_blk, "y", 0), (down_blk, "x", 2)], ends
    )
    (all_ends,), _ = gather_round([(ends, "z", 0)])
    all_ends, gating_w, upward_w = tied(all_ends, gating_w, upward_w)
    (all_ends,), _ = gather_round([(all_ends, "y", 0)])
    all_ends, down_w = tied(all_ends.reshape(chips, *ends.shape), down_w)
    gating_w, upward_w, down_w = (w.reshape(-1, w.shape[-1]) for w in (gating_w, upward_w, down_w))
    products, lasts = all_ends[:, 0], all_ends[:, 1]
    state = half(init_state[0], core, 0)
    start = state
    for i in range(chips):
        start = jnp.where(chip == i, state, start)
        state = products[i] * state + lasts[i]
    states = local + product * start
    mixed_rec = (states * side_act).astype(BF16)
    branch_part = dot(mixed_rec, out_w, 1, 0)
    resid = tokens + (branch_part + swap_cores(branch_part))

    nx = lax.axis_size("x")
    mid_scale = rms_scale(resid)
    mid_low = (resid * mid_scale * mid_gain).astype(BF16)
    gate_pre = dot(mid_low, gating_w, 1, 0)
    up_pre = dot(mid_low, upward_w, 1, 0)
    gate_act, gelu_back = jax.vjp(jax.nn.gelu, gate_pre)
    hidden = (gate_act * up_pre).astype(BF16)
    grad_down = dot(hidden, grad_low, 0, 0).astype(BF16)
    grad_down = lax.psum_scatter(grad_down, "y", scatter_dimension=0, tiled=True)
    grad_hidden = dot(grad_low, down_w, 1, 1)
    grad_gate = gelu_back(grad_hidden * up_pre)[0].astype(BF16)
    grad_up = (grad_hidden * gate_act).astype(BF16)
    grad_gating = dot(mid_low, grad_gate, 0, 0).astype(BF16)
    gating_parts = scatter_send(split_cols(grad_gating, shard), "z", 1)
    grad_upward = dot(mid_low, grad_up, 0, 0).astype(BF16)
    upward_parts = scatter_send(split_cols(grad_upward, shard), "x", 3)
    mid_part = dot(grad_gate, gating_w, 1, 1) + dot(grad_up, upward_w, 1, 1)
    grad_mid = mid_part + swap_cores(mid_part.astype(BF16)).astype(F32)
    scaled = mid_gain * grad_mid
    grad_resid = (
        grad_low.astype(F32)
        + mid_scale * scaled
        - resid * mid_scale**3 * jnp.mean(scaled * resid, axis=-1, keepdims=True)
    )

    grad_branch = grad_resid.astype(BF16)
    grad_mixed = dot(grad_branch, out_w, 1, 1)
    grad_states = grad_mixed * side_act
    grad_side = side_back(grad_mixed * states)[0].astype(BF16)
    grad_out = dot(mixed_rec, grad_branch, 0, 0).astype(BF16)
    grad_out = lax.psum_scatter(grad_out, "y", scatter_dimension=0, tiled=True)
    back_local, back_product, back_first = run_reverse(grad_states, forget, prm)
    back_first, gating_parts, upward_parts = tied(back_first, gating_parts, upward_parts)
    (firsts,), _ = gather_round([(back_first, "z", 0)])
    (firsts,), _ = gather_round([(firsts, "y", 0)])
    firsts = firsts.reshape(chips, *back_first.shape)[:, 0]
    grad_sidebranch = dot(normed, grad_side, 0, 0).astype(BF16)
    grad_sidebranch = lax.psum_scatter(grad_sidebranch, "y", scatter_dimension=0, tiled=True)
    carry = jnp.zeros((width,), F32)
    coming = carry
    for i in reversed(range(chips)):
        coming = jnp.where(chip == i, carry, coming)
        carry = firsts[i] + products[i] * carry
    mlp_grads = jnp.concatenate(
        [add_up(parts).astype(BF16).reshape(ny, -1, hidden_width) for parts in (gating_parts, upward_parts)], axis=2
    )
    mlp_grads, coming = tied(mlp_grads, coming)
    mlp_parts = scatter_send(mlp_grads, "y", 0)
    grad_ext, grad_head, grad_open, grad_shut, sums = run_gates_back(
        branch_ext, open_w, shut_w, prm,
        jnp.concatenate([start[None], coming[None], jnp.zeros((6, width), F32)], axis=0),
        mixed, opened, forget, states, back_local, back_product,
    )
    grad_head, mlp_parts = tied(grad_head, mlp_parts)
    from_next = lax.ppermute(grad_head, ("y", "z"), back)
    grad_x = jnp.concatenate([grad_ext[:-8], grad_ext[-8:] + from_next], axis=0).astype(BF16)
    grad_recurrent = dot(normed, grad_x, 0, 0)

    sums = jnp.concatenate([sums[:7], sums[7:] * (-8.0 * jax.nn.sigmoid(rate))[None]], axis=0)
    gate_grads = jnp.concatenate(
        [unpaired(grad_open), unpaired(grad_shut), jnp.pad(sums.T, ((0, 0), (0, 120)))], axis=1
    )
    gate_parts = scatter_send(split_rows(gate_grads, tall), "x", 2)
    rec_parts = scatter_send(split_cols(grad_recurrent, shard), "y", 0)
    pre_part = dot(grad_x, rec_w, 1, 1) + dot(grad_side, side_w, 1, 1)
    rec_parts, gate_parts = tied(rec_parts, gate_parts)

    def flat(grad):
        return grad.astype(BF16).reshape(*grad.shape[:2], shard, -1)

    def side_by_side(grad):
        grad = grad.astype(BF16)
        return jnp.concatenate([grad[:, 0], grad[:, 1]], axis=-1)

    over_z = jnp.concatenate(
        [
            side_by_side(grad_sidebranch.reshape(nz, 2, nx, shard, width)),
            side_by_side(add_up(rec_parts)),
            flat(grad_out.reshape(nz, nx, tall, model)),
            flat(grad_down.reshape(nz, nx, -1, model)),
        ],
        axis=-1,
    )
    over_z, over_y = tied(scatter_send(over_z, "z", 0), scatter_send(add_up(gate_parts), "y", 0))
    swapped = swap_cores(half(pre_part, 1 - core, 0).astype(BF16))
    mlp_sum = add_up(mlp_parts).astype(BF16)
    gating_sum = mlp_sum[:, :hidden_width].reshape(1, 2, nx, shard, hidden_width)
    upward_sum = mlp_sum[:, hidden_width:].reshape(nz, 2, 1, shard, hidden_width)
    over_x = jnp.concatenate([add_up(over_z).astype(BF16), side_by_side(gating_sum)[0]], axis=-1)
    over_z = jnp.concatenate([flat(add_up(over_y)[:, None])[:, 0], side_by_side(upward_sum)[:, 0]], axis=-1)
    over_x, over_z, swapped = tied(scatter_send(over_x, "x", 0), scatter_send(over_z, "z", 0), swapped)
    over_x, over_z = add_up(over_x), add_up(over_z)
    sizes = [2 * width, 2 * width, outproject.size // shard, downward.size // shard]
    side, rec, out, down, gating_g = jnp.split(over_x, [sum(sizes[: i + 1]) for i in range(4)], axis=1)
    gates_g, upward_g = jnp.split(over_z, [gate_grads.shape[1] * tall // shard], axis=1)
    lows = jnp.concatenate(
        [side[:, :width], rec[:, :width], gating_g[:, :hidden_width], upward_g[:, :hidden_width]], axis=1
    )
    highs = jnp.concatenate(
        [side[:, width:], rec[:, width:], gating_g[:, hidden_width:], upward_g[:, hidden_width:]], axis=1
    )
    rows_out = jnp.concatenate(
        [out.reshape(outproject.shape), gates_g.reshape(tall, -1), down.reshape(tall, -1)], axis=1
    )
    kept = jnp.where(first, lows, highs)
    came, rows_out = tied(swap_cores(jnp.where(first, highs, lows)), to_owner(rows_out))

    def whole(at, size):
        return in_order(kept[:, at : at + size], came[:, at : at + size], axis=1)

    grad_sidebranch = whole(0, width)
    grad_recurrent = whole(width, width)
    grad_gating = whole(2 * width, hidden_width)
    grad_upward = whole(2 * width + hidden_width, hidden_width)
    grad_out, gate_grads, grad_down = jnp.split(rows_out, [model, model + 2 * head + 128], axis=1)
    grad_down = grad_down.reshape(downward.shape)

    grad_pre = half(pre_part, core, 0) + swapped.astype(F32)
    own = block_in[0].astype(F32)
    own_scale = rms_scale(own)
    scaled = pre_gain * grad_pre
    grad_in = half(grad_resid, core, 0) + (
        own_scale * scaled - own * own_scale**3 * jnp.mean(scaled * own, axis=-1, keepdims=True)
    )
    result_part = dot(hidden, down_w, 1, 0)
    result = half(resid + result_part, core, 0) + swap_cores(half(result_part, 1 - core, 0).astype(BF16)).astype(F32)

    def along(weight, grad):
        return jnp.sum(weight.astype(F32) * grad, axis=1)

    grad_prenorm = (along(recurrent, grad_recurrent) + along(sidebranch, grad_sidebranch)) / prenorm.astype(F32)
    grad_midnorm = (along(gating, grad_gating) + along(upward, grad_upward)) / midnorm.astype(F32)
    small = gate_grads[:, 2 * head : 2 * head + 8].T

    finals = jnp.concatenate([all_ends[-1, 8 - taps + 1 :], state[None]], axis=0)
    finals = jnp.where(core == lax.axis_index("y") // (ny // 2), finals, swap_cores(finals))
    slot = width // chips
    finals = lax.dynamic_slice_in_dim(finals, ((chip * 2 + core) % chips) * slot, slot, axis=1)

    return (
        result.astype(BF16)[None],
        grad_in.astype(BF16)[None],
        finals[None, : taps - 1],
        finals[None, taps - 1],
        grad_prenorm,
        grad_recurrent,
        grad_sidebranch,
        small[:4],
        small[4],
        gate_grads[:, :head],
        small[5],
        gate_grads[:, head : 2 * head],
        small[6],
        small[7],
        grad_out,
        grad_midnorm,
        grad_gating,
        grad_upward,
        grad_down,
    )


def solution(mesh):
    seq, dp = mesh.shape["seq"], mesh.shape["dp"]
    side = next(s for s in range(1, seq + 1) if 2 * s * s >= seq)
    fine = Mesh(mesh.devices.reshape(side, side, 2, dp), ("y", "z", "c", "x"))
    part = ("y", "z", "c")
    every = ("y", "z", "c", "x")
    vector, matrix = P(every), P(every, None)
    placed = (
        P("x", part, None),
        P("x", None, None),
        P("x", None),
        P("x", part, None),
        vector,
        matrix,
        matrix,
        P(None, every),
        vector,
        matrix,
        vector,
        matrix,
        vector,
        vector,
        matrix,
        vector,
        matrix,
        matrix,
        matrix,
    )
    return jax.shard_map(
        on_device,
        mesh=fine,
        in_specs=placed,
        out_specs=(P("x", part, None), P("x", part, None), P("x", None, part), P("x", part)) + placed[4:],
        check_vma=False,
    )
```

```python
import functools

import jax
import jax.numpy as jnp
from jax import lax
from jax.experimental import pallas as pl
from jax.experimental.pallas import tpu as pltpu
from jax.sharding import Mesh
from jax.sharding import PartitionSpec as P

EPSILON = 1e-06
F32 = jnp.float32
BF16 = jnp.bfloat16
RANK = {"y": 0, "z": 1, "c": 2, "x": 3}
SWAP = [(0, 1), (1, 0)]
VMEM = 20 * 1024 * 1024


def dot(left, right, left_dim, right_dim):
    return lax.dot_general(
        left, right, (((left_dim,), (right_dim,)), ((), ())), preferred_element_type=F32
    )


def rms_scale(values):
    return lax.rsqrt(jnp.mean(values * values, axis=-1, keepdims=True) + EPSILON)


def fetch(block, axis, by):
    count = lax.axis_size(axis)
    return lax.ppermute(block, axis, [(i, (i - by) % count) for i in range(count)])


def swap_cores(block):
    return lax.ppermute(block, "c", SWAP)


def place_of(held, axis):
    return sum(RANK[h] < RANK[axis] for h in held)


def gather_round(jobs, *others):
    pieces = [[fetch(block, axis, by) for by in range(1, lax.axis_size(axis))] for block, axis, _ in jobs]
    pieces, others = lax.optimization_barrier((pieces, others))
    results = []
    for (block, axis, place), held in zip(jobs, pieces):
        count, me = lax.axis_size(axis), lax.axis_index(axis)
        shape = block.shape[:place] + (count,) + block.shape[place:]
        out = jnp.broadcast_to(jnp.expand_dims(block, place), shape)
        for by, piece in enumerate(held, 1):
            out = lax.dynamic_update_index_in_dim(out, piece, (me + by) % count, place)
        results.append(out)
    return results, others


def scatter_send(array, axis, place, steps=None):
    array = array.astype(BF16)
    count, me = lax.axis_size(axis), lax.axis_index(axis)
    pick = lambda by: lax.dynamic_index_in_dim(array, (me + by) % count, place, keepdims=False)
    return [pick(by) if by == 0 else fetch(pick(by), axis, -by) for by in (steps or range(count))]


def add_up(pieces):
    total = pieces[0].astype(F32)
    for piece in pieces[1:]:
        total = total + piece.astype(F32)
    return total


def tied(*values):
    return lax.optimization_barrier(values)


def split_cols(grad, rows):
    sizes = [lax.axis_size(a) for a in ("y", "z", "c", "x")]
    return grad.astype(BF16).reshape(*sizes, rows, grad.shape[-1])


def split_rows(grad, rows):
    sizes = [lax.axis_size(a) for a in ("y", "z", "x")]
    return grad.astype(BF16).reshape(*sizes, rows, grad.shape[-1])


def owners(inverse):
    ny, nz = lax.axis_size("y"), lax.axis_size("z")
    pairs = []
    for y in range(ny):
        for z in range(nz):
            for c in (0, 1):
                block = ((y % (ny // 2)) * nz + z) * 2 + c
                pairs.append(((y * nz + z) * 2 + c, block * 2 + y // (ny // 2)))
    return [(b, a) for a, b in pairs] if inverse else pairs


def to_half(block):
    return lax.ppermute(block, ("y", "z", "c"), owners(False))


def to_owner(block):
    return lax.ppermute(block, ("y", "z", "c"), owners(True))


def one_less_square(log_decay, decay):
    twice = 2.0 * log_decay
    series = 1.0 + twice * (1.0 / 7.0)
    for order in (6.0, 5.0, 4.0, 3.0, 2.0):
        series = 1.0 + twice * (1.0 / order) * series
    return jnp.where(twice > -0.25, -twice * series, 1.0 - decay * decay)


def split_dot(values, weight):
    high = values.astype(BF16)
    rest = (values - high.astype(F32)).astype(BF16)
    return dot(high, weight, 1, 0) + dot(rest, weight, 1, 0)


def convolved(ext, prm, chunk):
    mixed = prm[4:5] + prm[0:1] * ext[8 : 8 + chunk]
    for tap in range(1, 4):
        mixed = mixed + prm[tap : tap + 1] * ext[8 - tap : 8 - tap + chunk]
    return mixed


def gates_kernel(
    ext_ref, open_ref, forget_ref, prm_ref,
    opened_out, forget_out, local_out, product_out,
    decay_s, drive_s, carry_s,
):
    step = pl.program_id(1)
    chunk, width = opened_out.shape

    @pl.when(step == 0)
    def _():
        carry_s[0:1, :] = jnp.zeros((1, width), F32)
        carry_s[1:2, :] = jnp.ones((1, width), F32)

    start = pl.multiple_of(step * chunk, chunk)
    ext = ext_ref[pl.ds(start, chunk + 8), :]
    prm = prm_ref[...]
    mixed = convolved(ext, prm, chunk)
    opened = jax.nn.sigmoid(split_dot(mixed, open_ref[...]) + prm[5:6])
    forget = jax.nn.sigmoid(split_dot(mixed, forget_ref[...]) + prm[6:7])
    log_decay = forget * prm[7:8]
    decay = jnp.exp(log_decay)
    opened_out[...] = opened
    forget_out[...] = forget
    decay_s[...] = decay
    drive_s[...] = jnp.sqrt(one_less_square(log_decay, decay)) * opened * mixed
    rows = lax.broadcasted_iota(jnp.int32, (8, width), 0)

    def group(index, carry):
        state, product = carry
        at = pl.ds(pl.multiple_of(index * 8, 8), 8)
        a, b = decay_s[at, :], drive_s[at, :]
        for by in (1, 2, 4):
            inside = rows >= by
            b = jnp.where(inside, a * pltpu.roll(b, by, 0) + b, b)
            a = jnp.where(inside, a * pltpu.roll(a, by, 0), a)
        local = b + a * state
        total = a * product
        local_out[at, :] = local
        product_out[at, :] = total
        return local[7:8], total[7:8]

    state, product = lax.fori_loop(0, chunk // 8, group, (carry_s[0:1, :], carry_s[1:2, :]), unroll=4)
    carry_s[0:1, :] = state
    carry_s[1:2, :] = product


def reverse_kernel(grad_ref, forget_ref, prm_ref, local_out, product_out, first_out, decay_s, carry_s):
    step = pl.program_id(1)
    chunk, width = local_out.shape

    @pl.when(step == 0)
    def _():
        carry_s[0:1, :] = jnp.zeros((1, width), F32)
        carry_s[1:2, :] = jnp.ones((1, width), F32)
        carry_s[2:3, :] = jnp.ones((1, width), F32)

    decay = jnp.exp(forget_ref[...] * prm_ref[7:8, :])
    last = carry_s[2:3, :]
    decay_s[0:chunk, :] = decay
    carry_s[2:3, :] = decay[0:1]
    rows = lax.broadcasted_iota(jnp.int32, (8, width), 0)
    following = jnp.where(
        lax.broadcasted_iota(jnp.int32, (chunk, width), 0) == chunk - 1, last, pltpu.roll(decay, chunk - 1, 0)
    )
    decay_s[...] = following

    def group(index, carry):
        state, product = carry
        at = pl.ds(pl.multiple_of(chunk - 8 - index * 8, 8), 8)
        a, b = decay_s[at, :], grad_ref[at, :]
        for by in (1, 2, 4):
            inside = rows < 8 - by
            b = jnp.where(inside, a * pltpu.roll(b, 8 - by, 0) + b, b)
            a = jnp.where(inside, a * pltpu.roll(a, 8 - by, 0), a)
        local = b + a * state
        total = a * product
        local_out[at, :] = local
        product_out[at, :] = total
        return local[0:1], total[0:1]

    state, product = lax.fori_loop(0, chunk // 8, group, (carry_s[0:1, :], carry_s[1:2, :]), unroll=4)
    carry_s[0:1, :] = state
    carry_s[1:2, :] = product
    first_out[...] = jnp.broadcast_to(decay[0:1] * state, (8, width))


def gates_back_kernel(
    ext_ref, open_ref, shut_ref, prm_ref, ends_ref,
    opened_ref, forget_ref, states_ref, local_ref, product_ref,
    grad_out, head_out, grad_open, grad_shut, sums_out,
    next_s,
):
    step = pl.program_id(1)
    steps = pl.num_programs(1)
    chunk, width = opened_ref.shape

    @pl.when(step == 0)
    def _():
        next_s[...] = jnp.zeros_like(next_s)
        grad_open[...] = jnp.zeros_like(grad_open)
        grad_shut[...] = jnp.zeros_like(grad_shut)
        sums_out[...] = jnp.zeros_like(sums_out)

    place = steps - 1 - step
    start = pl.multiple_of(place * chunk, chunk)
    prm = prm_ref[...]
    opened, forget = opened_ref[...], forget_ref[...]
    ext = ext_ref[pl.ds(start, chunk + 8), :]
    mixed = convolved(ext, prm, chunk)
    log_decay = forget * prm[7:8]
    decay = jnp.exp(log_decay)
    scaled = jnp.sqrt(one_less_square(log_decay, decay))
    grad_drive = local_ref[...] + product_ref[...] * ends_ref[1:2, :]
    states = states_ref[pl.ds(start, chunk), :]
    before = states_ref[pl.ds(pl.multiple_of(jnp.maximum(start - 8, 0), 8), 8), :]
    before = jnp.where(place == 0, ends_ref[0:1, :], before[7:8])
    prior = jnp.where(
        lax.broadcasted_iota(jnp.int32, (chunk, width), 0) == 0, before, pltpu.roll(states, 1, 0)
    )
    grad_scaled = grad_drive * opened * mixed
    grad_log = grad_drive * decay * prior - grad_scaled * decay * decay / scaled
    grad_opened = grad_drive * scaled * mixed * opened * (1.0 - opened)
    grad_forget = grad_log * prm[7:8] * forget * (1.0 - forget)
    low_mixed = mixed.astype(BF16)
    low_opened = grad_opened.astype(BF16)
    low_forget = grad_forget.astype(BF16)
    grad_open[...] += dot(low_mixed, low_opened, 0, 0)
    grad_shut[...] += dot(low_mixed, low_forget, 0, 0)
    grad_mixed = (
        grad_drive * scaled * opened
        + dot(low_opened, open_ref[...], 1, 1)
        + dot(low_forget, shut_ref[...], 1, 1)
    )
    spread = jnp.concatenate([grad_mixed, next_s[...]], axis=0)
    grad = prm[0:1] * grad_mixed
    for tap in range(1, 4):
        grad = grad + prm[tap : tap + 1] * spread[tap : tap + chunk]
    grad_out[...] = grad
    first = grad_mixed[0:8]
    next_s[...] = first
    lead = jnp.concatenate([jnp.zeros((8, width), F32), first], axis=0)
    head = jnp.zeros((8, width), F32)
    for tap in range(1, 4):
        head = head + prm[tap : tap + 1] * lead[tap : tap + 8]
    head_out[...] = head
    total = lambda v: jnp.sum(v, axis=0, keepdims=True)
    sums_out[...] += jnp.concatenate(
        [total(grad_mixed * ext[8 - tap : 8 - tap + chunk]) for tap in range(4)]
        + [total(grad_mixed), total(grad_opened), total(grad_forget), total(grad_log * forget)],
        axis=0,
    )


PAIR = 384
CHUNK = 256


def params_of(steps):
    return pltpu.CompilerParams(vmem_limit_bytes=VMEM, dimension_semantics=("arbitrary",) * steps)


def cost(microseconds):
    return pl.CostEstimate(flops=int(microseconds * 1e9), bytes_accessed=0, transcendentals=0)


def run_gates(ext, open_w, forget_w, prm):
    length, channels = ext.shape[0] - 8, ext.shape[1]
    chunk = min(CHUNK, length)
    grid = (channels // PAIR, length // chunk)
    whole = pl.BlockSpec((length + 8, PAIR), lambda j, i: (0, j))
    weight = pl.BlockSpec((None, PAIR, PAIR), lambda j, i: (j, 0, 0))
    row = pl.BlockSpec((8, PAIR), lambda j, i: (0, j))
    part = pl.BlockSpec((chunk, PAIR), lambda j, i: (i, j))
    return pl.pallas_call(
        gates_kernel,
        grid=grid,
        in_specs=[whole, weight, weight, row],
        out_specs=[part] * 4,
        out_shape=[jax.ShapeDtypeStruct((length, channels), F32)] * 4,
        scratch_shapes=[pltpu.VMEM((chunk, PAIR), F32)] * 2 + [pltpu.VMEM((8, PAIR), F32)],
        compiler_params=params_of(2),
        cost_estimate=cost(1),
        name="gates",
    )(ext, open_w, forget_w, prm)


def run_reverse(grad, forget, prm):
    length, channels = grad.shape
    chunk = min(CHUNK, length)
    steps = length // chunk
    row = pl.BlockSpec((8, PAIR), lambda j, i: (0, j))
    part = pl.BlockSpec((chunk, PAIR), lambda j, i: (steps - 1 - i, j))
    full = jax.ShapeDtypeStruct((length, channels), F32)
    return pl.pallas_call(
        reverse_kernel,
        grid=(channels // PAIR, steps),
        in_specs=[part, part, row],
        out_specs=[part, part, row],
        out_shape=[full, full, jax.ShapeDtypeStruct((8, channels), F32)],
        scratch_shapes=[pltpu.VMEM((chunk, PAIR), F32), pltpu.VMEM((8, PAIR), F32)],
        compiler_params=params_of(2),
        cost_estimate=cost(1),
        name="reverse",
    )(grad, forget, prm)


def run_gates_back(ext, open_w, forget_w, prm, ends, opened, forget, states, local, product):
    length, channels = opened.shape
    chunk = min(CHUNK, length)
    steps = length // chunk
    pairs = channels // PAIR
    whole = pl.BlockSpec((length + 8, PAIR), lambda j, i: (0, j))
    held = pl.BlockSpec((length, PAIR), lambda j, i: (0, j))
    weight = pl.BlockSpec((None, PAIR, PAIR), lambda j, i: (j, 0, 0))
    row = pl.BlockSpec((8, PAIR), lambda j, i: (0, j))
    part = pl.BlockSpec((chunk, PAIR), lambda j, i: (steps - 1 - i, j))
    return pl.pallas_call(
        gates_back_kernel,
        grid=(pairs, steps),
        in_specs=[whole, weight, weight, row, row, part, part, held, part, part],
        out_specs=[part, row, weight, weight, row],
        out_shape=[
            jax.ShapeDtypeStruct((length, channels), F32),
            jax.ShapeDtypeStruct((8, channels), F32),
            jax.ShapeDtypeStruct((pairs, PAIR, PAIR), F32),
            jax.ShapeDtypeStruct((pairs, PAIR, PAIR), F32),
            jax.ShapeDtypeStruct((8, channels), F32),
        ],
        scratch_shapes=[pltpu.VMEM((8, PAIR), F32)],
        compiler_params=params_of(2),
        cost_estimate=cost(1),
        name="gates_back",
    )(ext, open_w, forget_w, prm, ends, opened, forget, states, local, product)


def pick_kernel(core_ref, gating_ref, upward_ref, *refs, shard):
    downs, (gating_out, upward_out, down_out) = refs[:-3], refs[-3:]
    gating_out[...] = gating_ref[...]
    upward_out[...] = upward_ref[...]
    downs = [ref[...].astype(F32) for ref in downs]
    rows = downs[0].shape[0]
    down_out[...] = jnp.concatenate(
        [block[at : at + shard] for at in range(0, rows, shard) for block in downs], axis=0
    ).astype(down_out.dtype)


def run_pick(weights, core, width, at, model, parts, shard):
    rows = weights.shape[0]
    steps = 8 if rows // 16 >= shard and rows % 128 == 0 else 1
    block, short = rows // steps, rows // 2 // steps
    left = at // width
    first = (at + 4 * width) // model
    cols = lambda which: pl.BlockSpec((block, width), lambda i, core: (i, left + 2 * which + core[0]))
    part = lambda which: pl.BlockSpec((short, model), lambda i, core: (core[0] * steps + i, first + which))
    out = pl.BlockSpec((block, width), lambda i, core: (i, 0))
    return pl.pallas_call(
        functools.partial(pick_kernel, shard=shard),
        grid_spec=pltpu.PrefetchScalarGridSpec(
            num_scalar_prefetch=1,
            grid=(steps,),
            in_specs=[cols(0), cols(1)] + [part(i) for i in range(parts)],
            out_specs=[out, out, pl.BlockSpec((short * parts, model), lambda i, core: (i, 0))],
        ),
        out_shape=[jax.ShapeDtypeStruct((rows, width), BF16)] * 2
        + [jax.ShapeDtypeStruct((rows // 2 * parts, model), BF16)],
        compiler_params=params_of(1),
        cost_estimate=cost(6),
        name="pick",
    )(core.reshape(1), *[weights] * (2 + parts))


def paired(blocks):
    head = blocks.shape[1]
    split = blocks.reshape(-1, 2, head, head)
    none = jnp.zeros_like(split[:, 0])
    above = jnp.concatenate([split[:, 0], none], axis=2)
    below = jnp.concatenate([none, split[:, 1]], axis=2)
    return jnp.concatenate([above, below], axis=1)


def unpaired(pairs):
    head = pairs.shape[1] // 2
    blocks = jnp.stack([pairs[:, :head, :head], pairs[:, head:, head:]], axis=1)
    return blocks.reshape(-1, head)


def on_device(
    block_in,
    conv_state,
    init_state,
    cotangent,
    prenorm,
    recurrent,
    sidebranch,
    convolve,
    convbias,
    inputgate,
    inputbias,
    decaygate,
    decaybias,
    decayrate,
    outproject,
    midnorm,
    gating,
    upward,
    downward,
):
    core = lax.axis_index("c")
    first = core == 0
    ny, nz = lax.axis_size("y"), lax.axis_size("z")
    chips = ny * nz
    chip = lax.axis_index("y") * nz + lax.axis_index("z")
    rows = block_in.shape[1]
    width = recurrent.shape[1] // 2
    hidden_width = gating.shape[1] // 2
    head = inputgate.shape[1]
    model = block_in.shape[2]
    taps = convolve.shape[0]

    def in_order(own, other, axis=0):
        return jnp.concatenate([jnp.where(first, own, other), jnp.where(first, other, own)], axis=axis)

    def half(array, which, axis):
        size = array.shape[axis] // 2
        low = lax.slice_in_dim(array, 0, size, axis=axis)
        high = lax.slice_in_dim(array, size, 2 * size, axis=axis)
        return jnp.where(which == 0, low, high)

    shard = recurrent.shape[0]
    tall = inputgate.shape[0]
    short = tall - shard

    def as_blocks(rows):
        cols = rows.shape[1] // 2
        return jnp.concatenate([rows[:shard], jnp.concatenate([rows[shard:, :cols], rows[shard:, cols:]], axis=0)], axis=1)

    def as_rows(blocks, cols):
        rest = blocks[:, :, cols:]
        rest = jnp.concatenate([rest[:, :short], rest[:, short : 2 * short]], axis=2)
        return jnp.concatenate([blocks[:, :, :cols], rest], axis=1).reshape(-1, cols)

    vectors = jnp.concatenate([convolve, convbias[None], inputbias[None], decaybias[None], decayrate[None]], axis=0)
    gains = jnp.pad(jnp.concatenate([prenorm[None], midnorm[None]], axis=0), ((0, shard - 2), (0, 0)))
    vectors = jnp.concatenate([jnp.pad(vectors, ((0, shard - 8), (0, 0))), gains], axis=1)
    gate_blk = as_blocks(jnp.concatenate([inputgate, decaygate], axis=1))
    spare = -(gate_blk.shape[1] + vectors.shape[1]) % 128
    gate_blk = jnp.concatenate([gate_blk, vectors, jnp.zeros((shard, spare), BF16)], axis=1)
    everyone = ("y", "z", "c", "x")
    parts = downward.shape[0] // shard
    downs = [downward[i * shard : (i + 1) * shard] for i in range(parts)]
    weights = lax.all_gather(
        jnp.concatenate([recurrent, sidebranch, gating, upward] + downs + [as_blocks(outproject), gate_blk], axis=1),
        everyone,
        axis=0,
        tiled=True,
    )

    x_other, grad_other = tied(swap_cores(block_in[0]), swap_cores(cotangent[0]))
    x_low = in_order(block_in[0], x_other)
    grad_low = in_order(cotangent[0], grad_other)
    onward = [(i, i + 1) for i in range(chips - 1)]
    back = [(i + 1, i) for i in range(chips - 1)]
    x_before = lax.ppermute(x_low[-8:], ("y", "z"), onward)
    weights, x_low, grad_low, x_before = tied(weights, x_low, grad_low, x_before)

    def half_cols(at, size):
        return lax.dynamic_slice_in_dim(weights, at + core * size, size, axis=1)

    at = 4 * (width + hidden_width) + parts * model
    span = model + model // 2
    blocks = weights.reshape(-1, shard, weights.shape[1])
    owners_half = blocks.shape[0] // 2
    halved = lax.dynamic_slice(
        blocks, (core * owners_half, 0, at + span), (owners_half, shard, gate_blk.shape[1])
    )
    gate_w = as_rows(halved[:, :, : 3 * head], 2 * head)
    open_w, shut_w = paired(gate_w[:, :head]), paired(gate_w[:, head:])
    prm = halved[:, :8, 3 * head : 3 * head + tall].transpose(1, 0, 2).reshape(8, -1).astype(F32)
    rate = prm[7]
    prm = jnp.concatenate([prm[:7], -8.0 * jax.nn.softplus(rate)[None]], axis=0)
    gains_at = at + span + 3 * head + tall
    gains = blocks[:, :2, gains_at : gains_at + shard].astype(F32)
    pre_gain, mid_gain = gains[:, 0].reshape(-1), gains[:, 1].reshape(-1)
    rec_w = half_cols(0, width)
    side_w = half_cols(2 * width, width)
    gating_w, upward_w, down_w = run_pick(weights, core, hidden_width, 4 * width, model, parts, shard)

    def over_chips(rows):
        return lax.all_to_all(jnp.broadcast_to(rows[None], (chips, *rows.shape)), ("y", "z"), 0, 0, tiled=True)

    tokens = x_low.astype(F32)
    pre_scale = rms_scale(tokens)
    normed = (tokens * pre_scale * pre_gain).astype(BF16)
    before = x_before.astype(F32)
    normed_before = (before * rms_scale(before) * pre_gain).astype(BF16)
    branch_ext = dot(jnp.concatenate([normed_before, normed], axis=0), rec_w, 1, 0)
    conv_prev = jnp.pad(half(conv_state[0], core, 1), ((8 - taps + 1, 2 * rows), (0, 0)))
    is_before = lax.broadcasted_iota(jnp.int32, branch_ext.shape, 0) < 8
    branch_ext = jnp.where(is_before & (chip == 0), conv_prev, branch_ext)
    side_pre = dot(normed, side_w, 1, 0)
    side_act, side_back = jax.vjp(jax.nn.gelu, side_pre)
    opened, forget, local, product = run_gates(branch_ext, open_w, shut_w, prm)
    out_w = as_rows(
        lax.dynamic_slice(blocks, (core * owners_half, 0, at), (owners_half, shard, span)), model
    )
    ends, out_w = tied(over_chips(jnp.concatenate([product[-1:], local[-1:]], axis=0)), out_w)
    products, lasts = ends[:, 0], ends[:, 1]
    state = half(init_state[0], core, 0)
    start = state
    for i in range(chips):
        start = jnp.where(chip == i, state, start)
        state = products[i] * state + lasts[i]
    states = local + product * start
    mixed_rec = (states * side_act).astype(BF16)
    branch_part = dot(mixed_rec, out_w, 1, 0)
    resid = tokens + (branch_part + swap_cores(branch_part))

    nx = lax.axis_size("x")
    mid_scale = rms_scale(resid)
    mid_low = (resid * mid_scale * mid_gain).astype(BF16)
    gate_pre = dot(mid_low, gating_w, 1, 0)
    up_pre = dot(mid_low, upward_w, 1, 0)
    gate_act, gelu_back = jax.vjp(jax.nn.gelu, gate_pre)
    hidden = (gate_act * up_pre).astype(BF16)
    grad_down = dot(hidden, grad_low, 0, 0).astype(BF16)
    grad_down = lax.psum_scatter(grad_down, "y", scatter_dimension=0, tiled=True)
    grad_hidden = dot(grad_low, down_w, 1, 1)
    grad_gate = gelu_back(grad_hidden * up_pre)[0].astype(BF16)
    grad_up = (grad_hidden * gate_act).astype(BF16)
    near = [by for by in (0, 1, lax.axis_size("x") - 1)][: lax.axis_size("x")]
    far = list(range(2, lax.axis_size("x") - 1))
    grad_gating = split_cols(dot(mid_low, grad_gate, 0, 0), shard)
    grad_upward = split_cols(dot(mid_low, grad_up, 0, 0), shard)
    gating_parts = scatter_send(grad_gating, "z", 1, near)
    upward_parts = scatter_send(grad_upward, "x", 3, near)
    mid_part = dot(grad_gate, gating_w, 1, 1) + dot(grad_up, upward_w, 1, 1)
    grad_mid = mid_part + swap_cores(mid_part.astype(BF16)).astype(F32)
    scaled = mid_gain * grad_mid
    grad_resid = (
        grad_low.astype(F32)
        + mid_scale * scaled
        - resid * mid_scale**3 * jnp.mean(scaled * resid, axis=-1, keepdims=True)
    )

    grad_branch = grad_resid.astype(BF16)
    grad_mixed = dot(grad_branch, out_w, 1, 1)
    grad_states = grad_mixed * side_act
    grad_side = side_back(grad_mixed * states)[0].astype(BF16)
    back_local, back_product, back_first = run_reverse(grad_states, forget, prm)
    back_first, grad_gating, grad_upward = tied(back_first, grad_gating, grad_upward)
    gating_parts += scatter_send(grad_gating, "z", 1, far) if far else []
    upward_parts += scatter_send(grad_upward, "x", 3, far) if far else []
    grad_out = dot(mixed_rec, grad_branch, 0, 0).astype(BF16)
    grad_out = lax.psum_scatter(grad_out, "y", scatter_dimension=0, tiled=True)
    grad_sidebranch = split_cols(dot(normed, grad_side, 0, 0), shard)
    side_parts = scatter_send(grad_sidebranch, "x", 3)
    firsts, gating_parts, upward_parts, side_parts = tied(
        over_chips(jnp.concatenate([back_first[:1], branch_ext[-taps + 1 :]], axis=0)),
        gating_parts,
        upward_parts,
        side_parts,
    )
    firsts, tails = firsts[:, 0], firsts[-1, 1:]
    carry = jnp.zeros((width,), F32)
    coming = carry
    for i in reversed(range(chips)):
        coming = jnp.where(chip == i, carry, coming)
        carry = firsts[i] + products[i] * carry
    mlp_sum, coming = tied(
        jnp.concatenate(
            [
                add_up(p).astype(BF16).reshape(ny, -1, p[0].shape[-1])
                for p in (gating_parts, upward_parts, side_parts)
            ],
            axis=2,
        ),
        coming,
    )
    mlp_parts = scatter_send(mlp_sum, "y", 0)
    grad_ext, grad_head, grad_open, grad_shut, sums = run_gates_back(
        branch_ext, open_w, shut_w, prm,
        jnp.concatenate([start[None], coming[None], jnp.zeros((6, width), F32)], axis=0),
        opened, forget, states, back_local, back_product,
    )
    from_next = lax.ppermute(grad_head, ("y", "z"), back)
    grad_x = jnp.concatenate([grad_ext[:-8], grad_ext[-8:] + from_next], axis=0).astype(BF16)

    def flat(grad):
        return grad.astype(BF16).reshape(*grad.shape[:2], shard, -1)

    def both_halves(grad, place):
        kept = jnp.where(first, lax.index_in_dim(grad, 0, place, False), lax.index_in_dim(grad, 1, place, False))
        sent = jnp.where(first, lax.index_in_dim(grad, 1, place, False), lax.index_in_dim(grad, 0, place, False))
        return in_order(kept, swap_cores(sent), axis=-1)

    sums = jnp.concatenate([sums[:7], sums[7:] * (-8.0 * jax.nn.sigmoid(rate))[None]], axis=0)
    gate_grads = jnp.concatenate(
        [unpaired(grad_open), unpaired(grad_shut), jnp.pad(sums.T, ((0, 0), (0, 120)))], axis=1
    )
    gate_grads = gate_grads.astype(BF16).reshape(-1, tall, gate_grads.shape[1])
    grad_recurrent = dot(normed, grad_x, 0, 0).astype(BF16).reshape(-1, shard, width)
    gate_grads = lax.all_to_all(gate_grads, ("y", "z", "x"), 0, 0, tiled=True)
    grad_recurrent, mlp_parts, grad_out, grad_down = tied(grad_recurrent, mlp_parts, grad_out, grad_down)
    rec_all = lax.all_to_all(grad_recurrent, everyone, 0, 0, tiled=True)
    mlp_sum = add_up(mlp_parts).astype(BF16)
    gating_sum = mlp_sum[:, :hidden_width].reshape(2, nx, shard, hidden_width)
    late_sum = mlp_sum[:, hidden_width:].reshape(nz, 2, shard, hidden_width + width)
    split = nx // 2
    late_sum = late_sum.reshape(nz, 2, shard, split, -1).transpose(0, 1, 3, 2, 4).reshape(nz, nx, shard, -1)
    over_z = jnp.concatenate(
        [late_sum, flat(grad_out.reshape(nz, nx, tall, model)), flat(grad_down.reshape(nz, nx, -1, model))], axis=-1
    )
    over_z = scatter_send(over_z, "z", 0)
    pre_part = dot(grad_x, rec_w, 1, 1) + dot(grad_side, side_w, 1, 1)
    swapped = swap_cores(half(pre_part, 1 - core, 0).astype(BF16))
    gating_sum = both_halves(gating_sum, 0)
    over_z, swapped, gate_grads = tied(over_z, swapped, gate_grads)
    gate_grads = jnp.sum(gate_grads.astype(F32), axis=0)
    over_z = add_up(over_z)
    cut = (hidden_width + width) // split
    late_sum = over_z[..., :cut].reshape(2, split, shard, cut).transpose(0, 2, 1, 3).reshape(2, shard, -1)
    late_sum = both_halves(late_sum, 0)
    over_x = jnp.concatenate([gating_sum, over_z[..., cut:].astype(BF16)], axis=-1)
    over_x, late_sum = tied(scatter_send(over_x, "x", 0), late_sum)
    over_x = add_up(over_x)
    grad_gating, out, down = jnp.split(
        over_x, [2 * hidden_width, 2 * hidden_width + outproject.size // shard], axis=1
    )
    total = hidden_width + width
    grad_upward = jnp.concatenate([late_sum[:, :hidden_width], late_sum[:, total : total + hidden_width]], axis=1)
    grad_sidebranch = jnp.concatenate([late_sum[:, hidden_width:total], late_sum[:, total + hidden_width :]], axis=1)
    rows_out = to_owner(
        jnp.concatenate([out.reshape(outproject.shape), gate_grads, down.reshape(tall, -1)], axis=1)
    )
    rec_all = jnp.sum(rec_all.reshape(ny, nz, 2, nx, shard, width).astype(F32), axis=(0, 1, 3))
    grad_recurrent = jnp.concatenate([rec_all[0], rec_all[1]], axis=1)
    grad_out, gate_grads, grad_down = jnp.split(rows_out, [model, model + 2 * head + 128], axis=1)
    grad_down = grad_down.reshape(downward.shape)

    grad_pre = half(pre_part, core, 0) + swapped.astype(F32)
    own = block_in[0].astype(F32)
    own_scale = rms_scale(own)
    scaled = pre_gain * grad_pre
    grad_in = half(grad_resid, core, 0) + (
        own_scale * scaled - own * own_scale**3 * jnp.mean(scaled * own, axis=-1, keepdims=True)
    )
    result_part = dot(hidden, down_w, 1, 0)
    result = half(resid + result_part, core, 0) + swap_cores(half(result_part, 1 - core, 0).astype(BF16)).astype(F32)

    def along(left, grad_left, right, grad_right):
        return jnp.sum(left.astype(F32) * grad_left + right.astype(F32) * grad_right, axis=1)

    grad_prenorm = along(recurrent, grad_recurrent, sidebranch, grad_sidebranch) / prenorm.astype(F32)
    grad_midnorm = along(gating, grad_gating, upward, grad_upward) / midnorm.astype(F32)
    small = gate_grads[:, 2 * head : 2 * head + 8].T

    finals = jnp.concatenate([tails, state[None]], axis=0)
    finals = jnp.where(core == lax.axis_index("y") // (ny // 2), finals, swap_cores(finals))
    slot = width // chips
    finals = lax.dynamic_slice_in_dim(finals, ((chip * 2 + core) % chips) * slot, slot, axis=1)

    return (
        result.astype(BF16)[None],
        grad_in.astype(BF16)[None],
        finals[None, : taps - 1],
        finals[None, taps - 1],
        grad_prenorm,
        grad_recurrent,
        grad_sidebranch,
        small[:4],
        small[4],
        gate_grads[:, :head],
        small[5],
        gate_grads[:, head : 2 * head],
        small[6],
        small[7],
        grad_out,
        grad_midnorm,
        grad_gating,
        grad_upward,
        grad_down,
    )


def solution(mesh):
    seq, dp = mesh.shape["seq"], mesh.shape["dp"]
    side = next(s for s in range(1, seq + 1) if 2 * s * s >= seq)
    fine = Mesh(mesh.devices.reshape(side, side, 2, dp), ("y", "z", "c", "x"))
    part = ("y", "z", "c")
    every = ("y", "z", "c", "x")
    vector, matrix = P(every), P(every, None)
    placed = (
        P("x", part, None),
        P("x", None, None),
        P("x", None),
        P("x", part, None),
        vector,
        matrix,
        matrix,
        P(None, every),
        vector,
        matrix,
        vector,
        matrix,
        vector,
        vector,
        matrix,
        vector,
        matrix,
        matrix,
        matrix,
    )
    return jax.shard_map(
        on_device,
        mesh=fine,
        in_specs=placed,
        out_specs=(P("x", part, None), P("x", part, None), P("x", None, part), P("x", part)) + placed[4:],
        check_vma=False,
    )
```

```python
import functools

import jax
import jax.numpy as jnp
from jax import lax
from jax.experimental import pallas as pl
from jax.experimental.pallas import tpu as pltpu
from jax.sharding import Mesh
from jax.sharding import PartitionSpec as P

EPSILON = 1e-06
F32 = jnp.float32
BF16 = jnp.bfloat16
RANK = {"y": 0, "z": 1, "c": 2, "x": 3}
SWAP = [(0, 1), (1, 0)]
VMEM = 20 * 1024 * 1024


def dot(left, right, left_dim, right_dim):
    return lax.dot_general(
        left, right, (((left_dim,), (right_dim,)), ((), ())), preferred_element_type=F32
    )


def rms_scale(values):
    return lax.rsqrt(jnp.mean(values * values, axis=-1, keepdims=True) + EPSILON)


def fetch(block, axis, by):
    count = lax.axis_size(axis)
    return lax.ppermute(block, axis, [(i, (i - by) % count) for i in range(count)])


def swap_cores(block):
    return lax.ppermute(block, "c", SWAP)


def place_of(held, axis):
    return sum(RANK[h] < RANK[axis] for h in held)


def gather_round(jobs, *others):
    pieces = [[fetch(block, axis, by) for by in range(1, lax.axis_size(axis))] for block, axis, _ in jobs]
    pieces, others = lax.optimization_barrier((pieces, others))
    results = []
    for (block, axis, place), held in zip(jobs, pieces):
        count, me = lax.axis_size(axis), lax.axis_index(axis)
        shape = block.shape[:place] + (count,) + block.shape[place:]
        out = jnp.broadcast_to(jnp.expand_dims(block, place), shape)
        for by, piece in enumerate(held, 1):
            out = lax.dynamic_update_index_in_dim(out, piece, (me + by) % count, place)
        results.append(out)
    return results, others


def scatter_send(array, axis, place, steps=None):
    array = array.astype(BF16)
    count, me = lax.axis_size(axis), lax.axis_index(axis)
    pick = lambda by: lax.dynamic_index_in_dim(array, (me + by) % count, place, keepdims=False)
    return [pick(by) if by == 0 else fetch(pick(by), axis, -by) for by in (steps or range(count))]


def add_up(pieces):
    total = pieces[0].astype(F32)
    for piece in pieces[1:]:
        total = total + piece.astype(F32)
    return total


def tied(*values):
    return lax.optimization_barrier(values)


def split_cols(grad, rows):
    sizes = [lax.axis_size(a) for a in ("y", "z", "c", "x")]
    return grad.astype(BF16).reshape(*sizes, rows, grad.shape[-1])


def split_rows(grad, rows):
    sizes = [lax.axis_size(a) for a in ("y", "z", "x")]
    return grad.astype(BF16).reshape(*sizes, rows, grad.shape[-1])


def owners(inverse):
    ny, nz = lax.axis_size("y"), lax.axis_size("z")
    pairs = []
    for y in range(ny):
        for z in range(nz):
            for c in (0, 1):
                block = ((y % (ny // 2)) * nz + z) * 2 + c
                pairs.append(((y * nz + z) * 2 + c, block * 2 + y // (ny // 2)))
    return [(b, a) for a, b in pairs] if inverse else pairs


def to_half(block):
    return lax.ppermute(block, ("y", "z", "c"), owners(False))


def to_owner(block):
    return lax.ppermute(block, ("y", "z", "c"), owners(True))


def one_less_square(log_decay, decay):
    twice = 2.0 * log_decay
    series = 1.0 + twice * (1.0 / 7.0)
    for order in (6.0, 5.0, 4.0, 3.0, 2.0):
        series = 1.0 + twice * (1.0 / order) * series
    return jnp.where(twice > -0.25, -twice * series, 1.0 - decay * decay)


def split_dot(values, weight):
    high = values.astype(BF16)
    rest = (values - high.astype(F32)).astype(BF16)
    return dot(high, weight, 1, 0) + dot(rest, weight, 1, 0)


def convolved(ext, prm, chunk):
    mixed = prm[4:5] + prm[0:1] * ext[8 : 8 + chunk]
    for tap in range(1, 4):
        mixed = mixed + prm[tap : tap + 1] * ext[8 - tap : 8 - tap + chunk]
    return mixed


def gates_kernel(
    ext_ref, open_ref, forget_ref, prm_ref,
    opened_out, forget_out, local_out, product_out,
    decay_s, drive_s, carry_s,
):
    step = pl.program_id(1)
    chunk, width = opened_out.shape

    @pl.when(step == 0)
    def _():
        carry_s[0:1, :] = jnp.zeros((1, width), F32)
        carry_s[1:2, :] = jnp.ones((1, width), F32)

    start = pl.multiple_of(step * chunk, chunk)
    ext = ext_ref[pl.ds(start, chunk + 8), :]
    prm = prm_ref[...]
    mixed = convolved(ext, prm, chunk)
    opened = jax.nn.sigmoid(split_dot(mixed, open_ref[...]) + prm[5:6])
    forget = jax.nn.sigmoid(split_dot(mixed, forget_ref[...]) + prm[6:7])
    log_decay = forget * prm[7:8]
    decay = jnp.exp(log_decay)
    opened_out[...] = opened
    forget_out[...] = forget
    decay_s[...] = decay
    drive_s[...] = jnp.sqrt(one_less_square(log_decay, decay)) * opened * mixed
    rows = lax.broadcasted_iota(jnp.int32, (8, width), 0)

    def group(index, carry):
        state, product = carry
        at = pl.ds(pl.multiple_of(index * 8, 8), 8)
        a, b = decay_s[at, :], drive_s[at, :]
        for by in (1, 2, 4):
            inside = rows >= by
            b = jnp.where(inside, a * pltpu.roll(b, by, 0) + b, b)
            a = jnp.where(inside, a * pltpu.roll(a, by, 0), a)
        local = b + a * state
        total = a * product
        local_out[at, :] = local
        product_out[at, :] = total
        return local[7:8], total[7:8]

    state, product = lax.fori_loop(0, chunk // 8, group, (carry_s[0:1, :], carry_s[1:2, :]), unroll=4)
    carry_s[0:1, :] = state
    carry_s[1:2, :] = product


def reverse_kernel(grad_ref, forget_ref, prm_ref, local_out, product_out, first_out, decay_s, carry_s):
    step = pl.program_id(1)
    chunk, width = local_out.shape

    @pl.when(step == 0)
    def _():
        carry_s[0:1, :] = jnp.zeros((1, width), F32)
        carry_s[1:2, :] = jnp.ones((1, width), F32)
        carry_s[2:3, :] = jnp.ones((1, width), F32)

    decay = jnp.exp(forget_ref[...] * prm_ref[7:8, :])
    last = carry_s[2:3, :]
    decay_s[0:chunk, :] = decay
    carry_s[2:3, :] = decay[0:1]
    rows = lax.broadcasted_iota(jnp.int32, (8, width), 0)
    following = jnp.where(
        lax.broadcasted_iota(jnp.int32, (chunk, width), 0) == chunk - 1, last, pltpu.roll(decay, chunk - 1, 0)
    )
    decay_s[...] = following

    def group(index, carry):
        state, product = carry
        at = pl.ds(pl.multiple_of(chunk - 8 - index * 8, 8), 8)
        a, b = decay_s[at, :], grad_ref[at, :]
        for by in (1, 2, 4):
            inside = rows < 8 - by
            b = jnp.where(inside, a * pltpu.roll(b, 8 - by, 0) + b, b)
            a = jnp.where(inside, a * pltpu.roll(a, 8 - by, 0), a)
        local = b + a * state
        total = a * product
        local_out[at, :] = local
        product_out[at, :] = total
        return local[0:1], total[0:1]

    state, product = lax.fori_loop(0, chunk // 8, group, (carry_s[0:1, :], carry_s[1:2, :]), unroll=4)
    carry_s[0:1, :] = state
    carry_s[1:2, :] = product
    first_out[...] = jnp.broadcast_to(decay[0:1] * state, (8, width))


def gates_back_kernel(
    ext_ref, open_ref, shut_ref, prm_ref, ends_ref,
    opened_ref, forget_ref, states_ref, local_ref, product_ref,
    grad_out, head_out, grad_open, grad_shut, sums_out,
    next_s,
):
    step = pl.program_id(1)
    steps = pl.num_programs(1)
    chunk, width = opened_ref.shape

    @pl.when(step == 0)
    def _():
        next_s[...] = jnp.zeros_like(next_s)
        grad_open[...] = jnp.zeros_like(grad_open)
        grad_shut[...] = jnp.zeros_like(grad_shut)
        sums_out[...] = jnp.zeros_like(sums_out)

    place = steps - 1 - step
    start = pl.multiple_of(place * chunk, chunk)
    prm = prm_ref[...]
    opened, forget = opened_ref[...], forget_ref[...]
    ext = ext_ref[pl.ds(start, chunk + 8), :]
    mixed = convolved(ext, prm, chunk)
    log_decay = forget * prm[7:8]
    decay = jnp.exp(log_decay)
    square = one_less_square(log_decay, decay)
    inverse = lax.rsqrt(square)
    scaled = square * inverse
    grad_drive = local_ref[...] + product_ref[...] * ends_ref[1:2, :]
    states = states_ref[pl.ds(start, chunk), :]
    before = states_ref[pl.ds(pl.multiple_of(jnp.maximum(start - 8, 0), 8), 8), :]
    before = jnp.where(place == 0, ends_ref[0:1, :], before[7:8])
    prior = jnp.where(
        lax.broadcasted_iota(jnp.int32, (chunk, width), 0) == 0, before, pltpu.roll(states, 1, 0)
    )
    grad_scaled = grad_drive * opened * mixed
    grad_log = decay * (grad_drive * prior - grad_scaled * decay * inverse)
    grad_opened = scaled * grad_scaled * (1.0 - opened)
    grad_forget = grad_log * prm[7:8] * forget * (1.0 - forget)
    low_mixed = mixed.astype(BF16)
    low_opened = grad_opened.astype(BF16)
    low_forget = grad_forget.astype(BF16)
    grad_open[...] += dot(low_mixed, low_opened, 0, 0)
    grad_shut[...] += dot(low_mixed, low_forget, 0, 0)
    grad_mixed = (
        grad_drive * scaled * opened
        + dot(low_opened, open_ref[...], 1, 1)
        + dot(low_forget, shut_ref[...], 1, 1)
    )
    spread = jnp.concatenate([grad_mixed, next_s[...]], axis=0)
    grad = prm[0:1] * grad_mixed
    for tap in range(1, 4):
        grad = grad + prm[tap : tap + 1] * spread[tap : tap + chunk]
    grad_out[...] = grad
    first = grad_mixed[0:8]
    next_s[...] = first
    lead = jnp.concatenate([jnp.zeros((8, width), F32), first], axis=0)
    head = jnp.zeros((8, width), F32)
    for tap in range(1, 4):
        head = head + prm[tap : tap + 1] * lead[tap : tap + 8]
    head_out[...] = head
    total = lambda v: jnp.sum(v, axis=0, keepdims=True)
    sums_out[...] += jnp.concatenate(
        [total(grad_mixed * ext[8 - tap : 8 - tap + chunk]) for tap in range(4)]
        + [total(grad_mixed), total(grad_opened), total(grad_forget), total(grad_log * forget)],
        axis=0,
    )


PAIR = 384
CHUNK = 256


def params_of(steps):
    return pltpu.CompilerParams(vmem_limit_bytes=VMEM, dimension_semantics=("arbitrary",) * steps)


def cost(microseconds):
    return pl.CostEstimate(flops=int(microseconds * 1e9), bytes_accessed=0, transcendentals=0)


def in_hbm(array):
    return pltpu.with_memory_space_constraint(array, pltpu.HBM)


def run_gates(ext, open_w, forget_w, prm):
    length, channels = ext.shape[0] - 8, ext.shape[1]
    chunk = min(CHUNK, length)
    grid = (channels // PAIR, length // chunk)
    whole = pl.BlockSpec((length + 8, PAIR), lambda j, i: (0, j))
    weight = pl.BlockSpec((None, PAIR, PAIR), lambda j, i: (j, 0, 0))
    row = pl.BlockSpec((8, PAIR), lambda j, i: (0, j))
    part = pl.BlockSpec((chunk, PAIR), lambda j, i: (i, j))
    return pl.pallas_call(
        gates_kernel,
        grid=grid,
        in_specs=[whole, weight, weight, row],
        out_specs=[part] * 4,
        out_shape=[pltpu.HBM((length, channels), F32)] * 4,
        scratch_shapes=[pltpu.VMEM((chunk, PAIR), F32)] * 2 + [pltpu.VMEM((8, PAIR), F32)],
        compiler_params=params_of(2),
        cost_estimate=cost(1),
        name="gates",
    )(ext, open_w, forget_w, prm)


def run_reverse(grad, forget, prm):
    length, channels = grad.shape
    chunk = min(CHUNK, length)
    steps = length // chunk
    row = pl.BlockSpec((8, PAIR), lambda j, i: (0, j))
    part = pl.BlockSpec((chunk, PAIR), lambda j, i: (steps - 1 - i, j))
    full = pltpu.HBM((length, channels), F32)
    return pl.pallas_call(
        reverse_kernel,
        grid=(channels // PAIR, steps),
        in_specs=[part, part, row],
        out_specs=[part, part, row],
        out_shape=[full, full, jax.ShapeDtypeStruct((8, channels), F32)],
        scratch_shapes=[pltpu.VMEM((chunk, PAIR), F32), pltpu.VMEM((8, PAIR), F32)],
        compiler_params=params_of(2),
        cost_estimate=cost(1),
        name="reverse",
    )(grad, in_hbm(forget), prm)


def run_gates_back(ext, open_w, forget_w, prm, ends, opened, forget, states, local, product):
    length, channels = opened.shape
    chunk = min(CHUNK, length)
    steps = length // chunk
    pairs = channels // PAIR
    whole = pl.BlockSpec((length + 8, PAIR), lambda j, i: (0, j))
    held = pl.BlockSpec((length, PAIR), lambda j, i: (0, j))
    weight = pl.BlockSpec((None, PAIR, PAIR), lambda j, i: (j, 0, 0))
    row = pl.BlockSpec((8, PAIR), lambda j, i: (0, j))
    part = pl.BlockSpec((chunk, PAIR), lambda j, i: (steps - 1 - i, j))
    return pl.pallas_call(
        gates_back_kernel,
        grid=(pairs, steps),
        in_specs=[whole, weight, weight, row, row, part, part, held, part, part],
        out_specs=[part, row, weight, weight, row],
        out_shape=[
            jax.ShapeDtypeStruct((length, channels), F32),
            jax.ShapeDtypeStruct((8, channels), F32),
            jax.ShapeDtypeStruct((pairs, PAIR, PAIR), F32),
            jax.ShapeDtypeStruct((pairs, PAIR, PAIR), F32),
            jax.ShapeDtypeStruct((8, channels), F32),
        ],
        scratch_shapes=[pltpu.VMEM((8, PAIR), F32)],
        compiler_params=params_of(2),
        cost_estimate=cost(1),
        name="gates_back",
    )(ext, open_w, forget_w, prm, ends, *[in_hbm(v) for v in (opened, forget, states, local, product)])


def pick_kernel(core_ref, gating_ref, upward_ref, *refs, shard):
    downs, (gating_out, upward_out, down_out) = refs[:-3], refs[-3:]
    gating_out[...] = gating_ref[...]
    upward_out[...] = upward_ref[...]
    downs = [ref[...].astype(F32) for ref in downs]
    rows = downs[0].shape[0]
    down_out[...] = jnp.concatenate(
        [block[at : at + shard] for at in range(0, rows, shard) for block in downs], axis=0
    ).astype(down_out.dtype)


def run_pick(weights, core, width, at, model, parts, shard):
    rows = weights.shape[0]
    steps = 8 if rows // 16 >= shard and rows % 128 == 0 else 1
    block, short = rows // steps, rows // 2 // steps
    left = at // width
    first = (at + 4 * width) // model
    cols = lambda which: pl.BlockSpec((block, width), lambda i, core: (i, left + 2 * which + core[0]))
    part = lambda which: pl.BlockSpec((short, model), lambda i, core: (core[0] * steps + i, first + which))
    out = pl.BlockSpec((block, width), lambda i, core: (i, 0))
    return pl.pallas_call(
        functools.partial(pick_kernel, shard=shard),
        grid_spec=pltpu.PrefetchScalarGridSpec(
            num_scalar_prefetch=1,
            grid=(steps,),
            in_specs=[cols(0), cols(1)] + [part(i) for i in range(parts)],
            out_specs=[out, out, pl.BlockSpec((short * parts, model), lambda i, core: (i, 0))],
        ),
        out_shape=[jax.ShapeDtypeStruct((rows, width), BF16)] * 2
        + [jax.ShapeDtypeStruct((rows // 2 * parts, model), BF16)],
        compiler_params=params_of(1),
        cost_estimate=cost(6),
        name="pick",
    )(core.reshape(1), *[weights] * (2 + parts))


def paired(blocks):
    head = blocks.shape[1]
    split = blocks.reshape(-1, 2, head, head)
    none = jnp.zeros_like(split[:, 0])
    above = jnp.concatenate([split[:, 0], none], axis=2)
    below = jnp.concatenate([none, split[:, 1]], axis=2)
    return jnp.concatenate([above, below], axis=1)


def unpaired(pairs):
    head = pairs.shape[1] // 2
    blocks = jnp.stack([pairs[:, :head, :head], pairs[:, head:, head:]], axis=1)
    return blocks.reshape(-1, head)


def on_device(
    block_in,
    conv_state,
    init_state,
    cotangent,
    prenorm,
    recurrent,
    sidebranch,
    convolve,
    convbias,
    inputgate,
    inputbias,
    decaygate,
    decaybias,
    decayrate,
    outproject,
    midnorm,
    gating,
    upward,
    downward,
):
    core = lax.axis_index("c")
    first = core == 0
    ny, nz = lax.axis_size("y"), lax.axis_size("z")
    chips = ny * nz
    chip = lax.axis_index("y") * nz + lax.axis_index("z")
    rows = block_in.shape[1]
    width = recurrent.shape[1] // 2
    hidden_width = gating.shape[1] // 2
    head = inputgate.shape[1]
    model = block_in.shape[2]
    taps = convolve.shape[0]

    def in_order(own, other, axis=0):
        return jnp.concatenate([jnp.where(first, own, other), jnp.where(first, other, own)], axis=axis)

    def half(array, which, axis):
        size = array.shape[axis] // 2
        low = lax.slice_in_dim(array, 0, size, axis=axis)
        high = lax.slice_in_dim(array, size, 2 * size, axis=axis)
        return jnp.where(which == 0, low, high)

    shard = recurrent.shape[0]
    tall = inputgate.shape[0]
    short = tall - shard

    def as_blocks(rows):
        cols = rows.shape[1] // 2
        return jnp.concatenate([rows[:shard], jnp.concatenate([rows[shard:, :cols], rows[shard:, cols:]], axis=0)], axis=1)

    def as_rows(blocks, cols):
        rest = blocks[:, :, cols:]
        rest = jnp.concatenate([rest[:, :short], rest[:, short : 2 * short]], axis=2)
        return jnp.concatenate([blocks[:, :, :cols], rest], axis=1).reshape(-1, cols)

    vectors = jnp.concatenate([convolve, convbias[None], inputbias[None], decaybias[None], decayrate[None]], axis=0)
    gains = jnp.pad(jnp.concatenate([prenorm[None], midnorm[None]], axis=0), ((0, shard - 2), (0, 0)))
    vectors = jnp.concatenate([jnp.pad(vectors, ((0, shard - 8), (0, 0))), gains], axis=1)
    gate_blk = as_blocks(jnp.concatenate([inputgate, decaygate], axis=1))
    spare = -(gate_blk.shape[1] + vectors.shape[1]) % 128
    gate_blk = jnp.concatenate([gate_blk, vectors, jnp.zeros((shard, spare), BF16)], axis=1)
    everyone = ("y", "z", "c", "x")
    parts = downward.shape[0] // shard
    downs = [downward[i * shard : (i + 1) * shard] for i in range(parts)]
    weights = lax.all_gather(
        jnp.concatenate([recurrent, sidebranch, gating, upward] + downs + [as_blocks(outproject), gate_blk], axis=1),
        everyone,
        axis=0,
        tiled=True,
    )

    x_other, grad_other = tied(swap_cores(block_in[0]), swap_cores(cotangent[0]))
    x_low = in_order(block_in[0], x_other)
    grad_low = in_order(cotangent[0], grad_other)
    onward = [(i, i + 1) for i in range(chips - 1)]
    back = [(i + 1, i) for i in range(chips - 1)]
    x_before = lax.ppermute(x_low[-8:], ("y", "z"), onward)
    weights, x_low, grad_low, x_before = tied(weights, x_low, grad_low, x_before)

    def half_cols(at, size):
        return lax.dynamic_slice_in_dim(weights, at + core * size, size, axis=1)

    at = 4 * (width + hidden_width) + parts * model
    span = model + model // 2
    blocks = weights.reshape(-1, shard, weights.shape[1])
    owners_half = blocks.shape[0] // 2
    halved = lax.dynamic_slice(
        blocks, (core * owners_half, 0, at + span), (owners_half, shard, gate_blk.shape[1])
    )
    gate_w = as_rows(halved[:, :, : 3 * head], 2 * head)
    open_w, shut_w = paired(gate_w[:, :head]), paired(gate_w[:, head:])
    prm = halved[:, :8, 3 * head : 3 * head + tall].transpose(1, 0, 2).reshape(8, -1).astype(F32)
    rate = prm[7]
    prm = jnp.concatenate([prm[:7], -8.0 * jax.nn.softplus(rate)[None]], axis=0)
    gains_at = at + span + 3 * head + tall
    gains = blocks[:, :2, gains_at : gains_at + shard].astype(F32)
    pre_gain, mid_gain = gains[:, 0].reshape(-1), gains[:, 1].reshape(-1)
    rec_w = half_cols(0, width)
    side_w = half_cols(2 * width, width)
    gating_w, upward_w, down_w = run_pick(weights, core, hidden_width, 4 * width, model, parts, shard)

    def over_chips(rows):
        return lax.all_to_all(jnp.broadcast_to(rows[None], (chips, *rows.shape)), ("y", "z"), 0, 0, tiled=True)

    tokens = x_low.astype(F32)
    pre_scale = rms_scale(tokens)
    normed = (tokens * pre_scale * pre_gain).astype(BF16)
    before = x_before.astype(F32)
    normed_before = (before * rms_scale(before) * pre_gain).astype(BF16)
    branch_ext = dot(jnp.concatenate([normed_before, normed], axis=0), rec_w, 1, 0)
    conv_prev = jnp.pad(half(conv_state[0], core, 1), ((8 - taps + 1, 2 * rows), (0, 0)))
    is_before = lax.broadcasted_iota(jnp.int32, branch_ext.shape, 0) < 8
    branch_ext = jnp.where(is_before & (chip == 0), conv_prev, branch_ext)
    side_pre = dot(normed, side_w, 1, 0)
    side_act, side_back = jax.vjp(jax.nn.gelu, side_pre)
    opened, forget, local, product = run_gates(branch_ext, open_w, shut_w, prm)
    out_w = as_rows(
        lax.dynamic_slice(blocks, (core * owners_half, 0, at), (owners_half, shard, span)), model
    )
    ends, out_w = tied(over_chips(jnp.concatenate([product[-1:], local[-1:]], axis=0)), out_w)
    products, lasts = ends[:, 0], ends[:, 1]
    state = half(init_state[0], core, 0)
    start = state
    for i in range(chips):
        start = jnp.where(chip == i, state, start)
        state = products[i] * state + lasts[i]
    states = local + product * start
    mixed_rec = (states * side_act).astype(BF16)
    branch_part = dot(mixed_rec, out_w, 1, 0)
    resid = tokens + (branch_part + swap_cores(branch_part))

    nx = lax.axis_size("x")
    mid_scale = rms_scale(resid)
    mid_low = (resid * mid_scale * mid_gain).astype(BF16)
    gate_pre = dot(mid_low, gating_w, 1, 0)
    up_pre = dot(mid_low, upward_w, 1, 0)
    gate_act, gelu_back = jax.vjp(jax.nn.gelu, gate_pre)
    hidden = (gate_act * up_pre).astype(BF16)
    grad_hidden = dot(grad_low, down_w, 1, 1)
    grad_gate = gelu_back(grad_hidden * up_pre)[0].astype(BF16)
    grad_up = (grad_hidden * gate_act).astype(BF16)
    mid_part = dot(grad_gate, gating_w, 1, 1) + dot(grad_up, upward_w, 1, 1)
    mid_part, grad_gate, grad_up, hidden = tied(mid_part, grad_gate, grad_up, hidden)
    grad_down = dot(hidden, grad_low, 0, 0).astype(BF16)
    grad_down = lax.psum_scatter(grad_down, "y", scatter_dimension=0, tiled=True)
    grad_gating = dot(mid_low, grad_gate, 0, 0).astype(BF16)
    grad_gating = lax.psum_scatter(grad_gating, "y", scatter_dimension=0, tiled=True)
    upward_parts = scatter_send(split_cols(dot(mid_low, grad_up, 0, 0), shard), "x", 3)
    grad_mid = mid_part + swap_cores(mid_part.astype(BF16)).astype(F32)
    scaled = mid_gain * grad_mid
    grad_resid = (
        grad_low.astype(F32)
        + mid_scale * scaled
        - resid * mid_scale**3 * jnp.mean(scaled * resid, axis=-1, keepdims=True)
    )

    grad_branch = grad_resid.astype(BF16)
    grad_mixed = dot(grad_branch, out_w, 1, 1)
    grad_states = grad_mixed * side_act
    grad_side = side_back(grad_mixed * states)[0].astype(BF16)
    back_local, back_product, back_first = run_reverse(grad_states, forget, prm)
    grad_out = dot(mixed_rec, grad_branch, 0, 0).astype(BF16)
    grad_sidebranch = dot(normed, grad_side, 0, 0).astype(BF16)
    firsts = over_chips(jnp.concatenate([back_first[:1], branch_ext[-taps + 1 :]], axis=0))
    firsts, tails = firsts[:, 0], firsts[-1, 1:]
    carry = jnp.zeros((width,), F32)
    coming = carry
    for i in reversed(range(chips)):
        coming = jnp.where(chip == i, carry, coming)
        carry = firsts[i] + products[i] * carry
    grad_ext, grad_head, grad_open, grad_shut, sums = run_gates_back(
        branch_ext, open_w, shut_w, prm,
        jnp.concatenate([start[None], coming[None], jnp.zeros((6, width), F32)], axis=0),
        opened, forget, states, back_local, back_product,
    )
    from_next = lax.ppermute(grad_head, ("y", "z"), back)
    grad_x = jnp.concatenate([grad_ext[:-8], grad_ext[-8:] + from_next], axis=0).astype(BF16)

    def flat(grad):
        return grad.astype(BF16).reshape(*grad.shape[:2], shard, -1)

    def both_halves(grad, place):
        kept = jnp.where(first, lax.index_in_dim(grad, 0, place, False), lax.index_in_dim(grad, 1, place, False))
        sent = jnp.where(first, lax.index_in_dim(grad, 1, place, False), lax.index_in_dim(grad, 0, place, False))
        return in_order(kept, swap_cores(sent), axis=-1)

    sums = jnp.concatenate([sums[:7], sums[7:] * (-8.0 * jax.nn.sigmoid(rate))[None]], axis=0)
    gate_grads = jnp.concatenate(
        [unpaired(grad_open), unpaired(grad_shut), jnp.pad(sums.T, ((0, 0), (0, 120)))], axis=1
    )
    row_grads = jnp.concatenate([grad_out, gate_grads.astype(BF16)], axis=1).reshape(ny, nz, nx * tall, -1)
    rec_parts = scatter_send(split_cols(dot(normed, grad_x, 0, 0), shard), "y", 0)
    side_parts = scatter_send(split_cols(grad_sidebranch, shard), "x", 3)
    row_parts = scatter_send(row_grads, "z", 1)
    pre_part = dot(grad_x, rec_w, 1, 1) + dot(grad_side, side_w, 1, 1)
    rec_parts, side_parts, row_parts, upward_parts = tied(rec_parts, side_parts, row_parts, upward_parts)

    square = 2 * nx * shard
    downs = grad_down.reshape(nz, -1, model)
    rest = downs[:, square:]
    over_z = jnp.concatenate(
        [
            grad_gating.reshape(nz, square, hidden_width),
            add_up(rec_parts).astype(BF16).reshape(nz, square, width),
            downs[:, :square],
            jnp.concatenate([rest[..., : model // 2], rest[..., model // 2 :]], axis=1),
        ],
        axis=2,
    )
    over_z = scatter_send(over_z, "z", 0)
    late = jnp.concatenate([add_up(upward_parts).astype(BF16), add_up(side_parts).astype(BF16)], axis=4)
    late = scatter_send(late, "y", 0)
    row_parts = scatter_send(add_up(row_parts).reshape(ny, nx, tall, -1), "x", 1)
    swapped = swap_cores(half(pre_part, 1 - core, 0).astype(BF16))
    over_z, late, row_parts, swapped = tied(over_z, late, row_parts, swapped)

    over_z = add_up(over_z).astype(BF16)
    cut = hidden_width + width
    wide = over_z[:, :cut].reshape(2, nx, shard, cut)
    rest = over_z[:, cut + model :]
    rest = jnp.concatenate([rest[: square // 2], rest[square // 2 :]], axis=1)
    downs = jnp.concatenate([over_z[:, cut : cut + model], rest], axis=0).reshape(nx, parts * shard, model)
    over_x = jnp.concatenate(
        [wide[0], wide[1]] + [downs[:, i * shard : (i + 1) * shard] for i in range(parts)], axis=2
    )
    over_x = scatter_send(over_x, "x", 0)
    late = scatter_send(add_up(late), "z", 0)
    row_parts = scatter_send(add_up(row_parts), "y", 0)
    over_x, late, row_parts = tied(over_x, late, row_parts)
    over_x, late, row_sum = add_up(over_x), add_up(late), add_up(row_parts)
    pair = [jnp.concatenate([over_x[:, i * cut : (i + 1) * cut], late[i]], axis=1) for i in (0, 1)]
    cut *= 2
    kept, sent = jnp.where(first, pair[0], pair[1]), jnp.where(first, pair[1], pair[0])
    down = jnp.concatenate([over_x[:, cut + i * model : cut + (i + 1) * model] for i in range(parts)], axis=0)
    rows_out = jnp.concatenate([row_sum, down.reshape(tall, -1)], axis=1)
    came, rows_out = tied(swap_cores(sent), to_owner(rows_out))

    def whole(at, size):
        return in_order(kept[:, at : at + size], came[:, at : at + size], axis=1)

    grad_gating = whole(0, hidden_width)
    grad_recurrent = whole(hidden_width, width)
    grad_upward = whole(hidden_width + width, hidden_width)
    grad_sidebranch = whole(2 * hidden_width + width, width)
    grad_out, gate_grads, grad_down = jnp.split(rows_out, [model, model + 2 * head + 128], axis=1)
    grad_down = grad_down.reshape(downward.shape)

    grad_pre = half(pre_part, core, 0) + swapped.astype(F32)
    own = block_in[0].astype(F32)
    own_scale = rms_scale(own)
    scaled = pre_gain * grad_pre
    grad_in = half(grad_resid, core, 0) + (
        own_scale * scaled - own * own_scale**3 * jnp.mean(scaled * own, axis=-1, keepdims=True)
    )
    result_part = dot(hidden, down_w, 1, 0)
    result = half(resid + result_part, core, 0) + swap_cores(half(result_part, 1 - core, 0).astype(BF16)).astype(F32)

    def along(left, grad_left, right, grad_right):
        return jnp.sum(left.astype(F32) * grad_left + right.astype(F32) * grad_right, axis=1)

    grad_prenorm = along(recurrent, grad_recurrent, sidebranch, grad_sidebranch) / prenorm.astype(F32)
    grad_midnorm = along(gating, grad_gating, upward, grad_upward) / midnorm.astype(F32)
    small = gate_grads[:, 2 * head : 2 * head + 8].T

    finals = jnp.concatenate([tails, state[None]], axis=0)
    finals = jnp.where(core == lax.axis_index("y") // (ny // 2), finals, swap_cores(finals))
    slot = width // chips
    finals = lax.dynamic_slice_in_dim(finals, ((chip * 2 + core) % chips) * slot, slot, axis=1)

    return (
        result.astype(BF16)[None],
        grad_in.astype(BF16)[None],
        finals[None, : taps - 1],
        finals[None, taps - 1],
        grad_prenorm,
        grad_recurrent,
        grad_sidebranch,
        small[:4],
        small[4],
        gate_grads[:, :head],
        small[5],
        gate_grads[:, head : 2 * head],
        small[6],
        small[7],
        grad_out,
        grad_midnorm,
        grad_gating,
        grad_upward,
        grad_down,
    )


def solution(mesh):
    seq, dp = mesh.shape["seq"], mesh.shape["dp"]
    side = next(s for s in range(1, seq + 1) if 2 * s * s >= seq)
    fine = Mesh(mesh.devices.reshape(side, side, 2, dp), ("y", "z", "c", "x"))
    part = ("y", "z", "c")
    every = ("y", "z", "c", "x")
    vector, matrix = P(every), P(every, None)
    placed = (
        P("x", part, None),
        P("x", None, None),
        P("x", None),
        P("x", part, None),
        vector,
        matrix,
        matrix,
        P(None, every),
        vector,
        matrix,
        vector,
        matrix,
        vector,
        vector,
        matrix,
        vector,
        matrix,
        matrix,
        matrix,
    )
    return jax.shard_map(
        on_device,
        mesh=fine,
        in_specs=placed,
        out_specs=(P("x", part, None), P("x", part, None), P("x", None, part), P("x", part)) + placed[4:],
        check_vma=False,
    )
```

```python
import functools

import jax
import jax.numpy as jnp
from jax import lax
from jax.experimental import pallas as pl
from jax.experimental.pallas import tpu as pltpu
from jax.sharding import Mesh
from jax.sharding import PartitionSpec as P

EPSILON = 1e-06
F32 = jnp.float32
BF16 = jnp.bfloat16
RANK = {"y": 0, "z": 1, "c": 2, "x": 3}
SWAP = [(0, 1), (1, 0)]
VMEM = 20 * 1024 * 1024


def dot(left, right, left_dim, right_dim):
    return lax.dot_general(
        left, right, (((left_dim,), (right_dim,)), ((), ())), preferred_element_type=F32
    )


def rms_scale(values):
    return lax.rsqrt(jnp.mean(values * values, axis=-1, keepdims=True) + EPSILON)


def fetch(block, axis, by):
    count = lax.axis_size(axis)
    return lax.ppermute(block, axis, [(i, (i - by) % count) for i in range(count)])


def swap_cores(block):
    return lax.ppermute(block, "c", SWAP)


def place_of(held, axis):
    return sum(RANK[h] < RANK[axis] for h in held)


def gather_round(jobs, *others):
    pieces = [[fetch(block, axis, by) for by in range(1, lax.axis_size(axis))] for block, axis, _ in jobs]
    pieces, others = lax.optimization_barrier((pieces, others))
    results = []
    for (block, axis, place), held in zip(jobs, pieces):
        count, me = lax.axis_size(axis), lax.axis_index(axis)
        shape = block.shape[:place] + (count,) + block.shape[place:]
        out = jnp.broadcast_to(jnp.expand_dims(block, place), shape)
        for by, piece in enumerate(held, 1):
            out = lax.dynamic_update_index_in_dim(out, piece, (me + by) % count, place)
        results.append(out)
    return results, others


def slices_of(array, axis, place):
    array = array.astype(BF16)
    count, me = lax.axis_size(axis), lax.axis_index(axis)
    return [lax.dynamic_index_in_dim(array, (me + by) % count, place, keepdims=False) for by in range(count)]


def send_slices(slices, axis):
    return slices[:1] + [fetch(piece, axis, -by) for by, piece in enumerate(slices) if by]


def scatter_send(array, axis, place):
    return send_slices(slices_of(array, axis, place), axis)


def add_up(pieces):
    total = pieces[0].astype(F32)
    for piece in pieces[1:]:
        total = total + piece.astype(F32)
    return total


def tied(*values):
    return lax.optimization_barrier(values)


def split_cols(grad, rows):
    sizes = [lax.axis_size(a) for a in ("y", "z", "c", "x")]
    return grad.astype(BF16).reshape(*sizes, rows, grad.shape[-1])


def split_rows(grad, rows):
    sizes = [lax.axis_size(a) for a in ("y", "z", "x")]
    return grad.astype(BF16).reshape(*sizes, rows, grad.shape[-1])


def owners(inverse):
    ny, nz = lax.axis_size("y"), lax.axis_size("z")
    pairs = []
    for y in range(ny):
        for z in range(nz):
            for c in (0, 1):
                block = ((y % (ny // 2)) * nz + z) * 2 + c
                pairs.append(((y * nz + z) * 2 + c, block * 2 + y // (ny // 2)))
    return [(b, a) for a, b in pairs] if inverse else pairs


def to_half(block):
    return lax.ppermute(block, ("y", "z", "c"), owners(False))


def to_owner(block):
    return lax.ppermute(block, ("y", "z", "c"), owners(True))


def one_less_square(log_decay, decay):
    twice = 2.0 * log_decay
    series = 1.0 + twice * (1.0 / 7.0)
    for order in (6.0, 5.0, 4.0, 3.0, 2.0):
        series = 1.0 + twice * (1.0 / order) * series
    return jnp.where(twice > -0.25, -twice * series, 1.0 - decay * decay)


def split_dot(values, weight):
    high = values.astype(BF16)
    rest = (values - high.astype(F32)).astype(BF16)
    return dot(high, weight, 1, 0) + dot(rest, weight, 1, 0)


def convolved(ext, prm, chunk):
    mixed = prm[4:5] + prm[0:1] * ext[8 : 8 + chunk]
    for tap in range(1, 4):
        mixed = mixed + prm[tap : tap + 1] * ext[8 - tap : 8 - tap + chunk]
    return mixed


def gates_kernel(
    ext_ref, open_ref, forget_ref, prm_ref,
    opened_out, forget_out, local_out, product_out,
    decay_s, drive_s, carry_s,
):
    step = pl.program_id(1)
    chunk, width = opened_out.shape

    @pl.when(step == 0)
    def _():
        carry_s[0:1, :] = jnp.zeros((1, width), F32)
        carry_s[1:2, :] = jnp.ones((1, width), F32)

    start = pl.multiple_of(step * chunk, chunk)
    ext = ext_ref[pl.ds(start, chunk + 8), :]
    prm = prm_ref[...]
    mixed = convolved(ext, prm, chunk)
    opened = jax.nn.sigmoid(split_dot(mixed, open_ref[...]) + prm[5:6])
    forget = jax.nn.sigmoid(split_dot(mixed, forget_ref[...]) + prm[6:7])
    log_decay = forget * prm[7:8]
    decay = jnp.exp(log_decay)
    opened_out[...] = opened
    forget_out[...] = forget
    decay_s[...] = decay
    drive_s[...] = jnp.sqrt(one_less_square(log_decay, decay)) * opened * mixed
    rows = lax.broadcasted_iota(jnp.int32, (8, width), 0)

    def group(index, carry):
        state, product = carry
        at = pl.ds(pl.multiple_of(index * 8, 8), 8)
        a, b = decay_s[at, :], drive_s[at, :]
        for by in (1, 2, 4):
            inside = rows >= by
            b = jnp.where(inside, a * pltpu.roll(b, by, 0) + b, b)
            a = jnp.where(inside, a * pltpu.roll(a, by, 0), a)
        local = b + a * state
        total = a * product
        local_out[at, :] = local
        product_out[at, :] = total
        return local[7:8], total[7:8]

    state, product = lax.fori_loop(0, chunk // 8, group, (carry_s[0:1, :], carry_s[1:2, :]), unroll=4)
    carry_s[0:1, :] = state
    carry_s[1:2, :] = product


def reverse_kernel(grad_ref, forget_ref, prm_ref, local_out, product_out, first_out, decay_s, carry_s):
    step = pl.program_id(1)
    chunk, width = local_out.shape

    @pl.when(step == 0)
    def _():
        carry_s[0:1, :] = jnp.zeros((1, width), F32)
        carry_s[1:2, :] = jnp.ones((1, width), F32)
        carry_s[2:3, :] = jnp.ones((1, width), F32)

    decay = jnp.exp(forget_ref[...] * prm_ref[7:8, :])
    last = carry_s[2:3, :]
    decay_s[0:chunk, :] = decay
    carry_s[2:3, :] = decay[0:1]
    rows = lax.broadcasted_iota(jnp.int32, (8, width), 0)
    following = jnp.where(
        lax.broadcasted_iota(jnp.int32, (chunk, width), 0) == chunk - 1, last, pltpu.roll(decay, chunk - 1, 0)
    )
    decay_s[...] = following

    def group(index, carry):
        state, product = carry
        at = pl.ds(pl.multiple_of(chunk - 8 - index * 8, 8), 8)
        a, b = decay_s[at, :], grad_ref[at, :]
        for by in (1, 2, 4):
            inside = rows < 8 - by
            b = jnp.where(inside, a * pltpu.roll(b, 8 - by, 0) + b, b)
            a = jnp.where(inside, a * pltpu.roll(a, 8 - by, 0), a)
        local = b + a * state
        total = a * product
        local_out[at, :] = local
        product_out[at, :] = total
        return local[0:1], total[0:1]

    state, product = lax.fori_loop(0, chunk // 8, group, (carry_s[0:1, :], carry_s[1:2, :]), unroll=4)
    carry_s[0:1, :] = state
    carry_s[1:2, :] = product
    first_out[...] = jnp.broadcast_to(decay[0:1] * state, (8, width))


def gates_back_kernel(
    ext_ref, open_ref, shut_ref, prm_ref, ends_ref,
    opened_ref, forget_ref, states_ref, local_ref, product_ref,
    grad_out, head_out, grad_open, grad_shut, sums_out,
    next_s,
):
    step = pl.program_id(1)
    steps = pl.num_programs(1)
    chunk, width = opened_ref.shape

    @pl.when(step == 0)
    def _():
        next_s[...] = jnp.zeros_like(next_s)
        grad_open[...] = jnp.zeros_like(grad_open)
        grad_shut[...] = jnp.zeros_like(grad_shut)
        sums_out[...] = jnp.zeros_like(sums_out)

    place = steps - 1 - step
    start = pl.multiple_of(place * chunk, chunk)
    prm = prm_ref[...]
    opened, forget = opened_ref[...], forget_ref[...]
    ext = ext_ref[pl.ds(start, chunk + 8), :]
    mixed = convolved(ext, prm, chunk)
    log_decay = forget * prm[7:8]
    decay = jnp.exp(log_decay)
    square = one_less_square(log_decay, decay)
    inverse = lax.rsqrt(square)
    scaled = square * inverse
    grad_drive = local_ref[...] + product_ref[...] * ends_ref[1:2, :]
    states = states_ref[pl.ds(start, chunk), :]
    before = states_ref[pl.ds(pl.multiple_of(jnp.maximum(start - 8, 0), 8), 8), :]
    before = jnp.where(place == 0, ends_ref[0:1, :], before[7:8])
    prior = jnp.where(
        lax.broadcasted_iota(jnp.int32, (chunk, width), 0) == 0, before, pltpu.roll(states, 1, 0)
    )
    grad_scaled = grad_drive * opened * mixed
    grad_log = decay * (grad_drive * prior - grad_scaled * decay * inverse)
    grad_opened = scaled * grad_scaled * (1.0 - opened)
    grad_forget = grad_log * prm[7:8] * forget * (1.0 - forget)
    low_mixed = mixed.astype(BF16)
    low_opened = grad_opened.astype(BF16)
    low_forget = grad_forget.astype(BF16)
    grad_open[...] += dot(low_mixed, low_opened, 0, 0)
    grad_shut[...] += dot(low_mixed, low_forget, 0, 0)
    grad_mixed = (
        grad_drive * scaled * opened
        + dot(low_opened, open_ref[...], 1, 1)
        + dot(low_forget, shut_ref[...], 1, 1)
    )
    spread = jnp.concatenate([grad_mixed, next_s[...]], axis=0)
    grad = prm[0:1] * grad_mixed
    for tap in range(1, 4):
        grad = grad + prm[tap : tap + 1] * spread[tap : tap + chunk]
    grad_out[...] = grad
    first = grad_mixed[0:8]
    next_s[...] = first
    lead = jnp.concatenate([jnp.zeros((8, width), F32), first], axis=0)
    head = jnp.zeros((8, width), F32)
    for tap in range(1, 4):
        head = head + prm[tap : tap + 1] * lead[tap : tap + 8]
    head_out[...] = head
    total = lambda v: jnp.sum(v, axis=0, keepdims=True)
    sums_out[...] += jnp.concatenate(
        [total(grad_mixed * ext[8 - tap : 8 - tap + chunk]) for tap in range(4)]
        + [total(grad_mixed), total(grad_opened), total(grad_forget), total(grad_log * forget)],
        axis=0,
    )


PAIR = 384
CHUNK = 256


def params_of(steps):
    return pltpu.CompilerParams(vmem_limit_bytes=VMEM, dimension_semantics=("arbitrary",) * steps)


def cost(microseconds):
    return pl.CostEstimate(flops=int(microseconds * 1e9), bytes_accessed=0, transcendentals=0)


def in_hbm(array):
    return pltpu.with_memory_space_constraint(array, pltpu.HBM)


def run_gates(ext, open_w, forget_w, prm):
    length, channels = ext.shape[0] - 8, ext.shape[1]
    chunk = min(CHUNK, length)
    grid = (channels // PAIR, length // chunk)
    whole = pl.BlockSpec((length + 8, PAIR), lambda j, i: (0, j))
    weight = pl.BlockSpec((None, PAIR, PAIR), lambda j, i: (j, 0, 0))
    row = pl.BlockSpec((8, PAIR), lambda j, i: (0, j))
    part = pl.BlockSpec((chunk, PAIR), lambda j, i: (i, j))
    return pl.pallas_call(
        gates_kernel,
        grid=grid,
        in_specs=[whole, weight, weight, row],
        out_specs=[part] * 4,
        out_shape=[pltpu.HBM((length, channels), F32)] * 4,
        scratch_shapes=[pltpu.VMEM((chunk, PAIR), F32)] * 2 + [pltpu.VMEM((8, PAIR), F32)],
        compiler_params=params_of(2),
        cost_estimate=cost(1),
        name="gates",
    )(ext, open_w, forget_w, prm)


def run_reverse(grad, forget, prm):
    length, channels = grad.shape
    chunk = min(CHUNK, length)
    steps = length // chunk
    row = pl.BlockSpec((8, PAIR), lambda j, i: (0, j))
    part = pl.BlockSpec((chunk, PAIR), lambda j, i: (steps - 1 - i, j))
    full = pltpu.HBM((length, channels), F32)
    return pl.pallas_call(
        reverse_kernel,
        grid=(channels // PAIR, steps),
        in_specs=[part, part, row],
        out_specs=[part, part, row],
        out_shape=[full, full, jax.ShapeDtypeStruct((8, channels), F32)],
        scratch_shapes=[pltpu.VMEM((chunk, PAIR), F32), pltpu.VMEM((8, PAIR), F32)],
        compiler_params=params_of(2),
        cost_estimate=cost(1),
        name="reverse",
    )(grad, in_hbm(forget), prm)


def run_gates_back(ext, open_w, forget_w, prm, ends, opened, forget, states, local, product):
    length, channels = opened.shape
    chunk = min(CHUNK, length)
    steps = length // chunk
    pairs = channels // PAIR
    whole = pl.BlockSpec((length + 8, PAIR), lambda j, i: (0, j))
    held = pl.BlockSpec((length, PAIR), lambda j, i: (0, j))
    weight = pl.BlockSpec((None, PAIR, PAIR), lambda j, i: (j, 0, 0))
    row = pl.BlockSpec((8, PAIR), lambda j, i: (0, j))
    part = pl.BlockSpec((chunk, PAIR), lambda j, i: (steps - 1 - i, j))
    return pl.pallas_call(
        gates_back_kernel,
        grid=(pairs, steps),
        in_specs=[whole, weight, weight, row, row, part, part, held, part, part],
        out_specs=[part, row, weight, weight, row],
        out_shape=[
            jax.ShapeDtypeStruct((length, channels), F32),
            jax.ShapeDtypeStruct((8, channels), F32),
            jax.ShapeDtypeStruct((pairs, PAIR, PAIR), F32),
            jax.ShapeDtypeStruct((pairs, PAIR, PAIR), F32),
            jax.ShapeDtypeStruct((8, channels), F32),
        ],
        scratch_shapes=[pltpu.VMEM((8, PAIR), F32)],
        compiler_params=params_of(2),
        cost_estimate=cost(1),
        name="gates_back",
    )(ext, open_w, forget_w, prm, ends, *[in_hbm(v) for v in (opened, forget, states, local, product)])


def pick_kernel(core_ref, gating_ref, upward_ref, *refs, shard):
    downs, (gating_out, upward_out, down_out) = refs[:-3], refs[-3:]
    gating_out[...] = gating_ref[...]
    upward_out[...] = upward_ref[...]
    downs = [ref[...].astype(F32) for ref in downs]
    rows = downs[0].shape[0]
    down_out[...] = jnp.concatenate(
        [block[at : at + shard] for at in range(0, rows, shard) for block in downs], axis=0
    ).astype(down_out.dtype)


def run_pick(weights, core, width, at, model, parts, shard):
    rows = weights.shape[0]
    steps = 8 if rows // 16 >= shard and rows % 128 == 0 else 1
    block, short = rows // steps, rows // 2 // steps
    left = at // width
    first = (at + 4 * width) // model
    cols = lambda which: pl.BlockSpec((block, width), lambda i, core: (i, left + 2 * which + core[0]))
    part = lambda which: pl.BlockSpec((short, model), lambda i, core: (core[0] * steps + i, first + which))
    out = pl.BlockSpec((block, width), lambda i, core: (i, 0))
    return pl.pallas_call(
        functools.partial(pick_kernel, shard=shard),
        grid_spec=pltpu.PrefetchScalarGridSpec(
            num_scalar_prefetch=1,
            grid=(steps,),
            in_specs=[cols(0), cols(1)] + [part(i) for i in range(parts)],
            out_specs=[out, out, pl.BlockSpec((short * parts, model), lambda i, core: (i, 0))],
        ),
        out_shape=[jax.ShapeDtypeStruct((rows, width), BF16)] * 2
        + [jax.ShapeDtypeStruct((rows // 2 * parts, model), BF16)],
        compiler_params=params_of(1),
        cost_estimate=cost(6),
        name="pick",
    )(core.reshape(1), *[weights] * (2 + parts))


def paired(blocks):
    head = blocks.shape[1]
    split = blocks.reshape(-1, 2, head, head)
    none = jnp.zeros_like(split[:, 0])
    above = jnp.concatenate([split[:, 0], none], axis=2)
    below = jnp.concatenate([none, split[:, 1]], axis=2)
    return jnp.concatenate([above, below], axis=1)


def unpaired(pairs):
    head = pairs.shape[1] // 2
    blocks = jnp.stack([pairs[:, :head, :head], pairs[:, head:, head:]], axis=1)
    return blocks.reshape(-1, head)


def on_device(
    block_in,
    conv_state,
    init_state,
    cotangent,
    prenorm,
    recurrent,
    sidebranch,
    convolve,
    convbias,
    inputgate,
    inputbias,
    decaygate,
    decaybias,
    decayrate,
    outproject,
    midnorm,
    gating,
    upward,
    downward,
):
    core = lax.axis_index("c")
    first = core == 0
    ny, nz = lax.axis_size("y"), lax.axis_size("z")
    chips = ny * nz
    chip = lax.axis_index("y") * nz + lax.axis_index("z")
    rows = block_in.shape[1]
    width = recurrent.shape[1] // 2
    hidden_width = gating.shape[1] // 2
    head = inputgate.shape[1]
    model = block_in.shape[2]
    taps = convolve.shape[0]

    def in_order(own, other, axis=0):
        return jnp.concatenate([jnp.where(first, own, other), jnp.where(first, other, own)], axis=axis)

    def half(array, which, axis):
        size = array.shape[axis] // 2
        low = lax.slice_in_dim(array, 0, size, axis=axis)
        high = lax.slice_in_dim(array, size, 2 * size, axis=axis)
        return jnp.where(which == 0, low, high)

    shard = recurrent.shape[0]
    tall = inputgate.shape[0]
    short = tall - shard

    def as_blocks(rows):
        cols = rows.shape[1] // 2
        return jnp.concatenate([rows[:shard], jnp.concatenate([rows[shard:, :cols], rows[shard:, cols:]], axis=0)], axis=1)

    def as_rows(blocks, cols):
        rest = blocks[:, :, cols:]
        rest = jnp.concatenate([rest[:, :short], rest[:, short : 2 * short]], axis=2)
        return jnp.concatenate([blocks[:, :, :cols], rest], axis=1).reshape(-1, cols)

    vectors = jnp.concatenate([convolve, convbias[None], inputbias[None], decaybias[None], decayrate[None]], axis=0)
    gains = jnp.pad(jnp.concatenate([prenorm[None], midnorm[None]], axis=0), ((0, shard - 2), (0, 0)))
    vectors = jnp.concatenate([jnp.pad(vectors, ((0, shard - 8), (0, 0))), gains], axis=1)
    gate_blk = as_blocks(jnp.concatenate([inputgate, decaygate], axis=1))
    spare = -(gate_blk.shape[1] + vectors.shape[1]) % 128
    gate_blk = jnp.concatenate([gate_blk, vectors, jnp.zeros((shard, spare), BF16)], axis=1)
    everyone = ("y", "z", "c", "x")
    parts = downward.shape[0] // shard
    downs = [downward[i * shard : (i + 1) * shard] for i in range(parts)]
    weights = lax.all_gather(
        jnp.concatenate([recurrent, sidebranch, gating, upward] + downs + [as_blocks(outproject), gate_blk], axis=1),
        everyone,
        axis=0,
        tiled=True,
    )

    x_other, grad_other = tied(swap_cores(block_in[0]), swap_cores(cotangent[0]))
    x_low = in_order(block_in[0], x_other)
    grad_low = in_order(cotangent[0], grad_other)
    onward = [(i, i + 1) for i in range(chips - 1)]
    back = [(i + 1, i) for i in range(chips - 1)]
    x_before = lax.ppermute(x_low[-8:], ("y", "z"), onward)
    weights, x_low, grad_low, x_before = tied(weights, x_low, grad_low, x_before)

    def half_cols(at, size):
        return lax.dynamic_slice_in_dim(weights, at + core * size, size, axis=1)

    at = 4 * (width + hidden_width) + parts * model
    span = model + model // 2
    blocks = weights.reshape(-1, shard, weights.shape[1])
    owners_half = blocks.shape[0] // 2
    halved = lax.dynamic_slice(
        blocks, (core * owners_half, 0, at + span), (owners_half, shard, gate_blk.shape[1])
    )
    gate_w = as_rows(halved[:, :, : 3 * head], 2 * head)
    open_w, shut_w = paired(gate_w[:, :head]), paired(gate_w[:, head:])
    prm = halved[:, :8, 3 * head : 3 * head + tall].transpose(1, 0, 2).reshape(8, -1).astype(F32)
    rate = prm[7]
    prm = jnp.concatenate([prm[:7], -8.0 * jax.nn.softplus(rate)[None]], axis=0)
    gains_at = at + span + 3 * head + tall
    gains = blocks[:, :2, gains_at : gains_at + shard].astype(F32)
    pre_gain, mid_gain = gains[:, 0].reshape(-1), gains[:, 1].reshape(-1)
    rec_w = half_cols(0, width)
    side_w = half_cols(2 * width, width)
    gating_w, upward_w, down_w = run_pick(weights, core, hidden_width, 4 * width, model, parts, shard)

    def over_chips(rows):
        return lax.all_to_all(jnp.broadcast_to(rows[None], (chips, *rows.shape)), ("y", "z"), 0, 0, tiled=True)

    tokens = x_low.astype(F32)
    pre_scale = rms_scale(tokens)
    normed = (tokens * pre_scale * pre_gain).astype(BF16)
    before = x_before.astype(F32)
    normed_before = (before * rms_scale(before) * pre_gain).astype(BF16)
    branch_ext = dot(jnp.concatenate([normed_before, normed], axis=0), rec_w, 1, 0)
    conv_prev = jnp.pad(half(conv_state[0], core, 1), ((8 - taps + 1, 2 * rows), (0, 0)))
    is_before = lax.broadcasted_iota(jnp.int32, branch_ext.shape, 0) < 8
    branch_ext = jnp.where(is_before & (chip == 0), conv_prev, branch_ext)
    side_pre = dot(normed, side_w, 1, 0)
    side_act, side_back = jax.vjp(jax.nn.gelu, side_pre)
    opened, forget, local, product = run_gates(branch_ext, open_w, shut_w, prm)
    out_w = as_rows(
        lax.dynamic_slice(blocks, (core * owners_half, 0, at), (owners_half, shard, span)), model
    )
    ends, out_w = tied(over_chips(jnp.concatenate([product[-1:], local[-1:]], axis=0)), out_w)
    products, lasts = ends[:, 0], ends[:, 1]
    state = half(init_state[0], core, 0)
    start = state
    for i in range(chips):
        start = jnp.where(chip == i, state, start)
        state = products[i] * state + lasts[i]
    states = local + product * start
    mixed_rec = (states * side_act).astype(BF16)
    branch_part = dot(mixed_rec, out_w, 1, 0)
    resid = tokens + (branch_part + swap_cores(branch_part))

    nx = lax.axis_size("x")
    mid_scale = rms_scale(resid)
    mid_low = (resid * mid_scale * mid_gain).astype(BF16)
    gate_pre = dot(mid_low, gating_w, 1, 0)
    up_pre = dot(mid_low, upward_w, 1, 0)
    gate_act, gelu_back = jax.vjp(jax.nn.gelu, gate_pre)
    hidden = (gate_act * up_pre).astype(BF16)
    grad_hidden = dot(grad_low, down_w, 1, 1)
    grad_gate = gelu_back(grad_hidden * up_pre)[0].astype(BF16)
    grad_up = (grad_hidden * gate_act).astype(BF16)
    mid_part = dot(grad_gate, gating_w, 1, 1) + dot(grad_up, upward_w, 1, 1)
    sent, grad_gate, grad_up, hidden = tied(mid_part.astype(BF16), grad_gate, grad_up, hidden)
    grad_down = dot(hidden, grad_low, 0, 0).astype(BF16)
    grad_down = lax.psum_scatter(grad_down, "y", scatter_dimension=0, tiled=True)
    grad_gating = dot(mid_low, grad_gate, 0, 0).astype(BF16)
    grad_gating = lax.psum_scatter(grad_gating, "y", scatter_dimension=0, tiled=True)
    upward_parts = scatter_send(split_cols(dot(mid_low, grad_up, 0, 0), shard), "x", 3)
    grad_mid = mid_part + swap_cores(sent).astype(F32)
    scaled = mid_gain * grad_mid
    grad_resid = (
        grad_low.astype(F32)
        + mid_scale * scaled
        - resid * mid_scale**3 * jnp.mean(scaled * resid, axis=-1, keepdims=True)
    )

    grad_branch = grad_resid.astype(BF16)
    grad_mixed = dot(grad_branch, out_w, 1, 1)
    grad_states = grad_mixed * side_act
    grad_side = side_back(grad_mixed * states)[0].astype(BF16)
    back_local, back_product, back_first = run_reverse(grad_states, forget, prm)
    grad_out = dot(mixed_rec, grad_branch, 0, 0).astype(BF16)
    grad_sidebranch = dot(normed, grad_side, 0, 0).astype(BF16)
    firsts, upward_parts = tied(
        over_chips(jnp.concatenate([back_first[:1], branch_ext[-taps + 1 :]], axis=0)), upward_parts
    )
    out_parts = scatter_send(grad_out.reshape(ny, nz, nx * tall, model), "z", 1)
    side_parts = scatter_send(split_cols(grad_sidebranch, shard), "x", 3)
    firsts, tails = firsts[:, 0], firsts[-1, 1:]
    carry = jnp.zeros((width,), F32)
    coming = carry
    for i in reversed(range(chips)):
        coming = jnp.where(chip == i, carry, coming)
        carry = firsts[i] + products[i] * carry
    grad_ext, grad_head, grad_open, grad_shut, sums = run_gates_back(
        branch_ext, open_w, shut_w, prm,
        jnp.concatenate([start[None], coming[None], jnp.zeros((6, width), F32)], axis=0),
        opened, forget, states, back_local, back_product,
    )
    from_next, out_parts, side_parts = tied(
        lax.ppermute(grad_head, ("y", "z"), back), out_parts, side_parts
    )
    grad_x = jnp.concatenate([grad_ext[:-8], grad_ext[-8:] + from_next], axis=0).astype(BF16)

    def flat(grad):
        return grad.astype(BF16).reshape(*grad.shape[:2], shard, -1)

    def both_halves(grad, place):
        kept = jnp.where(first, lax.index_in_dim(grad, 0, place, False), lax.index_in_dim(grad, 1, place, False))
        sent = jnp.where(first, lax.index_in_dim(grad, 1, place, False), lax.index_in_dim(grad, 0, place, False))
        return in_order(kept, swap_cores(sent), axis=-1)

    sums = jnp.concatenate([sums[:7], sums[7:] * (-8.0 * jax.nn.sigmoid(rate))[None]], axis=0)
    gate_grads = jnp.concatenate(
        [unpaired(grad_open), unpaired(grad_shut), jnp.pad(sums.T, ((0, 0), (0, 120)))], axis=1
    )
    row_grads = gate_grads.astype(BF16).reshape(ny, nz, nx * tall, -1)
    rec_parts = scatter_send(split_cols(dot(normed, grad_x, 0, 0), shard), "y", 0)
    row_parts = scatter_send(row_grads, "z", 1)
    pre_part = dot(grad_x, rec_w, 1, 1) + dot(grad_side, side_w, 1, 1)
    square = 2 * nx * shard
    downs = grad_down.reshape(nz, -1, model)
    rest = downs[:, square:]
    over_z = jnp.concatenate(
        [
            grad_gating.reshape(nz, square, hidden_width),
            downs[:, :square],
            jnp.concatenate([rest[..., : model // 2], rest[..., model // 2 :]], axis=1),
        ],
        axis=2,
    )
    late = jnp.concatenate([add_up(upward_parts).astype(BF16), add_up(side_parts).astype(BF16)], axis=4)
    out_sum = add_up(out_parts).astype(BF16)
    rec_parts, row_parts, late, out_sum, over_z = tied(
        rec_parts, row_parts, slices_of(late, "y", 0), out_sum, slices_of(over_z, "z", 0)
    )

    over_z = send_slices(over_z, "z")
    rec_parts = scatter_send(add_up(rec_parts), "z", 0)
    late = send_slices(late, "y")
    row_sum = jnp.concatenate([out_sum, add_up(row_parts).astype(BF16)], axis=2)
    row_parts = scatter_send(row_sum.reshape(ny, nx, tall, -1), "x", 1)
    swapped = swap_cores(half(pre_part, 1 - core, 0).astype(BF16))
    over_z, rec_parts, late, row_parts, swapped = tied(over_z, rec_parts, late, row_parts, swapped)

    mlp_sum = add_up(over_z).astype(BF16)
    cut = hidden_width
    gating_sum = mlp_sum[:, :cut].reshape(2, nx, shard, cut)
    rec_sum = add_up(rec_parts).astype(BF16)
    rest = mlp_sum[:, cut + model :]
    rest = jnp.concatenate([rest[: square // 2], rest[square // 2 :]], axis=1)
    downs = jnp.concatenate([mlp_sum[:, cut : cut + model], rest], axis=0).reshape(nx, parts * shard, model)
    over_x = jnp.concatenate(
        [gating_sum[0], rec_sum[0], gating_sum[1], rec_sum[1]]
        + [downs[:, i * shard : (i + 1) * shard] for i in range(parts)],
        axis=2,
    )
    cut = hidden_width + width
    over_x = scatter_send(over_x, "x", 0)
    late = scatter_send(add_up(late), "z", 0)
    row_parts = scatter_send(add_up(row_parts), "y", 0)
    over_x, late, row_parts = tied(over_x, late, row_parts)
    over_x, late, row_sum = add_up(over_x), add_up(late), add_up(row_parts)
    pair = [jnp.concatenate([over_x[:, i * cut : (i + 1) * cut], late[i]], axis=1) for i in (0, 1)]
    cut *= 2
    kept, sent = jnp.where(first, pair[0], pair[1]), jnp.where(first, pair[1], pair[0])
    down = jnp.concatenate([over_x[:, cut + i * model : cut + (i + 1) * model] for i in range(parts)], axis=0)
    rows_out = jnp.concatenate([row_sum, down.reshape(tall, -1)], axis=1)
    came, rows_out = tied(swap_cores(sent), to_owner(rows_out))

    def whole(at, size):
        return in_order(kept[:, at : at + size], came[:, at : at + size], axis=1)

    grad_gating = whole(0, hidden_width)
    grad_recurrent = whole(hidden_width, width)
    grad_upward = whole(hidden_width + width, hidden_width)
    grad_sidebranch = whole(2 * hidden_width + width, width)
    grad_out, gate_grads, grad_down = jnp.split(rows_out, [model, model + 2 * head + 128], axis=1)
    grad_down = grad_down.reshape(downward.shape)

    grad_pre = half(pre_part, core, 0) + swapped.astype(F32)
    own = block_in[0].astype(F32)
    own_scale = rms_scale(own)
    scaled = pre_gain * grad_pre
    grad_in = half(grad_resid, core, 0) + (
        own_scale * scaled - own * own_scale**3 * jnp.mean(scaled * own, axis=-1, keepdims=True)
    )
    result_part = dot(hidden, down_w, 1, 0)
    result = half(resid + result_part, core, 0) + swap_cores(half(result_part, 1 - core, 0).astype(BF16)).astype(F32)

    def along(left, grad_left, right, grad_right):
        return jnp.sum(left.astype(F32) * grad_left + right.astype(F32) * grad_right, axis=1)

    grad_prenorm = along(recurrent, grad_recurrent, sidebranch, grad_sidebranch) / prenorm.astype(F32)
    grad_midnorm = along(gating, grad_gating, upward, grad_upward) / midnorm.astype(F32)
    small = gate_grads[:, 2 * head : 2 * head + 8].T

    finals = jnp.concatenate([tails, state[None]], axis=0)
    finals = jnp.where(core == lax.axis_index("y") // (ny // 2), finals, swap_cores(finals))
    slot = width // chips
    finals = lax.dynamic_slice_in_dim(finals, ((chip * 2 + core) % chips) * slot, slot, axis=1)

    return (
        result.astype(BF16)[None],
        grad_in.astype(BF16)[None],
        finals[None, : taps - 1],
        finals[None, taps - 1],
        grad_prenorm,
        grad_recurrent,
        grad_sidebranch,
        small[:4],
        small[4],
        gate_grads[:, :head],
        small[5],
        gate_grads[:, head : 2 * head],
        small[6],
        small[7],
        grad_out,
        grad_midnorm,
        grad_gating,
        grad_upward,
        grad_down,
    )


def solution(mesh):
    seq, dp = mesh.shape["seq"], mesh.shape["dp"]
    side = next(s for s in range(1, seq + 1) if 2 * s * s >= seq)
    fine = Mesh(mesh.devices.reshape(side, side, 2, dp), ("y", "z", "c", "x"))
    part = ("y", "z", "c")
    every = ("y", "z", "c", "x")
    vector, matrix = P(every), P(every, None)
    placed = (
        P("x", part, None),
        P("x", None, None),
        P("x", None),
        P("x", part, None),
        vector,
        matrix,
        matrix,
        P(None, every),
        vector,
        matrix,
        vector,
        matrix,
        vector,
        vector,
        matrix,
        vector,
        matrix,
        matrix,
        matrix,
    )
    return jax.shard_map(
        on_device,
        mesh=fine,
        in_specs=placed,
        out_specs=(P("x", part, None), P("x", part, None), P("x", None, part), P("x", part)) + placed[4:],
        check_vma=False,
    )
```

```python
import functools

import jax
import jax.numpy as jnp
from jax import lax
from jax.experimental import pallas as pl
from jax.experimental.pallas import tpu as pltpu
from jax.sharding import Mesh
from jax.sharding import PartitionSpec as P

EPSILON = 1e-06
F32 = jnp.float32
BF16 = jnp.bfloat16
RANK = {"y": 0, "z": 1, "c": 2, "x": 3}
SWAP = [(0, 1), (1, 0)]
VMEM = 20 * 1024 * 1024


def dot(left, right, left_dim, right_dim):
    return lax.dot_general(
        left, right, (((left_dim,), (right_dim,)), ((), ())), preferred_element_type=F32
    )


def rms_scale(values):
    return lax.rsqrt(jnp.mean(values * values, axis=-1, keepdims=True) + EPSILON)


def fetch(block, axis, by):
    count = lax.axis_size(axis)
    return lax.ppermute(block, axis, [(i, (i - by) % count) for i in range(count)])


def swap_cores(block):
    return lax.ppermute(block, "c", SWAP)


def place_of(held, axis):
    return sum(RANK[h] < RANK[axis] for h in held)


def gather_round(jobs, *others):
    pieces = [[fetch(block, axis, by) for by in range(1, lax.axis_size(axis))] for block, axis, _ in jobs]
    pieces, others = lax.optimization_barrier((pieces, others))
    results = []
    for (block, axis, place), held in zip(jobs, pieces):
        count, me = lax.axis_size(axis), lax.axis_index(axis)
        shape = block.shape[:place] + (count,) + block.shape[place:]
        out = jnp.broadcast_to(jnp.expand_dims(block, place), shape)
        for by, piece in enumerate(held, 1):
            out = lax.dynamic_update_index_in_dim(out, piece, (me + by) % count, place)
        results.append(out)
    return results, others


def slices_of(array, axis, place):
    array = array.astype(BF16)
    count, me = lax.axis_size(axis), lax.axis_index(axis)
    return [lax.dynamic_index_in_dim(array, (me + by) % count, place, keepdims=False) for by in range(count)]


def send_slices(slices, axis):
    return slices[:1] + [fetch(piece, axis, -by) for by, piece in enumerate(slices) if by]


def scatter_send(array, axis, place):
    return send_slices(slices_of(array, axis, place), axis)


def add_up(pieces):
    total = pieces[0].astype(F32)
    for piece in pieces[1:]:
        total = total + piece.astype(F32)
    return total


def tied(*values):
    return lax.optimization_barrier(values)


def split_cols(grad, rows):
    sizes = [lax.axis_size(a) for a in ("y", "z", "c", "x")]
    return grad.astype(BF16).reshape(*sizes, rows, grad.shape[-1])


def split_rows(grad, rows):
    sizes = [lax.axis_size(a) for a in ("y", "z", "x")]
    return grad.astype(BF16).reshape(*sizes, rows, grad.shape[-1])


def owners(inverse):
    ny, nz = lax.axis_size("y"), lax.axis_size("z")
    pairs = []
    for y in range(ny):
        for z in range(nz):
            for c in (0, 1):
                block = ((y % (ny // 2)) * nz + z) * 2 + c
                pairs.append(((y * nz + z) * 2 + c, block * 2 + y // (ny // 2)))
    return [(b, a) for a, b in pairs] if inverse else pairs


def to_half(block):
    return lax.ppermute(block, ("y", "z", "c"), owners(False))


def to_owner(block):
    return lax.ppermute(block, ("y", "z", "c"), owners(True))


def one_less_square(log_decay, decay):
    twice = 2.0 * log_decay
    series = 1.0 + twice * (1.0 / 7.0)
    for order in (6.0, 5.0, 4.0, 3.0, 2.0):
        series = 1.0 + twice * (1.0 / order) * series
    return jnp.where(twice > -0.25, -twice * series, 1.0 - decay * decay)


def split_dot(values, weight):
    high = values.astype(BF16)
    rest = (values - high.astype(F32)).astype(BF16)
    return dot(high, weight, 1, 0) + dot(rest, weight, 1, 0)


def convolved(ext, prm, chunk):
    mixed = prm[4:5] + prm[0:1] * ext[8 : 8 + chunk]
    for tap in range(1, 4):
        mixed = mixed + prm[tap : tap + 1] * ext[8 - tap : 8 - tap + chunk]
    return mixed


def gates_kernel(
    ext_ref, open_ref, forget_ref, prm_ref,
    opened_out, forget_out, local_out, product_out,
    decay_s, drive_s, carry_s,
):
    step = pl.program_id(1)
    chunk, width = opened_out.shape

    @pl.when(step == 0)
    def _():
        carry_s[0:1, :] = jnp.zeros((1, width), F32)
        carry_s[1:2, :] = jnp.ones((1, width), F32)

    start = pl.multiple_of(step * chunk, chunk)
    ext = ext_ref[pl.ds(start, chunk + 8), :]
    prm = prm_ref[...]
    mixed = convolved(ext, prm, chunk)
    opened = jax.nn.sigmoid(split_dot(mixed, open_ref[...]) + prm[5:6])
    forget = jax.nn.sigmoid(split_dot(mixed, forget_ref[...]) + prm[6:7])
    log_decay = forget * prm[7:8]
    decay = jnp.exp(log_decay)
    opened_out[...] = opened
    forget_out[...] = forget
    decay_s[...] = decay
    drive_s[...] = jnp.sqrt(one_less_square(log_decay, decay)) * opened * mixed
    rows = lax.broadcasted_iota(jnp.int32, (8, width), 0)

    def group(index, carry):
        state, product = carry
        at = pl.ds(pl.multiple_of(index * 8, 8), 8)
        a, b = decay_s[at, :], drive_s[at, :]
        for by in (1, 2, 4):
            inside = rows >= by
            b = jnp.where(inside, a * pltpu.roll(b, by, 0) + b, b)
            a = jnp.where(inside, a * pltpu.roll(a, by, 0), a)
        local = b + a * state
        total = a * product
        local_out[at, :] = local
        product_out[at, :] = total
        return local[7:8], total[7:8]

    state, product = lax.fori_loop(0, chunk // 8, group, (carry_s[0:1, :], carry_s[1:2, :]), unroll=4)
    carry_s[0:1, :] = state
    carry_s[1:2, :] = product


def reverse_kernel(grad_ref, forget_ref, prm_ref, local_out, product_out, first_out, decay_s, carry_s):
    step = pl.program_id(1)
    chunk, width = local_out.shape

    @pl.when(step == 0)
    def _():
        carry_s[0:1, :] = jnp.zeros((1, width), F32)
        carry_s[1:2, :] = jnp.ones((1, width), F32)
        carry_s[2:3, :] = jnp.ones((1, width), F32)

    decay = jnp.exp(forget_ref[...] * prm_ref[7:8, :])
    last = carry_s[2:3, :]
    decay_s[0:chunk, :] = decay
    carry_s[2:3, :] = decay[0:1]
    rows = lax.broadcasted_iota(jnp.int32, (8, width), 0)
    following = jnp.where(
        lax.broadcasted_iota(jnp.int32, (chunk, width), 0) == chunk - 1, last, pltpu.roll(decay, chunk - 1, 0)
    )
    decay_s[...] = following

    def group(index, carry):
        state, product = carry
        at = pl.ds(pl.multiple_of(chunk - 8 - index * 8, 8), 8)
        a, b = decay_s[at, :], grad_ref[at, :]
        for by in (1, 2, 4):
            inside = rows < 8 - by
            b = jnp.where(inside, a * pltpu.roll(b, 8 - by, 0) + b, b)
            a = jnp.where(inside, a * pltpu.roll(a, 8 - by, 0), a)
        local = b + a * state
        total = a * product
        local_out[at, :] = local
        product_out[at, :] = total
        return local[0:1], total[0:1]

    state, product = lax.fori_loop(0, chunk // 8, group, (carry_s[0:1, :], carry_s[1:2, :]), unroll=4)
    carry_s[0:1, :] = state
    carry_s[1:2, :] = product
    first_out[...] = jnp.broadcast_to(decay[0:1] * state, (8, width))


def gates_back_kernel(
    ext_ref, open_ref, shut_ref, prm_ref, ends_ref,
    opened_ref, forget_ref, states_ref, local_ref, product_ref,
    grad_out, head_out, grad_open, grad_shut, sums_out,
    next_s,
):
    step = pl.program_id(1)
    steps = pl.num_programs(1)
    chunk, width = opened_ref.shape

    @pl.when(step == 0)
    def _():
        next_s[...] = jnp.zeros_like(next_s)
        grad_open[...] = jnp.zeros_like(grad_open)
        grad_shut[...] = jnp.zeros_like(grad_shut)
        sums_out[...] = jnp.zeros_like(sums_out)

    place = steps - 1 - step
    start = pl.multiple_of(place * chunk, chunk)
    prm = prm_ref[...]
    opened, forget = opened_ref[...], forget_ref[...]
    ext = ext_ref[pl.ds(start, chunk + 8), :]
    mixed = convolved(ext, prm, chunk)
    log_decay = forget * prm[7:8]
    decay = jnp.exp(log_decay)
    square = one_less_square(log_decay, decay)
    inverse = lax.rsqrt(square)
    scaled = square * inverse
    grad_drive = local_ref[...] + product_ref[...] * ends_ref[1:2, :]
    states = states_ref[pl.ds(start, chunk), :]
    before = states_ref[pl.ds(pl.multiple_of(jnp.maximum(start - 8, 0), 8), 8), :]
    before = jnp.where(place == 0, ends_ref[0:1, :], before[7:8])
    prior = jnp.where(
        lax.broadcasted_iota(jnp.int32, (chunk, width), 0) == 0, before, pltpu.roll(states, 1, 0)
    )
    grad_scaled = grad_drive * opened * mixed
    grad_log = decay * (grad_drive * prior - grad_scaled * decay * inverse)
    grad_opened = scaled * grad_scaled * (1.0 - opened)
    grad_forget = grad_log * prm[7:8] * forget * (1.0 - forget)
    low_mixed = mixed.astype(BF16)
    low_opened = grad_opened.astype(BF16)
    low_forget = grad_forget.astype(BF16)
    grad_open[...] += dot(low_mixed, low_opened, 0, 0)
    grad_shut[...] += dot(low_mixed, low_forget, 0, 0)
    grad_mixed = (
        grad_drive * scaled * opened
        + dot(low_opened, open_ref[...], 1, 1)
        + dot(low_forget, shut_ref[...], 1, 1)
    )
    spread = jnp.concatenate([grad_mixed, next_s[...]], axis=0)
    grad = prm[0:1] * grad_mixed
    for tap in range(1, 4):
        grad = grad + prm[tap : tap + 1] * spread[tap : tap + chunk]
    grad_out[...] = grad
    first = grad_mixed[0:8]
    next_s[...] = first
    lead = jnp.concatenate([jnp.zeros((8, width), F32), first], axis=0)
    head = jnp.zeros((8, width), F32)
    for tap in range(1, 4):
        head = head + prm[tap : tap + 1] * lead[tap : tap + 8]
    head_out[...] = head
    total = lambda v: jnp.sum(v, axis=0, keepdims=True)
    sums_out[...] += jnp.concatenate(
        [total(grad_mixed * ext[8 - tap : 8 - tap + chunk]) for tap in range(4)]
        + [total(grad_mixed), total(grad_opened), total(grad_forget), total(grad_log * forget)],
        axis=0,
    )


PAIR = 384
CHUNK = 256


def params_of(steps):
    return pltpu.CompilerParams(vmem_limit_bytes=VMEM, dimension_semantics=("arbitrary",) * steps)


def cost(microseconds):
    return pl.CostEstimate(flops=int(microseconds * 1e9), bytes_accessed=0, transcendentals=0)


def in_hbm(array):
    return pltpu.with_memory_space_constraint(array, pltpu.HBM)


def run_gates(ext, open_w, forget_w, prm):
    length, channels = ext.shape[0] - 8, ext.shape[1]
    chunk = min(CHUNK, length)
    grid = (channels // PAIR, length // chunk)
    whole = pl.BlockSpec((length + 8, PAIR), lambda j, i: (0, j))
    weight = pl.BlockSpec((None, PAIR, PAIR), lambda j, i: (j, 0, 0))
    row = pl.BlockSpec((8, PAIR), lambda j, i: (0, j))
    part = pl.BlockSpec((chunk, PAIR), lambda j, i: (i, j))
    return pl.pallas_call(
        gates_kernel,
        grid=grid,
        in_specs=[whole, weight, weight, row],
        out_specs=[part] * 4,
        out_shape=[pltpu.HBM((length, channels), F32)] * 4,
        scratch_shapes=[pltpu.VMEM((chunk, PAIR), F32)] * 2 + [pltpu.VMEM((8, PAIR), F32)],
        compiler_params=params_of(2),
        cost_estimate=cost(1),
        name="gates",
    )(ext, open_w, forget_w, prm)


def run_reverse(grad, forget, prm):
    length, channels = grad.shape
    chunk = min(CHUNK, length)
    steps = length // chunk
    row = pl.BlockSpec((8, PAIR), lambda j, i: (0, j))
    part = pl.BlockSpec((chunk, PAIR), lambda j, i: (steps - 1 - i, j))
    full = pltpu.HBM((length, channels), F32)
    return pl.pallas_call(
        reverse_kernel,
        grid=(channels // PAIR, steps),
        in_specs=[part, part, row],
        out_specs=[part, part, row],
        out_shape=[full, full, jax.ShapeDtypeStruct((8, channels), F32)],
        scratch_shapes=[pltpu.VMEM((chunk, PAIR), F32), pltpu.VMEM((8, PAIR), F32)],
        compiler_params=params_of(2),
        cost_estimate=cost(1),
        name="reverse",
    )(grad, in_hbm(forget), prm)


def run_gates_back(ext, open_w, forget_w, prm, ends, opened, forget, states, local, product):
    length, channels = opened.shape
    chunk = min(CHUNK, length)
    steps = length // chunk
    pairs = channels // PAIR
    whole = pl.BlockSpec((length + 8, PAIR), lambda j, i: (0, j))
    held = pl.BlockSpec((length, PAIR), lambda j, i: (0, j))
    weight = pl.BlockSpec((None, PAIR, PAIR), lambda j, i: (j, 0, 0))
    row = pl.BlockSpec((8, PAIR), lambda j, i: (0, j))
    part = pl.BlockSpec((chunk, PAIR), lambda j, i: (steps - 1 - i, j))
    return pl.pallas_call(
        gates_back_kernel,
        grid=(pairs, steps),
        in_specs=[whole, weight, weight, row, row, part, part, held, part, part],
        out_specs=[part, row, weight, weight, row],
        out_shape=[
            jax.ShapeDtypeStruct((length, channels), F32),
            jax.ShapeDtypeStruct((8, channels), F32),
            jax.ShapeDtypeStruct((pairs, PAIR, PAIR), F32),
            jax.ShapeDtypeStruct((pairs, PAIR, PAIR), F32),
            jax.ShapeDtypeStruct((8, channels), F32),
        ],
        scratch_shapes=[pltpu.VMEM((8, PAIR), F32)],
        compiler_params=params_of(2),
        cost_estimate=cost(1),
        name="gates_back",
    )(ext, open_w, forget_w, prm, ends, *[in_hbm(v) for v in (opened, forget, states, local, product)])


def pick_kernel(core_ref, gating_ref, upward_ref, *refs, shard):
    downs, (gating_out, upward_out, down_out) = refs[:-3], refs[-3:]
    gating_out[...] = gating_ref[...]
    upward_out[...] = upward_ref[...]
    downs = [ref[...].astype(F32) for ref in downs]
    rows = downs[0].shape[0]
    down_out[...] = jnp.concatenate(
        [block[at : at + shard] for at in range(0, rows, shard) for block in downs], axis=0
    ).astype(down_out.dtype)


def run_pick(weights, core, width, at, model, parts, shard):
    rows = weights.shape[0]
    steps = 8 if rows // 16 >= shard and rows % 128 == 0 else 1
    block, short = rows // steps, rows // 2 // steps
    left = at // width
    first = (at + 4 * width) // model
    cols = lambda which: pl.BlockSpec((block, width), lambda i, core: (i, left + 2 * which + core[0]))
    part = lambda which: pl.BlockSpec((short, model), lambda i, core: (core[0] * steps + i, first + which))
    out = pl.BlockSpec((block, width), lambda i, core: (i, 0))
    return pl.pallas_call(
        functools.partial(pick_kernel, shard=shard),
        grid_spec=pltpu.PrefetchScalarGridSpec(
            num_scalar_prefetch=1,
            grid=(steps,),
            in_specs=[cols(0), cols(1)] + [part(i) for i in range(parts)],
            out_specs=[out, out, pl.BlockSpec((short * parts, model), lambda i, core: (i, 0))],
        ),
        out_shape=[jax.ShapeDtypeStruct((rows, width), BF16)] * 2
        + [jax.ShapeDtypeStruct((rows // 2 * parts, model), BF16)],
        compiler_params=params_of(1),
        cost_estimate=cost(6),
        name="pick",
    )(core.reshape(1), *[weights] * (2 + parts))


def paired(blocks):
    head = blocks.shape[1]
    split = blocks.reshape(-1, 2, head, head)
    none = jnp.zeros_like(split[:, 0])
    above = jnp.concatenate([split[:, 0], none], axis=2)
    below = jnp.concatenate([none, split[:, 1]], axis=2)
    return jnp.concatenate([above, below], axis=1)


def unpaired(pairs):
    head = pairs.shape[1] // 2
    blocks = jnp.stack([pairs[:, :head, :head], pairs[:, head:, head:]], axis=1)
    return blocks.reshape(-1, head)


def on_device(
    block_in,
    conv_state,
    init_state,
    cotangent,
    prenorm,
    recurrent,
    sidebranch,
    convolve,
    convbias,
    inputgate,
    inputbias,
    decaygate,
    decaybias,
    decayrate,
    outproject,
    midnorm,
    gating,
    upward,
    downward,
):
    core = lax.axis_index("c")
    first = core == 0
    ny, nz = lax.axis_size("y"), lax.axis_size("z")
    chips = ny * nz
    chip = lax.axis_index("y") * nz + lax.axis_index("z")
    rows = block_in.shape[1]
    width = recurrent.shape[1] // 2
    hidden_width = gating.shape[1] // 2
    head = inputgate.shape[1]
    model = block_in.shape[2]
    taps = convolve.shape[0]

    def in_order(own, other, axis=0):
        return jnp.concatenate([jnp.where(first, own, other), jnp.where(first, other, own)], axis=axis)

    def half(array, which, axis):
        size = array.shape[axis] // 2
        low = lax.slice_in_dim(array, 0, size, axis=axis)
        high = lax.slice_in_dim(array, size, 2 * size, axis=axis)
        return jnp.where(which == 0, low, high)

    shard = recurrent.shape[0]
    tall = inputgate.shape[0]
    short = tall - shard

    def as_blocks(rows):
        cols = rows.shape[1] // 2
        return jnp.concatenate([rows[:shard], jnp.concatenate([rows[shard:, :cols], rows[shard:, cols:]], axis=0)], axis=1)

    def as_rows(blocks, cols):
        rest = blocks[:, :, cols:]
        rest = jnp.concatenate([rest[:, :short], rest[:, short : 2 * short]], axis=2)
        return jnp.concatenate([blocks[:, :, :cols], rest], axis=1).reshape(-1, cols)

    vectors = jnp.concatenate([convolve, convbias[None], inputbias[None], decaybias[None], decayrate[None]], axis=0)
    gains = jnp.pad(jnp.concatenate([prenorm[None], midnorm[None]], axis=0), ((0, shard - 2), (0, 0)))
    vectors = jnp.concatenate([jnp.pad(vectors, ((0, shard - 8), (0, 0))), gains], axis=1)
    gate_blk = as_blocks(jnp.concatenate([inputgate, decaygate], axis=1))
    spare = -(gate_blk.shape[1] + vectors.shape[1]) % 128
    gate_blk = jnp.concatenate([gate_blk, vectors, jnp.zeros((shard, spare), BF16)], axis=1)
    everyone = ("y", "z", "c", "x")
    parts = downward.shape[0] // shard
    downs = [downward[i * shard : (i + 1) * shard] for i in range(parts)]
    weights = lax.all_gather(
        jnp.concatenate([recurrent, sidebranch, gating, upward] + downs + [as_blocks(outproject), gate_blk], axis=1),
        everyone,
        axis=0,
        tiled=True,
    )

    x_other, grad_other = tied(swap_cores(block_in[0]), swap_cores(cotangent[0]))
    x_low = in_order(block_in[0], x_other)
    grad_low = in_order(cotangent[0], grad_other)
    onward = [(i, i + 1) for i in range(chips - 1)]
    back = [(i + 1, i) for i in range(chips - 1)]
    x_before = lax.ppermute(x_low[-8:], ("y", "z"), onward)
    weights, x_low, grad_low, x_before = tied(weights, x_low, grad_low, x_before)

    def half_cols(at, size):
        return lax.dynamic_slice_in_dim(weights, at + core * size, size, axis=1)

    at = 4 * (width + hidden_width) + parts * model
    span = model + model // 2
    blocks = weights.reshape(-1, shard, weights.shape[1])
    owners_half = blocks.shape[0] // 2
    halved = lax.dynamic_slice(
        blocks, (core * owners_half, 0, at + span), (owners_half, shard, gate_blk.shape[1])
    )
    gate_w = as_rows(halved[:, :, : 3 * head], 2 * head)
    open_w, shut_w = paired(gate_w[:, :head]), paired(gate_w[:, head:])
    prm = halved[:, :8, 3 * head : 3 * head + tall].transpose(1, 0, 2).reshape(8, -1).astype(F32)
    rate = prm[7]
    prm = jnp.concatenate([prm[:7], -8.0 * jax.nn.softplus(rate)[None]], axis=0)
    gains_at = at + span + 3 * head + tall
    gains = blocks[:, :2, gains_at : gains_at + shard].astype(F32)
    pre_gain, mid_gain = gains[:, 0].reshape(-1), gains[:, 1].reshape(-1)
    rec_w = half_cols(0, width)
    side_w = half_cols(2 * width, width)
    gating_w, upward_w, down_w = run_pick(weights, core, hidden_width, 4 * width, model, parts, shard)

    def over_chips(rows):
        return lax.all_to_all(jnp.broadcast_to(rows[None], (chips, *rows.shape)), ("y", "z"), 0, 0, tiled=True)

    tokens = x_low.astype(F32)
    pre_scale = rms_scale(tokens)
    normed = (tokens * pre_scale * pre_gain).astype(BF16)
    before = x_before.astype(F32)
    normed_before = (before * rms_scale(before) * pre_gain).astype(BF16)
    branch_ext = dot(jnp.concatenate([normed_before, normed], axis=0), rec_w, 1, 0)
    conv_prev = jnp.pad(half(conv_state[0], core, 1), ((8 - taps + 1, 2 * rows), (0, 0)))
    is_before = lax.broadcasted_iota(jnp.int32, branch_ext.shape, 0) < 8
    branch_ext = jnp.where(is_before & (chip == 0), conv_prev, branch_ext)
    side_pre = dot(normed, side_w, 1, 0)
    side_act, side_back = jax.vjp(jax.nn.gelu, side_pre)
    opened, forget, local, product = run_gates(branch_ext, open_w, shut_w, prm)
    out_w = as_rows(
        lax.dynamic_slice(blocks, (core * owners_half, 0, at), (owners_half, shard, span)), model
    )
    ends, out_w = tied(over_chips(jnp.concatenate([product[-1:], local[-1:]], axis=0)), out_w)
    products, lasts = ends[:, 0], ends[:, 1]
    state = half(init_state[0], core, 0)
    start = state
    for i in range(chips):
        start = jnp.where(chip == i, state, start)
        state = products[i] * state + lasts[i]
    states = local + product * start
    mixed_rec = (states * side_act).astype(BF16)
    branch_part = dot(mixed_rec, out_w, 1, 0)
    resid = tokens + (branch_part + swap_cores(branch_part))

    nx = lax.axis_size("x")
    mid_scale = rms_scale(resid)
    mid_low = (resid * mid_scale * mid_gain).astype(BF16)
    gate_pre = dot(mid_low, gating_w, 1, 0)
    up_pre = dot(mid_low, upward_w, 1, 0)
    gate_act, gelu_back = jax.vjp(jax.nn.gelu, gate_pre)
    hidden = (gate_act * up_pre).astype(BF16)
    grad_hidden = dot(grad_low, down_w, 1, 1)
    grad_gate = gelu_back(grad_hidden * up_pre)[0].astype(BF16)
    grad_up = (grad_hidden * gate_act).astype(BF16)
    mid_part = dot(grad_gate, gating_w, 1, 1) + dot(grad_up, upward_w, 1, 1)
    sent, grad_gate, grad_up, hidden = tied(mid_part.astype(BF16), grad_gate, grad_up, hidden)
    grad_down = dot(hidden, grad_low, 0, 0).astype(BF16)
    grad_down = lax.psum_scatter(grad_down, "y", scatter_dimension=0, tiled=True)
    grad_gating = dot(mid_low, grad_gate, 0, 0).astype(BF16)
    grad_gating = lax.psum_scatter(grad_gating, "y", scatter_dimension=0, tiled=True)
    upward_parts = scatter_send(split_cols(dot(mid_low, grad_up, 0, 0), shard), "x", 3)
    grad_mid = mid_part + swap_cores(sent).astype(F32)
    scaled = mid_gain * grad_mid
    grad_resid = (
        grad_low.astype(F32)
        + mid_scale * scaled
        - resid * mid_scale**3 * jnp.mean(scaled * resid, axis=-1, keepdims=True)
    )

    grad_branch = grad_resid.astype(BF16)
    grad_mixed = dot(grad_branch, out_w, 1, 1)
    grad_states = grad_mixed * side_act
    grad_side = side_back(grad_mixed * states)[0].astype(BF16)
    back_local, back_product, back_first = run_reverse(grad_states, forget, prm)
    grad_out = dot(mixed_rec, grad_branch, 0, 0).astype(BF16)
    grad_sidebranch = dot(normed, grad_side, 0, 0).astype(BF16)
    result_part = dot(hidden, down_w, 1, 0)
    firsts, upward_parts, result_other = tied(
        over_chips(jnp.concatenate([back_first[:1], branch_ext[-taps + 1 :]], axis=0)),
        upward_parts,
        swap_cores(half(result_part, 1 - core, 0).astype(BF16)),
    )
    out_parts = scatter_send(grad_out.reshape(ny, nz, nx * tall, model), "z", 1)
    side_parts = scatter_send(split_cols(grad_sidebranch, shard), "x", 3)
    firsts, tails = firsts[:, 0], firsts[-1, 1:]
    carry = jnp.zeros((width,), F32)
    coming = carry
    for i in reversed(range(chips)):
        coming = jnp.where(chip == i, carry, coming)
        carry = firsts[i] + products[i] * carry
    grad_ext, grad_head, grad_open, grad_shut, sums = run_gates_back(
        branch_ext, open_w, shut_w, prm,
        jnp.concatenate([start[None], coming[None], jnp.zeros((6, width), F32)], axis=0),
        opened, forget, states, back_local, back_product,
    )
    finals = jnp.concatenate([tails, state[None]], axis=0)
    from_next, out_parts, side_parts, finals_other = tied(
        lax.ppermute(grad_head, ("y", "z"), back), out_parts, side_parts, swap_cores(finals)
    )
    grad_x = jnp.concatenate([grad_ext[:-8], grad_ext[-8:] + from_next], axis=0).astype(BF16)

    def flat(grad):
        return grad.astype(BF16).reshape(*grad.shape[:2], shard, -1)

    def both_halves(grad, place):
        kept = jnp.where(first, lax.index_in_dim(grad, 0, place, False), lax.index_in_dim(grad, 1, place, False))
        sent = jnp.where(first, lax.index_in_dim(grad, 1, place, False), lax.index_in_dim(grad, 0, place, False))
        return in_order(kept, swap_cores(sent), axis=-1)

    sums = jnp.concatenate([sums[:7], sums[7:] * (-8.0 * jax.nn.sigmoid(rate))[None]], axis=0)
    gate_grads = jnp.concatenate(
        [unpaired(grad_open), unpaired(grad_shut), jnp.pad(sums.T, ((0, 0), (0, 120)))], axis=1
    )
    row_grads = gate_grads.astype(BF16).reshape(ny, nz, nx * tall, -1)
    rec_parts = scatter_send(split_cols(dot(normed, grad_x, 0, 0), shard), "y", 0)
    row_parts = scatter_send(row_grads, "z", 1)
    pre_part = dot(grad_x, rec_w, 1, 1) + dot(grad_side, side_w, 1, 1)
    square = 2 * nx * shard
    downs = grad_down.reshape(nz, -1, model)
    rest = downs[:, square:]
    over_z = jnp.concatenate(
        [
            grad_gating.reshape(nz, square, hidden_width),
            downs[:, :square],
            jnp.concatenate([rest[..., : model // 2], rest[..., model // 2 :]], axis=1),
        ],
        axis=2,
    )
    late = jnp.concatenate([add_up(upward_parts).astype(BF16), add_up(side_parts).astype(BF16)], axis=4)
    out_sum = add_up(out_parts).astype(BF16)
    rec_parts, row_parts, late, out_sum, over_z = tied(
        rec_parts, row_parts, slices_of(late, "y", 0), out_sum, slices_of(over_z, "z", 0)
    )

    over_z = send_slices(over_z, "z")
    rec_parts = scatter_send(add_up(rec_parts), "z", 0)
    late = send_slices(late, "y")
    row_sum = jnp.concatenate([out_sum, add_up(row_parts).astype(BF16)], axis=2)
    row_parts = scatter_send(row_sum.reshape(ny, nx, tall, -1), "x", 1)
    pre_sent = half(pre_part, 1 - core, 0).astype(BF16)
    over_z, rec_parts, late, row_parts, pre_sent = tied(over_z, rec_parts, late, row_parts, pre_sent)
    swapped = swap_cores(pre_sent)

    mlp_sum = add_up(over_z).astype(BF16)
    cut = hidden_width
    gating_sum = mlp_sum[:, :cut].reshape(2, nx, shard, cut)
    rec_sum = add_up(rec_parts).astype(BF16)
    rest = mlp_sum[:, cut + model :]
    rest = jnp.concatenate([rest[: square // 2], rest[square // 2 :]], axis=1)
    downs = jnp.concatenate([mlp_sum[:, cut : cut + model], rest], axis=0).reshape(nx, parts * shard, model)
    over_x = jnp.concatenate(
        [gating_sum[0], rec_sum[0], gating_sum[1], rec_sum[1]]
        + [downs[:, i * shard : (i + 1) * shard] for i in range(parts)],
        axis=2,
    )
    cut = hidden_width + width
    over_x = scatter_send(over_x, "x", 0)
    late = scatter_send(add_up(late), "z", 0)
    row_parts = scatter_send(add_up(row_parts), "y", 0)
    over_x, late, row_parts, swapped = tied(over_x, late, row_parts, swapped)
    over_x, late, row_sum = add_up(over_x), add_up(late), add_up(row_parts)
    pair = [jnp.concatenate([over_x[:, i * cut : (i + 1) * cut], late[i]], axis=1) for i in (0, 1)]
    cut *= 2
    kept, sent = jnp.where(first, pair[0], pair[1]), jnp.where(first, pair[1], pair[0])
    down = jnp.concatenate([over_x[:, cut + i * model : cut + (i + 1) * model] for i in range(parts)], axis=0)
    rows_out = jnp.concatenate([row_sum, down.reshape(tall, -1)], axis=1)
    came, rows_out = tied(swap_cores(sent), to_owner(rows_out))

    def whole(at, size):
        return in_order(kept[:, at : at + size], came[:, at : at + size], axis=1)

    grad_gating = whole(0, hidden_width)
    grad_recurrent = whole(hidden_width, width)
    grad_upward = whole(hidden_width + width, hidden_width)
    grad_sidebranch = whole(2 * hidden_width + width, width)
    grad_out, gate_grads, grad_down = jnp.split(rows_out, [model, model + 2 * head + 128], axis=1)
    grad_down = grad_down.reshape(downward.shape)

    grad_pre = half(pre_part, core, 0) + swapped.astype(F32)
    own = block_in[0].astype(F32)
    own_scale = rms_scale(own)
    scaled = pre_gain * grad_pre
    grad_in = half(grad_resid, core, 0) + (
        own_scale * scaled - own * own_scale**3 * jnp.mean(scaled * own, axis=-1, keepdims=True)
    )
    result = half(resid + result_part, core, 0) + result_other.astype(F32)

    def along(left, grad_left, right, grad_right):
        return jnp.sum(left.astype(F32) * grad_left + right.astype(F32) * grad_right, axis=1)

    grad_prenorm = along(recurrent, grad_recurrent, sidebranch, grad_sidebranch) / prenorm.astype(F32)
    grad_midnorm = along(gating, grad_gating, upward, grad_upward) / midnorm.astype(F32)
    small = gate_grads[:, 2 * head : 2 * head + 8].T

    finals = jnp.where(core == lax.axis_index("y") // (ny // 2), finals, finals_other)
    slot = width // chips
    finals = lax.dynamic_slice_in_dim(finals, ((chip * 2 + core) % chips) * slot, slot, axis=1)

    return (
        result.astype(BF16)[None],
        grad_in.astype(BF16)[None],
        finals[None, : taps - 1],
        finals[None, taps - 1],
        grad_prenorm,
        grad_recurrent,
        grad_sidebranch,
        small[:4],
        small[4],
        gate_grads[:, :head],
        small[5],
        gate_grads[:, head : 2 * head],
        small[6],
        small[7],
        grad_out,
        grad_midnorm,
        grad_gating,
        grad_upward,
        grad_down,
    )


def solution(mesh):
    seq, dp = mesh.shape["seq"], mesh.shape["dp"]
    side = next(s for s in range(1, seq + 1) if 2 * s * s >= seq)
    fine = Mesh(mesh.devices.reshape(side, side, 2, dp), ("y", "z", "c", "x"))
    part = ("y", "z", "c")
    every = ("y", "z", "c", "x")
    vector, matrix = P(every), P(every, None)
    placed = (
        P("x", part, None),
        P("x", None, None),
        P("x", None),
        P("x", part, None),
        vector,
        matrix,
        matrix,
        P(None, every),
        vector,
        matrix,
        vector,
        matrix,
        vector,
        vector,
        matrix,
        vector,
        matrix,
        matrix,
        matrix,
    )
    return jax.shard_map(
        on_device,
        mesh=fine,
        in_specs=placed,
        out_specs=(P("x", part, None), P("x", part, None), P("x", None, part), P("x", part)) + placed[4:],
        check_vma=False,
    )
```

```python
import functools

import jax
import jax.numpy as jnp
from jax import lax
from jax.experimental import pallas as pl
from jax.experimental.pallas import tpu as pltpu
from jax.sharding import Mesh
from jax.sharding import PartitionSpec as P

EPSILON = 1e-06
F32 = jnp.float32
BF16 = jnp.bfloat16
RANK = {"y": 0, "z": 1, "c": 2, "x": 3}
SWAP = [(0, 1), (1, 0)]
VMEM = 20 * 1024 * 1024


def dot(left, right, left_dim, right_dim):
    return lax.dot_general(
        left, right, (((left_dim,), (right_dim,)), ((), ())), preferred_element_type=F32
    )


def rms_scale(values):
    return lax.rsqrt(jnp.mean(values * values, axis=-1, keepdims=True) + EPSILON)


def fetch(block, axis, by):
    count = lax.axis_size(axis)
    return lax.ppermute(block, axis, [(i, (i - by) % count) for i in range(count)])


def swap_cores(block):
    return lax.ppermute(block, "c", SWAP)


def place_of(held, axis):
    return sum(RANK[h] < RANK[axis] for h in held)


def gather_round(jobs, *others):
    pieces = [[fetch(block, axis, by) for by in range(1, lax.axis_size(axis))] for block, axis, _ in jobs]
    pieces, others = lax.optimization_barrier((pieces, others))
    results = []
    for (block, axis, place), held in zip(jobs, pieces):
        count, me = lax.axis_size(axis), lax.axis_index(axis)
        shape = block.shape[:place] + (count,) + block.shape[place:]
        out = jnp.broadcast_to(jnp.expand_dims(block, place), shape)
        for by, piece in enumerate(held, 1):
            out = lax.dynamic_update_index_in_dim(out, piece, (me + by) % count, place)
        results.append(out)
    return results, others


def slices_of(array, axis, place):
    array = array.astype(BF16)
    count, me = lax.axis_size(axis), lax.axis_index(axis)
    return [lax.dynamic_index_in_dim(array, (me + by) % count, place, keepdims=False) for by in range(count)]


def send_slices(slices, axis):
    return slices[:1] + [fetch(piece, axis, -by) for by, piece in enumerate(slices) if by]


def scatter_send(array, axis, place):
    return send_slices(slices_of(array, axis, place), axis)


def add_up(pieces):
    total = pieces[0].astype(F32)
    for piece in pieces[1:]:
        total = total + piece.astype(F32)
    return total


def tied(*values):
    return lax.optimization_barrier(values)


def split_cols(grad, rows):
    sizes = [lax.axis_size(a) for a in ("y", "z", "c", "x")]
    return grad.astype(BF16).reshape(*sizes, rows, grad.shape[-1])


def split_rows(grad, rows):
    sizes = [lax.axis_size(a) for a in ("y", "z", "x")]
    return grad.astype(BF16).reshape(*sizes, rows, grad.shape[-1])


def owners(inverse):
    ny, nz = lax.axis_size("y"), lax.axis_size("z")
    pairs = []
    for y in range(ny):
        for z in range(nz):
            for c in (0, 1):
                block = ((y % (ny // 2)) * nz + z) * 2 + c
                pairs.append(((y * nz + z) * 2 + c, block * 2 + y // (ny // 2)))
    return [(b, a) for a, b in pairs] if inverse else pairs


def to_half(block):
    return lax.ppermute(block, ("y", "z", "c"), owners(False))


def to_owner(block):
    return lax.ppermute(block, ("y", "z", "c"), owners(True))


def one_less_square(log_decay, decay):
    twice = 2.0 * log_decay
    series = 1.0 + twice * (1.0 / 7.0)
    for order in (6.0, 5.0, 4.0, 3.0, 2.0):
        series = 1.0 + twice * (1.0 / order) * series
    return jnp.where(twice > -0.25, -twice * series, 1.0 - decay * decay)


def split_dot(values, weight):
    high = values.astype(BF16)
    rest = (values - high.astype(F32)).astype(BF16)
    return dot(high, weight, 1, 0) + dot(rest, weight, 1, 0)


def convolved(ext, prm, chunk):
    mixed = prm[4:5] + prm[0:1] * ext[8 : 8 + chunk]
    for tap in range(1, 4):
        mixed = mixed + prm[tap : tap + 1] * ext[8 - tap : 8 - tap + chunk]
    return mixed


def gates_kernel(
    ext_ref, open_ref, forget_ref, prm_ref,
    opened_out, forget_out, local_out, product_out,
    decay_s, drive_s, carry_s,
):
    step = pl.program_id(1)
    chunk, width = opened_out.shape

    @pl.when(step == 0)
    def _():
        carry_s[0:1, :] = jnp.zeros((1, width), F32)
        carry_s[1:2, :] = jnp.ones((1, width), F32)

    start = pl.multiple_of(step * chunk, chunk)
    ext = ext_ref[pl.ds(start, chunk + 8), :]
    prm = prm_ref[...]
    mixed = convolved(ext, prm, chunk)
    opened = jax.nn.sigmoid(split_dot(mixed, open_ref[...]) + prm[5:6])
    forget = jax.nn.sigmoid(split_dot(mixed, forget_ref[...]) + prm[6:7])
    log_decay = forget * prm[7:8]
    decay = jnp.exp(log_decay)
    opened_out[...] = opened
    forget_out[...] = forget
    decay_s[...] = decay
    drive_s[...] = jnp.sqrt(one_less_square(log_decay, decay)) * opened * mixed
    rows = lax.broadcasted_iota(jnp.int32, (8, width), 0)

    def group(index, carry):
        state, product = carry
        at = pl.ds(pl.multiple_of(index * 8, 8), 8)
        a, b = decay_s[at, :], drive_s[at, :]
        for by in (1, 2, 4):
            inside = rows >= by
            b = jnp.where(inside, a * pltpu.roll(b, by, 0) + b, b)
            a = jnp.where(inside, a * pltpu.roll(a, by, 0), a)
        local = b + a * state
        total = a * product
        local_out[at, :] = local
        product_out[at, :] = total
        return local[7:8], total[7:8]

    state, product = lax.fori_loop(0, chunk // 8, group, (carry_s[0:1, :], carry_s[1:2, :]), unroll=4)
    carry_s[0:1, :] = state
    carry_s[1:2, :] = product


def reverse_kernel(grad_ref, forget_ref, prm_ref, local_out, product_out, first_out, decay_s, carry_s):
    step = pl.program_id(1)
    chunk, width = local_out.shape

    @pl.when(step == 0)
    def _():
        carry_s[0:1, :] = jnp.zeros((1, width), F32)
        carry_s[1:2, :] = jnp.ones((1, width), F32)
        carry_s[2:3, :] = jnp.ones((1, width), F32)

    decay = jnp.exp(forget_ref[...] * prm_ref[7:8, :])
    last = carry_s[2:3, :]
    decay_s[0:chunk, :] = decay
    carry_s[2:3, :] = decay[0:1]
    rows = lax.broadcasted_iota(jnp.int32, (8, width), 0)
    following = jnp.where(
        lax.broadcasted_iota(jnp.int32, (chunk, width), 0) == chunk - 1, last, pltpu.roll(decay, chunk - 1, 0)
    )
    decay_s[...] = following

    def group(index, carry):
        state, product = carry
        at = pl.ds(pl.multiple_of(chunk - 8 - index * 8, 8), 8)
        a, b = decay_s[at, :], grad_ref[at, :]
        for by in (1, 2, 4):
            inside = rows < 8 - by
            b = jnp.where(inside, a * pltpu.roll(b, 8 - by, 0) + b, b)
            a = jnp.where(inside, a * pltpu.roll(a, 8 - by, 0), a)
        local = b + a * state
        total = a * product
        local_out[at, :] = local
        product_out[at, :] = total
        return local[0:1], total[0:1]

    state, product = lax.fori_loop(0, chunk // 8, group, (carry_s[0:1, :], carry_s[1:2, :]), unroll=4)
    carry_s[0:1, :] = state
    carry_s[1:2, :] = product
    first_out[...] = jnp.broadcast_to(decay[0:1] * state, (8, width))


def gates_back_kernel(
    ext_ref, open_ref, shut_ref, prm_ref, ends_ref,
    opened_ref, forget_ref, states_ref, local_ref, product_ref,
    grad_out, head_out, grad_open, grad_shut, sums_out,
    next_s,
):
    step = pl.program_id(1)
    steps = pl.num_programs(1)
    chunk, width = opened_ref.shape

    @pl.when(step == 0)
    def _():
        next_s[...] = jnp.zeros_like(next_s)
        grad_open[...] = jnp.zeros_like(grad_open)
        grad_shut[...] = jnp.zeros_like(grad_shut)
        sums_out[...] = jnp.zeros_like(sums_out)

    place = steps - 1 - step
    start = pl.multiple_of(place * chunk, chunk)
    prm = prm_ref[...]
    opened, forget = opened_ref[...], forget_ref[...]
    ext = ext_ref[pl.ds(start, chunk + 8), :]
    mixed = convolved(ext, prm, chunk)
    log_decay = forget * prm[7:8]
    decay = jnp.exp(log_decay)
    square = one_less_square(log_decay, decay)
    inverse = lax.rsqrt(square)
    scaled = square * inverse
    grad_drive = local_ref[...] + product_ref[...] * ends_ref[1:2, :]
    states = states_ref[pl.ds(start, chunk), :]
    before = states_ref[pl.ds(pl.multiple_of(jnp.maximum(start - 8, 0), 8), 8), :]
    before = jnp.where(place == 0, ends_ref[0:1, :], before[7:8])
    prior = jnp.where(
        lax.broadcasted_iota(jnp.int32, (chunk, width), 0) == 0, before, pltpu.roll(states, 1, 0)
    )
    grad_scaled = grad_drive * opened * mixed
    grad_log = decay * (grad_drive * prior - grad_scaled * decay * inverse)
    grad_opened = scaled * grad_scaled * (1.0 - opened)
    grad_forget = grad_log * prm[7:8] * forget * (1.0 - forget)
    low_mixed = mixed.astype(BF16)
    low_opened = grad_opened.astype(BF16)
    low_forget = grad_forget.astype(BF16)
    grad_open[...] += dot(low_mixed, low_opened, 0, 0)
    grad_shut[...] += dot(low_mixed, low_forget, 0, 0)
    grad_mixed = (
        grad_drive * scaled * opened
        + dot(low_opened, open_ref[...], 1, 1)
        + dot(low_forget, shut_ref[...], 1, 1)
    )
    spread = jnp.concatenate([grad_mixed, next_s[...]], axis=0)
    grad = prm[0:1] * grad_mixed
    for tap in range(1, 4):
        grad = grad + prm[tap : tap + 1] * spread[tap : tap + chunk]
    grad_out[...] = grad
    first = grad_mixed[0:8]
    next_s[...] = first
    lead = jnp.concatenate([jnp.zeros((8, width), F32), first], axis=0)
    head = jnp.zeros((8, width), F32)
    for tap in range(1, 4):
        head = head + prm[tap : tap + 1] * lead[tap : tap + 8]
    head_out[...] = head
    total = lambda v: jnp.sum(v, axis=0, keepdims=True)
    sums_out[...] += jnp.concatenate(
        [total(grad_mixed * ext[8 - tap : 8 - tap + chunk]) for tap in range(4)]
        + [total(grad_mixed), total(grad_opened), total(grad_forget), total(grad_log * forget)],
        axis=0,
    )


PAIR = 384
CHUNK = 256


def params_of(steps):
    return pltpu.CompilerParams(vmem_limit_bytes=VMEM, dimension_semantics=("arbitrary",) * steps)


def cost(microseconds):
    return pl.CostEstimate(flops=int(microseconds * 1e9), bytes_accessed=0, transcendentals=0)


def in_hbm(array):
    return pltpu.with_memory_space_constraint(array, pltpu.HBM)


def run_gates(ext, open_w, forget_w, prm):
    length, channels = ext.shape[0] - 8, ext.shape[1]
    chunk = min(CHUNK, length)
    grid = (channels // PAIR, length // chunk)
    whole = pl.BlockSpec((length + 8, PAIR), lambda j, i: (0, j))
    weight = pl.BlockSpec((None, PAIR, PAIR), lambda j, i: (j, 0, 0))
    row = pl.BlockSpec((8, PAIR), lambda j, i: (0, j))
    part = pl.BlockSpec((chunk, PAIR), lambda j, i: (i, j))
    return pl.pallas_call(
        gates_kernel,
        grid=grid,
        in_specs=[whole, weight, weight, row],
        out_specs=[part] * 4,
        out_shape=[pltpu.HBM((length, channels), F32)] * 4,
        scratch_shapes=[pltpu.VMEM((chunk, PAIR), F32)] * 2 + [pltpu.VMEM((8, PAIR), F32)],
        compiler_params=params_of(2),
        cost_estimate=cost(1),
        name="gates",
    )(ext, open_w, forget_w, prm)


def run_reverse(grad, forget, prm):
    length, channels = grad.shape
    chunk = min(CHUNK, length)
    steps = length // chunk
    row = pl.BlockSpec((8, PAIR), lambda j, i: (0, j))
    part = pl.BlockSpec((chunk, PAIR), lambda j, i: (steps - 1 - i, j))
    full = pltpu.HBM((length, channels), F32)
    return pl.pallas_call(
        reverse_kernel,
        grid=(channels // PAIR, steps),
        in_specs=[part, part, row],
        out_specs=[part, part, row],
        out_shape=[full, full, jax.ShapeDtypeStruct((8, channels), F32)],
        scratch_shapes=[pltpu.VMEM((chunk, PAIR), F32), pltpu.VMEM((8, PAIR), F32)],
        compiler_params=params_of(2),
        cost_estimate=cost(1),
        name="reverse",
    )(grad, in_hbm(forget), prm)


def run_gates_back(ext, open_w, forget_w, prm, ends, opened, forget, states, local, product):
    length, channels = opened.shape
    chunk = min(CHUNK, length)
    steps = length // chunk
    pairs = channels // PAIR
    whole = pl.BlockSpec((length + 8, PAIR), lambda j, i: (0, j))
    held = pl.BlockSpec((length, PAIR), lambda j, i: (0, j))
    weight = pl.BlockSpec((None, PAIR, PAIR), lambda j, i: (j, 0, 0))
    row = pl.BlockSpec((8, PAIR), lambda j, i: (0, j))
    part = pl.BlockSpec((chunk, PAIR), lambda j, i: (steps - 1 - i, j))
    return pl.pallas_call(
        gates_back_kernel,
        grid=(pairs, steps),
        in_specs=[whole, weight, weight, row, row, part, part, held, part, part],
        out_specs=[part, row, weight, weight, row],
        out_shape=[
            jax.ShapeDtypeStruct((length, channels), F32),
            jax.ShapeDtypeStruct((8, channels), F32),
            jax.ShapeDtypeStruct((pairs, PAIR, PAIR), F32),
            jax.ShapeDtypeStruct((pairs, PAIR, PAIR), F32),
            jax.ShapeDtypeStruct((8, channels), F32),
        ],
        scratch_shapes=[pltpu.VMEM((8, PAIR), F32)],
        compiler_params=params_of(2),
        cost_estimate=cost(1),
        name="gates_back",
    )(ext, open_w, forget_w, prm, ends, *[in_hbm(v) for v in (opened, forget, states, local, product)])


def pick_kernel(core_ref, gating_ref, upward_ref, *refs, shard):
    downs, (gating_out, upward_out, down_out) = refs[:-3], refs[-3:]
    gating_out[...] = gating_ref[...]
    upward_out[...] = upward_ref[...]
    downs = [ref[...].astype(F32) for ref in downs]
    rows = downs[0].shape[0]
    down_out[...] = jnp.concatenate(
        [block[at : at + shard] for at in range(0, rows, shard) for block in downs], axis=0
    ).astype(down_out.dtype)


def run_pick(weights, core, width, at, model, parts, shard):
    rows = weights.shape[0]
    steps = 8 if rows // 16 >= shard and rows % 128 == 0 else 1
    block, short = rows // steps, rows // 2 // steps
    left = at // width
    first = (at + 4 * width) // model
    cols = lambda which: pl.BlockSpec((block, width), lambda i, core: (i, left + 2 * which + core[0]))
    part = lambda which: pl.BlockSpec((short, model), lambda i, core: (core[0] * steps + i, first + which))
    out = pl.BlockSpec((block, width), lambda i, core: (i, 0))
    return pl.pallas_call(
        functools.partial(pick_kernel, shard=shard),
        grid_spec=pltpu.PrefetchScalarGridSpec(
            num_scalar_prefetch=1,
            grid=(steps,),
            in_specs=[cols(0), cols(1)] + [part(i) for i in range(parts)],
            out_specs=[out, out, pl.BlockSpec((short * parts, model), lambda i, core: (i, 0))],
        ),
        out_shape=[jax.ShapeDtypeStruct((rows, width), BF16)] * 2
        + [jax.ShapeDtypeStruct((rows // 2 * parts, model), BF16)],
        compiler_params=params_of(1),
        cost_estimate=cost(6),
        name="pick",
    )(core.reshape(1), *[weights] * (2 + parts))


def paired(blocks):
    head = blocks.shape[1]
    split = blocks.reshape(-1, 2, head, head)
    none = jnp.zeros_like(split[:, 0])
    above = jnp.concatenate([split[:, 0], none], axis=2)
    below = jnp.concatenate([none, split[:, 1]], axis=2)
    return jnp.concatenate([above, below], axis=1)


def unpaired(pairs):
    head = pairs.shape[1] // 2
    blocks = jnp.stack([pairs[:, :head, :head], pairs[:, head:, head:]], axis=1)
    return blocks.reshape(-1, head)


def on_device(
    block_in,
    conv_state,
    init_state,
    cotangent,
    prenorm,
    recurrent,
    sidebranch,
    convolve,
    convbias,
    inputgate,
    inputbias,
    decaygate,
    decaybias,
    decayrate,
    outproject,
    midnorm,
    gating,
    upward,
    downward,
):
    core = lax.axis_index("c")
    first = core == 0
    ny, nz = lax.axis_size("y"), lax.axis_size("z")
    chips = ny * nz
    chip = lax.axis_index("y") * nz + lax.axis_index("z")
    rows = block_in.shape[1]
    width = recurrent.shape[1] // 2
    hidden_width = gating.shape[1] // 2
    head = inputgate.shape[1]
    model = block_in.shape[2]
    taps = convolve.shape[0]

    def in_order(own, other, axis=0):
        return jnp.concatenate([jnp.where(first, own, other), jnp.where(first, other, own)], axis=axis)

    def half(array, which, axis):
        size = array.shape[axis] // 2
        low = lax.slice_in_dim(array, 0, size, axis=axis)
        high = lax.slice_in_dim(array, size, 2 * size, axis=axis)
        return jnp.where(which == 0, low, high)

    shard = recurrent.shape[0]
    tall = inputgate.shape[0]
    short = tall - shard

    def as_blocks(rows):
        cols = rows.shape[1] // 2
        return jnp.concatenate([rows[:shard], jnp.concatenate([rows[shard:, :cols], rows[shard:, cols:]], axis=0)], axis=1)

    def as_rows(blocks, cols):
        rest = blocks[:, :, cols:]
        rest = jnp.concatenate([rest[:, :short], rest[:, short : 2 * short]], axis=2)
        return jnp.concatenate([blocks[:, :, :cols], rest], axis=1).reshape(-1, cols)

    vectors = jnp.concatenate([convolve, convbias[None], inputbias[None], decaybias[None], decayrate[None]], axis=0)
    gains = jnp.pad(jnp.concatenate([prenorm[None], midnorm[None]], axis=0), ((0, shard - 2), (0, 0)))
    vectors = jnp.concatenate([jnp.pad(vectors, ((0, shard - 8), (0, 0))), gains], axis=1)
    gate_blk = as_blocks(jnp.concatenate([inputgate, decaygate], axis=1))
    spare = -(gate_blk.shape[1] + vectors.shape[1]) % 128
    gate_blk = jnp.concatenate([gate_blk, vectors, jnp.zeros((shard, spare), BF16)], axis=1)
    everyone = ("y", "z", "c", "x")
    parts = downward.shape[0] // shard
    downs = [downward[i * shard : (i + 1) * shard] for i in range(parts)]
    weights = lax.all_gather(
        jnp.concatenate([recurrent, sidebranch, gating, upward] + downs + [as_blocks(outproject), gate_blk], axis=1),
        everyone,
        axis=0,
        tiled=True,
    )

    x_other, grad_other = tied(swap_cores(block_in[0]), swap_cores(cotangent[0]))
    x_low = in_order(block_in[0], x_other)
    grad_low = in_order(cotangent[0], grad_other)
    onward = [(i, i + 1) for i in range(chips - 1)]
    back = [(i + 1, i) for i in range(chips - 1)]
    x_before = lax.ppermute(x_low[-8:], ("y", "z"), onward)
    weights, x_low, grad_low, x_before = tied(weights, x_low, grad_low, x_before)

    def half_cols(at, size):
        return lax.dynamic_slice_in_dim(weights, at + core * size, size, axis=1)

    at = 4 * (width + hidden_width) + parts * model
    span = model + model // 2
    blocks = weights.reshape(-1, shard, weights.shape[1])
    owners_half = blocks.shape[0] // 2
    halved = lax.dynamic_slice(
        blocks, (core * owners_half, 0, at + span), (owners_half, shard, gate_blk.shape[1])
    )
    gate_w = as_rows(halved[:, :, : 3 * head], 2 * head)
    open_w, shut_w = paired(gate_w[:, :head]), paired(gate_w[:, head:])
    prm = halved[:, :8, 3 * head : 3 * head + tall].transpose(1, 0, 2).reshape(8, -1).astype(F32)
    rate = prm[7]
    prm = jnp.concatenate([prm[:7], -8.0 * jax.nn.softplus(rate)[None]], axis=0)
    gains_at = at + span + 3 * head + tall
    gains = blocks[:, :2, gains_at : gains_at + shard].astype(F32)
    pre_gain, mid_gain = gains[:, 0].reshape(-1), gains[:, 1].reshape(-1)
    rec_w = half_cols(0, width)
    side_w = half_cols(2 * width, width)
    gating_w, upward_w, down_w = run_pick(weights, core, hidden_width, 4 * width, model, parts, shard)

    def over_chips(rows):
        return lax.all_to_all(jnp.broadcast_to(rows[None], (chips, *rows.shape)), ("y", "z"), 0, 0, tiled=True)

    tokens = x_low.astype(F32)
    pre_scale = rms_scale(tokens)
    normed = (tokens * pre_scale * pre_gain).astype(BF16)
    before = x_before.astype(F32)
    normed_before = (before * rms_scale(before) * pre_gain).astype(BF16)
    branch_ext = dot(jnp.concatenate([normed_before, normed], axis=0), rec_w, 1, 0)
    conv_prev = jnp.pad(half(conv_state[0], core, 1), ((8 - taps + 1, 2 * rows), (0, 0)))
    is_before = lax.broadcasted_iota(jnp.int32, branch_ext.shape, 0) < 8
    branch_ext = jnp.where(is_before & (chip == 0), conv_prev, branch_ext)
    side_pre = dot(normed, side_w, 1, 0)
    side_act, side_back = jax.vjp(jax.nn.gelu, side_pre)
    opened, forget, local, product = run_gates(branch_ext, open_w, shut_w, prm)
    out_w = as_rows(
        lax.dynamic_slice(blocks, (core * owners_half, 0, at), (owners_half, shard, span)), model
    )
    ends, out_w = tied(over_chips(jnp.concatenate([product[-1:], local[-1:]], axis=0)), out_w)
    products, lasts = ends[:, 0], ends[:, 1]
    state = half(init_state[0], core, 0)
    start = state
    for i in range(chips):
        start = jnp.where(chip == i, state, start)
        state = products[i] * state + lasts[i]
    states = local + product * start
    mixed_rec = (states * side_act).astype(BF16)
    branch_part = dot(mixed_rec, out_w, 1, 0)
    resid = tokens + (branch_part + swap_cores(branch_part))

    nx = lax.axis_size("x")
    mid_scale = rms_scale(resid)
    mid_low = (resid * mid_scale * mid_gain).astype(BF16)
    gate_pre = dot(mid_low, gating_w, 1, 0)
    up_pre = dot(mid_low, upward_w, 1, 0)
    gate_act, gelu_back = jax.vjp(jax.nn.gelu, gate_pre)
    hidden = (gate_act * up_pre).astype(BF16)
    grad_hidden = dot(grad_low, down_w, 1, 1)
    grad_gate = gelu_back(grad_hidden * up_pre)[0].astype(BF16)
    grad_up = (grad_hidden * gate_act).astype(BF16)
    mid_part = dot(grad_gate, gating_w, 1, 1) + dot(grad_up, upward_w, 1, 1)
    sent, grad_gate, grad_up, hidden = tied(mid_part.astype(BF16), grad_gate, grad_up, hidden)
    grad_down = dot(hidden, grad_low, 0, 0).astype(BF16)
    grad_down = lax.psum_scatter(grad_down, "y", scatter_dimension=0, tiled=True)
    grad_gating = dot(mid_low, grad_gate, 0, 0).astype(BF16)
    grad_gating = lax.psum_scatter(grad_gating, "y", scatter_dimension=0, tiled=True)
    upward_parts = scatter_send(split_cols(dot(mid_low, grad_up, 0, 0), shard), "x", 3)
    grad_mid = mid_part + swap_cores(sent).astype(F32)
    scaled = mid_gain * grad_mid
    grad_resid = (
        grad_low.astype(F32)
        + mid_scale * scaled
        - resid * mid_scale**3 * jnp.mean(scaled * resid, axis=-1, keepdims=True)
    )

    grad_branch = grad_resid.astype(BF16)
    grad_mixed = dot(grad_branch, out_w, 1, 1)
    grad_states = grad_mixed * side_act
    grad_side = side_back(grad_mixed * states)[0].astype(BF16)
    back_local, back_product, back_first = run_reverse(grad_states, forget, prm)
    grad_out = dot(mixed_rec, grad_branch, 0, 0).astype(BF16)
    grad_sidebranch = dot(normed, grad_side, 0, 0).astype(BF16)
    result_part = dot(hidden, down_w, 1, 0)
    firsts, upward_parts, result_other = tied(
        over_chips(jnp.concatenate([back_first[:1], branch_ext[-taps + 1 :]], axis=0)),
        upward_parts,
        swap_cores(half(result_part, 1 - core, 0).astype(BF16)),
    )
    out_parts = scatter_send(grad_out.reshape(ny, nz, nx * tall, model), "z", 1)
    side_parts = scatter_send(split_cols(grad_sidebranch, shard), "x", 3)
    firsts, tails = firsts[:, 0], firsts[-1, 1:]
    carry = jnp.zeros((width,), F32)
    coming = carry
    for i in reversed(range(chips)):
        coming = jnp.where(chip == i, carry, coming)
        carry = firsts[i] + products[i] * carry
    grad_ext, grad_head, grad_open, grad_shut, sums = run_gates_back(
        branch_ext, open_w, shut_w, prm,
        jnp.concatenate([start[None], coming[None], jnp.zeros((6, width), F32)], axis=0),
        opened, forget, states, back_local, back_product,
    )
    finals = jnp.concatenate([tails, state[None]], axis=0)
    from_next, out_parts, side_parts, finals_other = tied(
        lax.ppermute(grad_head, ("y", "z"), back), out_parts, side_parts, swap_cores(finals)
    )
    grad_x = jnp.concatenate([grad_ext[:-8], grad_ext[-8:] + from_next], axis=0).astype(BF16)

    def flat(grad):
        return grad.astype(BF16).reshape(*grad.shape[:2], shard, -1)

    def both_halves(grad, place):
        kept = jnp.where(first, lax.index_in_dim(grad, 0, place, False), lax.index_in_dim(grad, 1, place, False))
        sent = jnp.where(first, lax.index_in_dim(grad, 1, place, False), lax.index_in_dim(grad, 0, place, False))
        return in_order(kept, swap_cores(sent), axis=-1)

    sums = jnp.concatenate([sums[:7], sums[7:] * (-8.0 * jax.nn.sigmoid(rate))[None]], axis=0)
    gate_grads = jnp.concatenate(
        [unpaired(grad_open), unpaired(grad_shut), jnp.pad(sums.T, ((0, 0), (0, 120)))], axis=1
    )
    row_grads = gate_grads.astype(BF16).reshape(ny, nz, nx * tall, -1)
    rec_parts = scatter_send(split_cols(dot(normed, grad_x, 0, 0), shard), "y", 0)
    row_cuts = slices_of(row_grads, "z", 1)
    across = list(range(2, nz - 1))
    row_parts = [cut if by == 0 else fetch(cut, "z", -by) for by, cut in enumerate(row_cuts) if by not in across]
    pre_part = dot(grad_x, rec_w, 1, 1) + dot(grad_side, side_w, 1, 1)
    square = 2 * nx * shard
    downs = grad_down.reshape(nz, -1, model)
    rest = downs[:, square:]
    over_z = jnp.concatenate(
        [
            grad_gating.reshape(nz, square, hidden_width),
            downs[:, :square],
            jnp.concatenate([rest[..., : model // 2], rest[..., model // 2 :]], axis=1),
        ],
        axis=2,
    )
    late = jnp.concatenate([add_up(upward_parts).astype(BF16), add_up(side_parts).astype(BF16)], axis=4)
    out_sum = add_up(out_parts).astype(BF16)
    rec_parts, row_parts, row_cuts, late, out_sum, over_z = tied(
        rec_parts, row_parts, [row_cuts[by] for by in across], slices_of(late, "y", 0), out_sum, slices_of(over_z, "z", 0)
    )

    over_z = send_slices(over_z, "z")
    rec_parts = scatter_send(add_up(rec_parts), "z", 0)
    late = send_slices(late, "y")
    row_parts += [fetch(cut, "z", -by) for by, cut in zip(across, row_cuts)]
    row_sum = jnp.concatenate([out_sum, add_up(row_parts).astype(BF16)], axis=2)
    row_parts = scatter_send(row_sum.reshape(ny, nx, tall, -1), "x", 1)
    pre_sent = half(pre_part, 1 - core, 0).astype(BF16)
    over_z, rec_parts, late, row_parts, pre_sent = tied(over_z, rec_parts, late, row_parts, pre_sent)
    swapped = swap_cores(pre_sent)

    mlp_sum = add_up(over_z).astype(BF16)
    cut = hidden_width
    gating_sum = mlp_sum[:, :cut].reshape(2, nx, shard, cut)
    rec_sum = add_up(rec_parts).astype(BF16)
    rest = mlp_sum[:, cut + model :]
    rest = jnp.concatenate([rest[: square // 2], rest[square // 2 :]], axis=1)
    downs = jnp.concatenate([mlp_sum[:, cut : cut + model], rest], axis=0).reshape(nx, parts * shard, model)
    over_x = jnp.concatenate(
        [gating_sum[0], rec_sum[0], gating_sum[1], rec_sum[1]]
        + [downs[:, i * shard : (i + 1) * shard] for i in range(parts)],
        axis=2,
    )
    cut = hidden_width + width
    over_x = scatter_send(over_x, "x", 0)
    late = scatter_send(add_up(late), "z", 0)
    row_parts = scatter_send(add_up(row_parts), "y", 0)
    over_x, late, row_parts, swapped = tied(over_x, late, row_parts, swapped)
    over_x, late, row_sum = add_up(over_x), add_up(late), add_up(row_parts)
    pair = [jnp.concatenate([over_x[:, i * cut : (i + 1) * cut], late[i]], axis=1) for i in (0, 1)]
    cut *= 2
    kept, sent = jnp.where(first, pair[0], pair[1]), jnp.where(first, pair[1], pair[0])
    down = jnp.concatenate([over_x[:, cut + i * model : cut + (i + 1) * model] for i in range(parts)], axis=0)
    rows_out = jnp.concatenate([row_sum, down.reshape(tall, -1)], axis=1)
    came, rows_out = tied(swap_cores(sent), to_owner(rows_out))

    def whole(at, size):
        return in_order(kept[:, at : at + size], came[:, at : at + size], axis=1)

    grad_gating = whole(0, hidden_width)
    grad_recurrent = whole(hidden_width, width)
    grad_upward = whole(hidden_width + width, hidden_width)
    grad_sidebranch = whole(2 * hidden_width + width, width)
    grad_out, gate_grads, grad_down = jnp.split(rows_out, [model, model + 2 * head + 128], axis=1)
    grad_down = grad_down.reshape(downward.shape)

    grad_pre = half(pre_part, core, 0) + swapped.astype(F32)
    own = block_in[0].astype(F32)
    own_scale = rms_scale(own)
    scaled = pre_gain * grad_pre
    grad_in = half(grad_resid, core, 0) + (
        own_scale * scaled - own * own_scale**3 * jnp.mean(scaled * own, axis=-1, keepdims=True)
    )
    result = half(resid + result_part, core, 0) + result_other.astype(F32)

    def along(left, grad_left, right, grad_right):
        return jnp.sum(left.astype(F32) * grad_left + right.astype(F32) * grad_right, axis=1)

    grad_prenorm = along(recurrent, grad_recurrent, sidebranch, grad_sidebranch) / prenorm.astype(F32)
    grad_midnorm = along(gating, grad_gating, upward, grad_upward) / midnorm.astype(F32)
    small = gate_grads[:, 2 * head : 2 * head + 8].T

    finals = jnp.where(core == lax.axis_index("y") // (ny // 2), finals, finals_other)
    slot = width // chips
    finals = lax.dynamic_slice_in_dim(finals, ((chip * 2 + core) % chips) * slot, slot, axis=1)

    return (
        result.astype(BF16)[None],
        grad_in.astype(BF16)[None],
        finals[None, : taps - 1],
        finals[None, taps - 1],
        grad_prenorm,
        grad_recurrent,
        grad_sidebranch,
        small[:4],
        small[4],
        gate_grads[:, :head],
        small[5],
        gate_grads[:, head : 2 * head],
        small[6],
        small[7],
        grad_out,
        grad_midnorm,
        grad_gating,
        grad_upward,
        grad_down,
    )


def solution(mesh):
    seq, dp = mesh.shape["seq"], mesh.shape["dp"]
    side = next(s for s in range(1, seq + 1) if 2 * s * s >= seq)
    fine = Mesh(mesh.devices.reshape(side, side, 2, dp), ("y", "z", "c", "x"))
    part = ("y", "z", "c")
    every = ("y", "z", "c", "x")
    vector, matrix = P(every), P(every, None)
    placed = (
        P("x", part, None),
        P("x", None, None),
        P("x", None),
        P("x", part, None),
        vector,
        matrix,
        matrix,
        P(None, every),
        vector,
        matrix,
        vector,
        matrix,
        vector,
        vector,
        matrix,
        vector,
        matrix,
        matrix,
        matrix,
    )
    return jax.shard_map(
        on_device,
        mesh=fine,
        in_specs=placed,
        out_specs=(P("x", part, None), P("x", part, None), P("x", None, part), P("x", part)) + placed[4:],
        check_vma=False,
    )
```
